32 devices in a mesh: dp: 4 (over y, core), fsdp: 8 (over z, x).
Axes of the slice: x: 2, y: 2, z: 4, core: 2. Of those that a mesh axis runs over, the one named last changes fastest.
Arguments:
- doc_inputs: float32 [32, 512, 768], P(('dp', 'fsdp')), may hold values from -6 to 6
- query_inputs: float32 [384, 32, 768], P(('dp', 'fsdp')), may hold values from -6 to 6
- doc_mask: int32 [32, 512], P(('dp', 'fsdp')), may hold values from 0 to 1, as said below
- query_lengths: int32 [384], P(('dp', 'fsdp')), may hold values from 8 to 32, as said below
- doc_cotangent: float32 [32, 512, 768], P(('dp', 'fsdp')), may hold values from -6 to 6
- query_cotangent: float32 [384, 32, 768], P(('dp', 'fsdp')), may hold values from -6 to 6
- qkv_weight: float32 [768, 2304], P(('dp', 'fsdp')), may hold values from -0.078125 to 0.078125
- out_weight: float32 [768, 768], P(('dp', 'fsdp')), may hold values from -1.75 to 1.75
- in_weight: float32 [768, 4096], P(('dp', 'fsdp')), may hold values from -0.21875 to 0.21875
- ff_weight: float32 [2048, 768], P(('dp', 'fsdp')), may hold values from -0.25 to 0.25
- attn_gain: float32 [768], replicated, may hold values from 0.1 to 1.9
- ffn_gain: float32 [768], replicated, may hold values from 0.1 to 1.9
- bias_table: float32 [32, 12], replicated, may hold values from -4 to 4
Outputs:
- doc_outputs: float32 [32, 512, 768], P(('dp', 'fsdp'))
- query_outputs: float32 [384, 32, 768], P(('dp', 'fsdp'))
- doc_input_grad: float32 [32, 512, 768], P(('dp', 'fsdp'))
- query_input_grad: float32 [384, 32, 768], P(('dp', 'fsdp'))
- qkv_weight_grad: float32 [768, 2304], P(('dp', 'fsdp'))
- out_weight_grad: float32 [768, 768], P(('dp', 'fsdp'))
- in_weight_grad: float32 [768, 4096], P(('dp', 'fsdp'))
- ff_weight_grad: float32 [2048, 768], P(('dp', 'fsdp'))
- attn_gain_grad: float32 [768], replicated
- ffn_gain_grad: float32 [768], replicated
- bias_table_grad: float32 [32, 12], replicated
The draws below stay inside these ranges and needn't reach their ends.
Inputs may be any that keep to these rules, and one draw needn't show every extreme that they name: `doc_mask`: each document's row is ones on a prefix of 256 or more positions and zeros after it; some document has no padding. `query_lengths`: some query group is full and some has exactly 8 real tokens.
All inputs are finite; a program needn't handle non-finite values.
Results may differ from the reference program's by a relative error of at most 0.014.
The reference program's roundings to bfloat16 on the way count: a program that leaves them out, or rounds other values in their place, can miss the bound.
Values may be sent and summed in bfloat16 or wider, within the bound.
No kernel may reach another device: no remote copies, remote signals or barrier semaphores. Data moves between devices by JAX's collectives and lax.ppermute only.
A program may use at most 192 MiB of HBM per device.

```python
import math
import jax
import jax.numpy as jnp
from jax import lax

D = 768
HEADS = 12
FF = 2048
BUCKETS = 32
DLEN = 512
QLEN = 32
DOCS = 32
QGROUPS = 384


def draw_doc_mask(key, part):
    key = jax.random.fold_in(key, 11)
    first_key, second_key = jax.random.split(key)
    doc_lengths = jax.random.randint(first_key, (DOCS,), DLEN // 2, DLEN + 1)
    chosen = jax.random.randint(second_key, (), 0, DOCS)
    doc_lengths = doc_lengths.at[chosen].set(DLEN)
    places = jnp.arange(DLEN, dtype=jnp.int32)
    return (places[None, :] < doc_lengths[:, None]).astype(jnp.int32)


def draw_query_lengths(key, part):
    key = jax.random.fold_in(key, 23)
    first_key, second_key, third_key = jax.random.split(key, 3)
    group_lengths = jax.random.randint(first_key, (QGROUPS,), QLEN // 4, QLEN + 1)
    full_index = jax.random.randint(second_key, (), 0, QGROUPS)
    short_index = (full_index + 1 + jax.random.randint(third_key, (), 0, QGROUPS - 1)) % QGROUPS
    group_lengths = group_lengths.at[full_index].set(QLEN)
    group_lengths = group_lengths.at[short_index].set(QLEN // 4)
    return group_lengths.astype(jnp.int32)


def levels(own_key, dims, cuts, low, top_value):
    level = 1.0
    for position, shards_of in cuts:
        steps = jax.random.uniform(jax.random.fold_in(jax.random.fold_in(own_key, 6), position), (shards_of,), jnp.float32, low / len(cuts), top_value / len(cuts))
        level = level * jnp.repeat(jnp.exp(steps), dims[position] // shards_of).reshape((-1,) + (1,) * (len(dims) - 1 - position))
    return level


def bell_draw(own_key, extent, width, most, cuts=(), kind=jnp.bfloat16):
    drawn = jax.random.normal(own_key, extent, jnp.float32) * width
    if len(cuts) > 0:
        drawn = levels(own_key, extent, cuts, -0.22, 0.18) * drawn
    return jnp.clip(drawn, min=-most, max=most).astype(kind)


def setup_inputs(seed: int = 0) -> dict:
    key_list = jax.random.split(jax.random.key(seed), 14)
    return {
        "doc_inputs": bell_draw(key_list[0], (DOCS, DLEN, D), 1.0, 6.0, ((0, 32),), jnp.float32),
        "query_inputs": bell_draw(key_list[1], (QGROUPS, QLEN, D), 1.0, 6.0, ((0, 32),), jnp.float32),
        "doc_mask": draw_doc_mask(jax.random.fold_in(key_list[13], 71), 0),
        "query_lengths": draw_query_lengths(jax.random.fold_in(key_list[13], 71), 0),
        "doc_cotangent": bell_draw(key_list[4], (DOCS, DLEN, D), 1.0, 6.0, ((0, 32),), jnp.float32),
        "query_cotangent": bell_draw(key_list[5], (QGROUPS, QLEN, D), 1.0, 6.0, ((0, 32),), jnp.float32),
        "qkv_weight": bell_draw(key_list[6], (D, 3 * D), (8 * D) ** -0.5, 0.078125, ((0, 32),), jnp.float32),
        "out_weight": bell_draw(key_list[7], (D, D), (D // 64) ** -0.5, 1.75, ((0, 32),), jnp.float32),
        "in_weight": bell_draw(key_list[8], (D, 2 * FF), D ** -0.5, 0.21875, ((0, 32),), jnp.float32),
        "ff_weight": bell_draw(key_list[9], (FF, D), (FF // 4) ** -0.5, 0.25, ((0, 32),), jnp.float32),
        "attn_gain": jnp.clip(1.0 + 0.18 * jax.random.normal(key_list[10], (D,), jnp.float32), 0.1, 1.9),
        "ffn_gain": jnp.clip(1.0 + 0.18 * jax.random.normal(key_list[11], (D,), jnp.float32), 0.1, 1.9),
        "bias_table": bell_draw(key_list[12], (BUCKETS, HEADS), 1.0, 4.0, (), jnp.float32),
    }


@jax.custom_vjp
def low(v):
    return lax.optimization_barrier(v.astype(jnp.bfloat16)).astype(jnp.float32)

@jax.custom_vjp
def low_back(v):
    return v

def low_keep(v):
    return (low(v), None)

def low_pass(kept, grad):
    return (grad,)

def back_keep(v):
    return (v, None)

def back_low(kept, grad):
    return (low(grad),)
low.defvjp(low_keep, low_pass)
low_back.defvjp(back_keep, back_low)
epsilon = 1e-06
highest = lax.Precision.HIGHEST

def rms_norm(values, gain_vector):
    inverse = lax.rsqrt(lax.optimization_barrier(jnp.mean(values * values, axis=-1, keepdims=True)) + epsilon)
    return values * inverse * gain_vector

def buckets_of(length):
    places = jnp.arange(length, dtype=jnp.int32)
    relative = places[None, :] - places[:, None]
    distance = jnp.abs(relative)
    larger = jnp.zeros_like(distance)
    for threshold in (12, 16, 23, 32, 46, 64, 91):
        larger = larger + (distance >= threshold).astype(jnp.int32)
    bucket = jnp.where(distance < 8, distance, 8 + larger)
    return bucket + 16 * (relative > 0).astype(jnp.int32)

def layer(params, inputs, key_mask, bucket):
    qkv_weight, out_weight, in_weight, ff_weight, attn_gain, ffn_gain, bias_table = params
    seq_count, length, model_width = inputs.shape
    head_count = bias_table.shape[1]
    normed = low(rms_norm(inputs, attn_gain))
    projected = low(low_back(jnp.einsum('bld,de->ble', normed, low(qkv_weight), precision=highest)))
    parted = projected.reshape(seq_count, length, 3, head_count, model_width // head_count)
    queries = parted[:, :, 0]
    key_rows = parted[:, :, 1]
    value_rows = parted[:, :, 2]
    position_bias = jnp.transpose(jnp.take(bias_table, bucket, axis=0), (2, 0, 1))
    masking = jnp.where(key_mask > 0, 0.0, -1000000000.0).astype(jnp.float32)
    scores = jnp.einsum('bqhc,bkhc->bhqk', queries, key_rows, precision=highest)
    scores = low_back(scores + position_bias[None] + masking[:, None, None, :])
    probs = low(jax.nn.softmax(scores, axis=-1))
    mixed_rows = jnp.einsum('bhqk,bkhc->bqhc', probs, value_rows, precision=highest)
    mixed_rows = low(low_back(mixed_rows.reshape(seq_count, length, model_width)))
    attended = low_back(jnp.einsum('bld,de->ble', mixed_rows, low(out_weight), precision=highest))
    middle = inputs + attended
    normed_two = low(rms_norm(middle, ffn_gain))
    gate_up = low_back(jnp.einsum('bld,de->ble', normed_two, low(in_weight), precision=highest))
    hidden_size = ff_weight.shape[0]
    activated = low(jax.nn.gelu(gate_up[..., :hidden_size], approximate=True) * gate_up[..., hidden_size:])
    output_branch = low_back(jnp.einsum('blf,fd->bld', activated, low(ff_weight), precision=highest))
    return middle + output_branch

def run_pass(params, inputs, key_mask, cotangent, most_block):
    seq_count, length, model_width = inputs.shape
    per_block = math.gcd(seq_count, most_block)
    bucket = buckets_of(length)
    steps_count = seq_count // per_block
    shaped = (inputs.reshape(steps_count, per_block, length, model_width), key_mask.reshape(steps_count, per_block, length), cotangent.reshape(steps_count, per_block, length, model_width))

    def one_block(running, pieces):
        block_inputs, block_mask, block_cotangent = pieces

        def forward(weights, values):
            return layer(weights, values, block_mask, bucket)
        outputs, pullback = jax.vjp(forward, params, block_inputs)
        param_grads, input_grads = pullback(block_cotangent)
        return (jax.tree.map(jnp.add, running, param_grads), (outputs, input_grads))
    zero_grads = jax.tree.map(jnp.zeros_like, params)
    totals, (outputs, input_grads) = lax.scan(one_block, zero_grads, shaped)
    return (totals, outputs.reshape(inputs.shape), input_grads.reshape(inputs.shape))

def reference(doc_inputs, query_inputs, doc_mask, query_lengths, doc_cotangent, query_cotangent, qkv_weight, out_weight, in_weight, ff_weight, attn_gain, ffn_gain, bias_table):
    params = (qkv_weight, out_weight, in_weight, ff_weight, attn_gain, ffn_gain, bias_table)
    places = jnp.arange(query_inputs.shape[1], dtype=jnp.int32)
    query_mask = (places[None, :] < query_lengths[:, None]).astype(jnp.int32)
    doc_grads, doc_outputs, doc_input_grad = run_pass(params, doc_inputs, doc_mask, doc_cotangent, 8)
    query_grads, query_outputs, query_input_grad = run_pass(params, query_inputs, query_mask, query_cotangent, 128)
    grads = jax.tree.map(jnp.add, doc_grads, query_grads)
    return (doc_outputs, query_outputs, doc_input_grad, query_input_grad, grads[0], grads[1], grads[2], grads[3], grads[4], grads[5], grads[6])
```

```python
import jax
import jax.numpy as jnp
from jax import lax
import numpy as np
from jax.experimental import pallas as pl
from jax.experimental.pallas import tpu as pltpu
from jax.sharding import PartitionSpec as P

both = ("dp", "fsdp")

epsilon = 1e-06
highest = lax.Precision.HIGHEST


def rms_norm(values, gain_vector):
    inverse = lax.rsqrt(jnp.mean(values * values, axis=-1, keepdims=True) + epsilon)
    return values * inverse * gain_vector


def buckets_of(length):
    places = jnp.arange(length, dtype=jnp.int32)
    relative = places[None, :] - places[:, None]
    distance = jnp.abs(relative)
    larger = jnp.zeros_like(distance)
    for threshold in (12, 16, 23, 32, 46, 64, 91):
        larger = larger + (distance >= threshold).astype(jnp.int32)
    bucket = jnp.where(distance < 8, distance, 8 + larger)
    return bucket + 16 * (relative > 0).astype(jnp.int32)


def bucket_tables(length, bias_table):
    labels = jnp.arange(bias_table.shape[0], dtype=jnp.int32)
    onehot = (buckets_of(length)[:, :, None] == labels).astype(jnp.float32)
    position_bias = jnp.einsum("qkn,nh->hqk", onehot, bias_table, precision=highest)
    return (position_bias, onehot.astype(jnp.bfloat16))


def gated_unit(gate_up):
    hidden_size = gate_up.shape[-1] // 2
    return jax.nn.gelu(gate_up[:, :hidden_size], approximate=True) * gate_up[:, hidden_size:]


def score_block(packed, key_mask, position_bias):
    queries = packed[:, :, 0]
    key_rows = packed[:, :, 1]
    masking = jnp.where(key_mask > 0, 0.0, -1000000000.0).astype(jnp.float32)
    scores = jnp.einsum("bqhc,bkhc->bhqk", queries, key_rows, preferred_element_type=jnp.float32)
    return scores + position_bias[None] + masking[:, None, None, :]


def attend_forward(packed, key_mask, position_bias):
    scores = score_block(packed, key_mask, position_bias)
    row_peak = jnp.max(scores, axis=-1, keepdims=True)
    raised = jnp.exp(scores - row_peak)
    row_total = jnp.sum(raised, axis=-1, keepdims=True)
    probs_low = (raised / row_total).astype(jnp.bfloat16)
    mixed_rows = jnp.einsum(
        "bhqk,bkhc->bqhc", probs_low, packed[:, :, 2], preferred_element_type=jnp.float32
    )
    return (mixed_rows.astype(jnp.bfloat16), row_peak[..., 0] + jnp.log(row_total[..., 0]))


def attend_backward(packed, key_mask, position_bias, onehot, log_total, grad_mixed):
    queries = packed[:, :, 0]
    key_rows = packed[:, :, 1]
    value_rows = packed[:, :, 2]
    scores = score_block(packed, key_mask, position_bias)
    probs = jnp.exp(scores - log_total[..., None])
    probs_low = probs.astype(jnp.bfloat16)
    grad_values = jnp.einsum(
        "bhqk,bqhc->bkhc", probs_low, grad_mixed, preferred_element_type=jnp.float32
    )
    grad_probs = jnp.einsum(
        "bqhc,bkhc->bhqk", grad_mixed, value_rows, preferred_element_type=jnp.float32
    )
    weighted = jnp.sum(probs * grad_probs, axis=-1, keepdims=True)
    grad_scores = (probs * (grad_probs - weighted)).astype(jnp.bfloat16)
    grad_queries = jnp.einsum(
        "bhqk,bkhc->bqhc", grad_scores, key_rows, preferred_element_type=jnp.float32
    )
    grad_keys = jnp.einsum(
        "bhqk,bqhc->bkhc", grad_scores, queries, preferred_element_type=jnp.float32
    )
    grad_table = jnp.einsum("bhqk,qkn->nh", grad_scores, onehot, preferred_element_type=jnp.float32)
    stacked = jnp.stack([grad_queries, grad_keys, grad_values], axis=2)
    return (stacked.astype(jnp.bfloat16), grad_table)


def place_index(y, c, z, x):
    return ((y * 2 + c) * 4 + z) * 2 + x


def flip_pairs(dy=0, dc=0, dz=0, dx=0):
    pairs = []
    for y in range(2):
        for c in range(2):
            for z in range(4):
                for x in range(2):
                    pairs.append(
                        (place_index(y, c, z, x), place_index(y ^ dy, c ^ dc, z ^ dz, x ^ dx))
                    )
    return pairs


def swap(values, **flips):
    return lax.ppermute(values, both, flip_pairs(**flips))


def own_place():
    outer = lax.axis_index("dp")
    inner = lax.axis_index("fsdp")
    return outer // 2, outer % 2, inner // 2, inner % 2


def unpack_kernel(place_ref, *refs):
    pieces, full_ref, sems = refs[:8], refs[8], refs[9]
    y, c, z, x = place_ref[0], place_ref[1], place_ref[2], place_ref[3]
    copies = []
    for number, piece in enumerate(pieces):
        flip_c, kind = number // 4, number % 4
        for first in range(2):
            for second in range(2):
                if kind < 2:
                    dx, dy, dz = first, kind, second
                else:
                    dy, dx, dz = first, kind - 2, second + 2
                target = place_index(y ^ dy, c ^ flip_c, z ^ dz, x ^ dx)
                copies.append(
                    pltpu.make_async_copy(
                        piece.at[first, second], full_ref.at[target], sems.at[len(copies)]
                    )
                )
    for copy in copies:
        copy.start()
    for copy in copies:
        copy.wait()


def unpack(place, pieces):
    rows, columns = pieces[0].shape[2:]
    return pl.pallas_call(
        unpack_kernel,
        out_shape=jax.ShapeDtypeStruct((32, rows, columns), pieces[0].dtype),
        in_specs=[pl.BlockSpec(memory_space=pltpu.SMEM)]
        + [pl.BlockSpec(memory_space=pl.ANY)] * 8,
        out_specs=pl.BlockSpec(memory_space=pltpu.VMEM),
        scratch_shapes=[pltpu.SemaphoreType.DMA((32,))],
        compiler_params=pltpu.CompilerParams(vmem_limit_bytes=24 * 2**20),
        name="unpack",
    )(place, *pieces).reshape(32 * rows, columns)


def hand_routed():
    return (lax.axis_size("dp"), lax.axis_size("fsdp")) == (4, 8)


def gather_rows(shard, place):
    if not hand_routed():
        return lax.all_gather(shard, both, axis=0, tiled=True)
    near = swap(shard, dz=1)
    first = jnp.stack([shard, near])
    second = jnp.stack([swap(shard, dz=2), swap(shard, dz=3)])
    first = jnp.stack([first, swap(first, dx=1)])
    second = jnp.stack([second, swap(second, dy=1)])
    first_far = swap(first, dy=1)
    second_far = swap(second, dx=1)
    here = [first, first_far, second, second_far]
    return unpack(place, here + [swap(piece, dc=1) for piece in here])


def added(kept, arrived):
    return (kept.astype(jnp.float32) + arrived.astype(jnp.float32)).astype(jnp.bfloat16)


def pick(values, index, axis):
    return lax.dynamic_index_in_dim(values, index, axis, keepdims=False)


def scatter_rows(partial, place):
    if not hand_routed():
        return lax.psum_scatter(
            partial.astype(jnp.float32), both, scatter_dimension=0, tiled=True
        )
    y, c, z, x = place
    rows = partial.shape[0] // 32
    parts = partial.reshape(2, 2, 4, 2, rows, partial.shape[1])
    parts = added(pick(parts, c, 1), swap(pick(parts, 1 - c, 1), dc=1))
    first, second = parts[:, :2], parts[:, 2:]
    first = added(pick(first, x, 2), swap(pick(first, 1 - x, 2), dx=1))
    second = added(pick(second, y, 0), swap(pick(second, 1 - y, 0), dy=1))
    first = added(pick(first, y, 0), swap(pick(first, 1 - y, 0), dy=1))
    second = added(pick(second, x, 1), swap(pick(second, 1 - x, 1), dx=1))
    column = jnp.concatenate([first, second], axis=0)
    total = pick(column, z, 0).astype(jnp.float32)
    for flip in (1, 2, 3):
        total = total + swap(pick(column, z ^ flip, 0), dz=flip).astype(jnp.float32)
    return total


def add_everywhere(values):
    if not hand_routed():
        return lax.psum(values, both)
    for flips in ({"dc": 1}, {"dx": 1}, {"dy": 1}, {"dz": 1}, {"dz": 2}):
        values = values + swap(values, **flips)
    return values


def body(
    doc_inputs,
    query_inputs,
    doc_mask,
    query_lengths,
    doc_cotangent,
    query_cotangent,
    qkv_weight,
    out_weight,
    in_weight,
    ff_weight,
    attn_gain,
    ffn_gain,
    bias_table,
):
    doc_count, doc_length, model_width = doc_inputs.shape
    group_count, group_length = (query_inputs.shape[0], query_inputs.shape[1])
    head_count = bias_table.shape[1]
    head_size = model_width // head_count
    doc_rows = doc_count * doc_length
    shards = (
        qkv_weight.astype(jnp.bfloat16),
        out_weight.astype(jnp.bfloat16),
        in_weight.astype(jnp.bfloat16),
        ff_weight.astype(jnp.bfloat16),
    )
    place = own_place()
    place_vector = jnp.stack(place).astype(jnp.int32)
    full_attention = gather_rows(jnp.concatenate([shards[0], shards[1]], axis=1), place_vector)
    full_qkv = full_attention[:, : 3 * model_width]
    full_out = full_attention[:, 3 * model_width :]
    full_in = gather_rows(shards[2], place_vector)
    full_ff = gather_rows(shards[3], place_vector)
    places = jnp.arange(group_length, dtype=jnp.int32)
    query_mask = (places[None, :] < query_lengths[:, None]).astype(jnp.int32)
    doc_bias, doc_onehot = bucket_tables(doc_length, bias_table)
    query_bias, query_onehot = bucket_tables(group_length, bias_table)
    rows = jnp.concatenate(
        [doc_inputs.reshape(doc_rows, model_width), query_inputs.reshape(-1, model_width)], axis=0
    )
    normed, norm_pull = jax.vjp(rms_norm, rows, attn_gain)
    normed_low = normed.astype(jnp.bfloat16)
    projected = jnp.dot(normed_low, full_qkv, preferred_element_type=jnp.float32).astype(
        jnp.bfloat16
    )
    doc_packed = projected[:doc_rows].reshape(doc_count, doc_length, 3, head_count, head_size)
    query_packed = projected[doc_rows:].reshape(group_count, group_length, 3, head_count, head_size)

    def doc_forward(pieces):
        packed, key_mask = pieces
        mixed_rows, log_total = attend_forward(packed[None], key_mask[None], doc_bias)
        return (mixed_rows[0], log_total[0])

    doc_mixed, doc_log_total = lax.map(doc_forward, (doc_packed, doc_mask))
    query_mixed, query_log_total = attend_forward(query_packed, query_mask, query_bias)
    mixed_all = jnp.concatenate(
        [doc_mixed.reshape(doc_rows, model_width), query_mixed.reshape(-1, model_width)], axis=0
    )
    middle = rows + jnp.dot(mixed_all, full_out, preferred_element_type=jnp.float32)
    normed_two, norm_pull_two = jax.vjp(rms_norm, middle, ffn_gain)
    normed_two_low = normed_two.astype(jnp.bfloat16)
    gate_up = jnp.dot(normed_two_low, full_in, preferred_element_type=jnp.float32)
    activated, gated_pull = jax.vjp(gated_unit, gate_up)
    activated_low = activated.astype(jnp.bfloat16)
    outputs = middle + jnp.dot(activated_low, full_ff, preferred_element_type=jnp.float32)
    cotangent = jnp.concatenate(
        [doc_cotangent.reshape(doc_rows, model_width), query_cotangent.reshape(-1, model_width)],
        axis=0,
    )
    cotangent_low = cotangent.astype(jnp.bfloat16)
    grad_ff = jnp.einsum(
        "rf,rd->fd", activated_low, cotangent_low, preferred_element_type=jnp.float32
    )
    grad_activated = jnp.einsum(
        "rd,fd->rf", cotangent_low, full_ff, preferred_element_type=jnp.float32
    )
    (grad_gate_up,) = gated_pull(grad_activated)
    grad_gate_low = grad_gate_up.astype(jnp.bfloat16)
    grad_in = jnp.einsum(
        "rd,re->de", normed_two_low, grad_gate_low, preferred_element_type=jnp.float32
    )
    grad_normed_two = jnp.einsum(
        "re,de->rd", grad_gate_low, full_in, preferred_element_type=jnp.float32
    )
    grad_middle, grad_ffn_gain = norm_pull_two(grad_normed_two)
    grad_middle = grad_middle + cotangent
    in_grad_shard = scatter_rows(grad_in.astype(jnp.bfloat16), place)
    ff_grad_shard = scatter_rows(grad_ff.astype(jnp.bfloat16), place)
    grad_middle_low = grad_middle.astype(jnp.bfloat16)
    grad_out = jnp.einsum(
        "rd,re->de", mixed_all, grad_middle_low, preferred_element_type=jnp.float32
    )
    grad_mixed = jnp.einsum(
        "re,de->rd", grad_middle_low, full_out, preferred_element_type=jnp.float32
    ).astype(jnp.bfloat16)
    doc_grad_mixed = grad_mixed[:doc_rows].reshape(doc_count, doc_length, head_count, head_size)
    query_grad_mixed = grad_mixed[doc_rows:].reshape(
        group_count, group_length, head_count, head_size
    )

    def doc_backward(running, pieces):
        packed, key_mask, log_total, grad_rows = pieces
        grad_packed, grad_table = attend_backward(
            packed[None], key_mask[None], doc_bias, doc_onehot, log_total[None], grad_rows[None]
        )
        return (running + grad_table, grad_packed[0])

    doc_table, doc_grad_packed = lax.scan(
        doc_backward,
        jnp.zeros_like(bias_table),
        (doc_packed, doc_mask, doc_log_total, doc_grad_mixed),
    )
    query_grad_packed, query_table = attend_backward(
        query_packed, query_mask, query_bias, query_onehot, query_log_total, query_grad_mixed
    )
    grad_projected = jnp.concatenate(
        [
            doc_grad_packed.reshape(doc_rows, 3 * model_width),
            query_grad_packed.reshape(-1, 3 * model_width),
        ],
        axis=0,
    )
    grad_qkv = jnp.einsum(
        "rd,re->de", normed_low, grad_projected, preferred_element_type=jnp.float32
    )
    grad_normed = jnp.einsum(
        "re,de->rd", grad_projected, full_qkv, preferred_element_type=jnp.float32
    )
    grad_rows, grad_attn_gain = norm_pull(grad_normed)
    grad_inputs = grad_middle + grad_rows
    attention_shard = scatter_rows(
        jnp.concatenate([grad_qkv, grad_out], axis=1).astype(jnp.bfloat16), place
    )
    qkv_grad_shard = attention_shard[:, : 3 * model_width]
    out_grad_shard = attention_shard[:, 3 * model_width :]
    small = jnp.concatenate(
        [grad_attn_gain, grad_ffn_gain, (doc_table + query_table).reshape(-1)]
    )
    small = add_everywhere(small)
    attn_gain_grad = small[:model_width]
    ffn_gain_grad = small[model_width : 2 * model_width]
    bias_table_grad = small[2 * model_width :].reshape(bias_table.shape)
    return (
        outputs[:doc_rows].reshape(doc_inputs.shape),
        outputs[doc_rows:].reshape(query_inputs.shape),
        grad_inputs[:doc_rows].reshape(doc_inputs.shape),
        grad_inputs[doc_rows:].reshape(query_inputs.shape),
        qkv_grad_shard,
        out_grad_shard,
        in_grad_shard,
        ff_grad_shard,
        attn_gain_grad,
        ffn_gain_grad,
        bias_table_grad,
    )


def solution(mesh):
    placed = (
        P(("dp", "fsdp"), None, None),
        P(("dp", "fsdp"), None, None),
        P(("dp", "fsdp"), None),
        P(("dp", "fsdp")),
        P(("dp", "fsdp"), None, None),
        P(("dp", "fsdp"), None, None),
        P(("dp", "fsdp"), None),
        P(("dp", "fsdp"), None),
        P(("dp", "fsdp"), None),
        P(("dp", "fsdp"), None),
        P(),
        P(),
        P(),
    )
    return jax.shard_map(
        body,
        mesh=mesh,
        in_specs=placed,
        out_specs=(
            P(("dp", "fsdp"), None, None),
            P(("dp", "fsdp"), None, None),
            P(("dp", "fsdp"), None, None),
            P(("dp", "fsdp"), None, None),
            P(("dp", "fsdp"), None),
            P(("dp", "fsdp"), None),
            P(("dp", "fsdp"), None),
            P(("dp", "fsdp"), None),
            P(),
            P(),
            P(),
        ),
        check_vma=False,
    )
```

```python
import functools

import jax
import jax.numpy as jnp
from jax import lax
from jax.experimental import pallas as pl
from jax.experimental.pallas import tpu as pltpu
from jax.sharding import PartitionSpec as P

both = ("dp", "fsdp")
epsilon = 1e-06
highest = lax.Precision.HIGHEST
anywhere = pl.BlockSpec(memory_space=pl.ANY)


def place_index(y, c, z, x):
    return ((y * 2 + c) * 4 + z) * 2 + x


def flip_pairs(dy=0, dc=0, dz=0, dx=0):
    pairs = []
    for y in range(2):
        for c in range(2):
            for z in range(4):
                for x in range(2):
                    pairs.append(
                        (place_index(y, c, z, x), place_index(y ^ dy, c ^ dc, z ^ dz, x ^ dx))
                    )
    return pairs


def swap(values, **flips):
    return lax.ppermute(values, both, flip_pairs(**flips))


def hand_routed():
    return (lax.axis_size("dp"), lax.axis_size("fsdp")) == (4, 8)


def own_place():
    outer = lax.axis_index("dp")
    inner = lax.axis_index("fsdp")
    return outer // 2, outer % 2, inner // 2, inner % 2


def after(values, *earlier):
    return lax.optimization_barrier((values, *earlier))[0]


def together(*values):
    return lax.optimization_barrier(values)


def fill_copies(place_ref, pieces, target, sems):
    if len(pieces) == 1:
        return [pltpu.make_async_copy(pieces[0], target, sems.at[0])]
    y, c, z, x = place_ref[0], place_ref[1], place_ref[2], place_ref[3]
    copies = []

    def add(piece, row, size):
        copies.append(
            pltpu.make_async_copy(
                piece, target.at[pl.ds(row, size)], sems.at[len(copies)]
            )
        )

    for number, piece in enumerate(pieces):
        core = c ^ (number // 4)
        kind = number % 4
        if kind < 2:
            add(piece, place_index(y ^ kind, core, z - z % 2, 0), 4)
        else:
            for outer in range(2):
                for inner in range(2):
                    row = place_index(outer, core, (z - z % 2) ^ 2, x ^ (kind - 2))
                    add(piece.at[pl.ds(2 * outer + inner, 1)], row + 2 * inner, 1)
    return copies


def filled(place_ref, pieces, full_ref, held, sems, body):
    step = pl.program_id(0)
    kept = pltpu.make_async_copy(held, full_ref, sems.at[32])

    @pl.when(step == 0)
    def _():
        copies = fill_copies(place_ref, pieces, held, sems)
        for copy in copies:
            copy.start()
        for copy in copies:
            copy.wait()
        kept.start()

    body()

    @pl.when(step == pl.num_programs(0) - 1)
    def _():
        kept.wait()


def gather_order(near, far, core_near, core_far):
    return (near[0], far[0], near[1], far[1], core_near[0], core_far[0], core_near[1], core_far[1])


def split_rows(full):
    return full.reshape(32, full.shape[0] // 32, full.shape[1])


def in_order(own, other, index):
    odd = index % 2 == 1
    return jnp.where(odd, other, own), jnp.where(odd, own, other)


def gather_column(shard):
    return tuple(swap(shard, dz=flip) for flip in (1, 2, 3))


def gather_plane(place, shard, column):
    first = jnp.stack(in_order(shard, column[0], place[2]))
    second = jnp.stack(in_order(column[1], column[2], place[2]))
    return first, second, swap(first, dx=1), swap(second, dy=1)


def gather_near(place, first, second, first_near, second_near):
    rows, columns = first.shape[1:]
    first = jnp.stack(in_order(first, first_near, place[3]), axis=1)
    second = jnp.stack(in_order(second, second_near, place[0]))
    return first.reshape(4, rows, columns), second.reshape(4, rows, columns)


def gather_far(first, second):
    return swap(first, dy=1), swap(second, dx=1)


def gather_core(*pieces):
    return tuple(swap(piece, dc=1) for piece in pieces)


def cut(values, places):
    start = [0 if place is None else place for place in places]
    sizes = [size if place is None else 1 for place, size in zip(places, values.shape)]
    kept = [size for place, size in zip(places, values.shape) if place is None]
    return lax.dynamic_slice(values, start, sizes).reshape(kept)


def summed(*terms):
    total = terms[0].astype(jnp.float32)
    for term in terms[1:]:
        total = total + term.astype(jnp.float32)
    return total


def low_sum(*terms):
    return summed(*terms).astype(jnp.bfloat16)


def joined_halves(kept, sent):
    return jnp.stack([kept, sent], axis=1).reshape(-1, kept.shape[2]).astype(jnp.float32)


class Scatter:
    def __init__(self, kept, sent, place):
        self.place = place
        self.shape = (2, 4, 2, kept.shape[1] // 8, kept.shape[2])
        self.kept = kept.reshape(self.shape)
        self.sent = sent

    def halves(self, got, cut_y, cut_x, half):
        y, c, z, x = self.place
        own = self.kept[:, 2 * half : 2 * half + 2]
        got = got[:, 2 * half : 2 * half + 2]
        places = (cut_y, None, cut_x, None, None)
        return cut(own, places), cut(got, places)

    def core(self):
        return swap(self.sent, dc=1).reshape(self.shape)

    def plane(self, got):
        y, c, z, x = self.place
        first = swap(low_sum(*self.halves(got, None, 1 - x, 0)), dx=1)
        second = swap(low_sum(*self.halves(got, 1 - y, None, 1)), dy=1)
        return first, second

    def far(self, got, near):
        y, c, z, x = self.place
        first = low_sum(
            *self.halves(got, 1 - y, x, 0), cut(near[0], (1 - y, None, None, None))
        )
        second = low_sum(
            *self.halves(got, y, 1 - x, 1), cut(near[1], (None, 1 - x, None, None))
        )
        return swap(first, dy=1), swap(second, dx=1)

    def column(self, got, near, far):
        y, c, z, x = self.place
        first = summed(*self.halves(got, y, x, 0), cut(near[0], (y, None, None, None)), far[0])
        second = summed(*self.halves(got, y, x, 1), cut(near[1], (None, x, None, None)), far[1])
        total = jnp.concatenate([first, second], axis=0)
        others = []
        for flip in (1, 2, 3):
            share = cut(total, (z ^ flip, None, None)).astype(jnp.bfloat16)
            others.append(swap(share, dz=flip))
        return cut(total, (z, None, None)), *others


def add_flipped(values, *steps):
    for flips in steps:
        values = values + swap(values, **flips)
    return values


count = 128


def relative_places():
    places = jnp.arange(4 * count, dtype=jnp.int32)
    return jnp.where(places < 3 * count, places - count, places - 5 * count)


def bucket_of(relative):
    distance = jnp.abs(relative)
    larger = jnp.zeros_like(distance)
    for threshold in (12, 16, 23, 32, 46, 64, 91):
        larger = larger + (distance >= threshold).astype(jnp.int32)
    bucket = jnp.where(distance < 8, distance, 8 + larger)
    return bucket + 16 * (relative > 0).astype(jnp.int32)


def lines_onehot(bucket_count):
    labels = jnp.arange(bucket_count, dtype=jnp.int32)
    return (bucket_of(relative_places())[:, None] == labels).astype(jnp.float32)


def own_lanes(head, shape):
    lanes = lax.broadcasted_iota(jnp.int32, shape, 1)
    return lanes < shape[1] // 2 if head == 0 else lanes >= shape[1] // 2


def keep_lanes(head, values):
    return jnp.where(own_lanes(head, values.shape), values, jnp.zeros_like(values))


def both_heads(values):
    return jnp.concatenate([keep_lanes(0, values), keep_lanes(1, values)], axis=0)


def joined(stacked):
    first, second = jnp.split(stacked, 2, axis=0)
    return jnp.where(own_lanes(0, first.shape), first, second).astype(jnp.bfloat16)


def softmax_rows(scores):
    raised = jnp.exp(scores - jnp.max(scores, axis=-1, keepdims=True))
    return raised * (1.0 / jnp.sum(raised, axis=-1, keepdims=True))


def dot_nt(left, right):
    return lax.dot_general(
        left, right, (((1,), (1,)), ((), ())), preferred_element_type=jnp.float32
    )


def dot_nn(left, right):
    return jnp.dot(left, right, preferred_element_type=jnp.float32)


def attend_kernel(
    docs, length, group, q_ref, k_ref, v_ref, line_ref, mask_ref, query_mask_ref,
    mixed_ref, doc_probs_ref, query_probs_ref, scores_scratch, probs_scratch,
):
    blocks = length // count
    query_start = docs * length
    query_blocks = (q_ref.shape[0] - query_start) // count
    row_group = lax.broadcasted_iota(jnp.int32, (count, count), 0) // group
    column_group = lax.broadcasted_iota(jnp.int32, (count, count), 1) // group
    bands, edges = [], []
    for head in range(2):
        line = line_ref[0, head : head + 1, :]
        band = pltpu.roll(
            jnp.broadcast_to(line, (count, 4 * count)), 0, 1, stride=1, stride_axis=0
        )
        bands.append(band)
        edges.append(
            (
                jnp.broadcast_to(line[:, 4 * count - 1 :], (1, count)),
                jnp.broadcast_to(line[:, 3 * count - 1 : 3 * count], (1, count)),
            )
        )
    for doc in range(docs):
        base = doc * length
        whole = slice(base, base + length)
        masking = mask_ref[doc : doc + 1, :]
        scores_scratch[...] = dot_nt(both_heads(q_ref[whole, :]), k_ref[whole, :])
        for head in range(2):
            for row in range(blocks):
                rows = slice(row * count, (row + 1) * count)
                stacked = slice(head * length + row * count, head * length + (row + 1) * count)
                shifted = []
                for column in range(blocks):
                    columns = slice(column * count, (column + 1) * count)
                    away = column - row
                    block = scores_scratch[stacked, columns]
                    if abs(away) > 1:
                        block = block + (edges[head][away > 0] + masking[:, columns])
                    else:
                        start = (away + 1) * count
                        block = block + bands[head][:, start : start + count]
                        block = block + masking[:, columns]
                    shifted.append(block)
                probs = softmax_rows(jnp.concatenate(shifted, axis=1))
                doc_probs_ref[head, base + row * count : base + (row + 1) * count, :] = probs
                probs_scratch[stacked, :] = probs.astype(jnp.bfloat16)
        mixed_ref[whole, :] = joined(dot_nn(probs_scratch[...], v_ref[whole, :]))
    for block in range(query_blocks):
        rows = slice(query_start + block * count, query_start + (block + 1) * count)
        masking = query_mask_ref[block]
        scores = dot_nt(both_heads(q_ref[rows, :]), k_ref[rows, :])
        low = []
        for head in range(2):
            bias = jnp.where(
                row_group == column_group, bands[head][:, count : 2 * count], -1e9
            )
            probs = softmax_rows(scores[head * count : (head + 1) * count, :] + bias + masking)
            query_probs_ref[head, block * count : (block + 1) * count, :] = probs
            low.append(probs.astype(jnp.bfloat16))
        mixed_ref[rows, :] = joined(dot_nn(jnp.concatenate(low, axis=0), v_ref[rows, :]))


def pair_spec(rows, offset):
    return pl.BlockSpec((rows, 2 * 64), lambda pair: (0, offset + pair))


def attend(projected, lines, doc_mask, query_mask, group):
    docs, length = doc_mask.shape
    rows, width = projected.shape[0], projected.shape[1] // 3
    pairs = lines.shape[0]
    query_rows = rows - docs * length
    return pl.pallas_call(
        functools.partial(attend_kernel, docs, length, group),
        grid=(pairs,),
        out_shape=(
            jax.ShapeDtypeStruct((rows, width), jnp.bfloat16),
            jax.ShapeDtypeStruct((2 * pairs, docs * length, length), jnp.float32),
            jax.ShapeDtypeStruct((2 * pairs, query_rows, count), jnp.float32),
        ),
        in_specs=[
            pair_spec(rows, 0),
            pair_spec(rows, pairs),
            pair_spec(rows, 2 * pairs),
            pl.BlockSpec((1, 2, 4 * count), lambda pair: (pair, 0, 0)),
            pl.BlockSpec((docs, length), lambda pair: (0, 0)),
            pl.BlockSpec(query_mask.shape, lambda pair: (0, 0, 0)),
        ],
        out_specs=(
            pair_spec(rows, 0),
            pl.BlockSpec((2, docs * length, length), lambda pair: (pair, 0, 0)),
            pl.BlockSpec((2, query_rows, count), lambda pair: (pair, 0, 0)),
        ),
        scratch_shapes=[
            pltpu.VMEM((2 * length, length), jnp.float32),
            pltpu.VMEM((2 * length, length), jnp.bfloat16),
        ],
        compiler_params=pltpu.CompilerParams(vmem_limit_bytes=40 * 2**20),
        cost_estimate=pl.CostEstimate(
            flops=2 * 2 * pairs * (docs * length * length + query_rows * count) * 128 * 2,
            bytes_accessed=rows * width * 8 + 8 * pairs * docs * length * length,
            transcendentals=2 * pairs * (docs * length * length + query_rows * count),
        ),
        name="attend",
    )(projected, projected, projected, lines, doc_mask, query_mask)


def attend_back_kernel(
    docs, length, q_ref, k_ref, v_ref, grad_ref, doc_probs_ref, query_probs_ref,
    out_ref, line_ref, grads_scratch, scores_scratch, probs_scratch,
):
    blocks = length // count
    query_start = docs * length
    query_blocks = (q_ref.shape[0] - query_start) // count
    low = jnp.bfloat16
    band = [[None] * 5, [None] * 5]

    def gather(head, place, block):
        held = band[head][place]
        band[head][place] = block if held is None else held + block

    def backward(probs, grad_probs):
        product = probs * grad_probs
        return product - probs * jnp.sum(product, axis=-1, keepdims=True)

    for doc in range(docs):
        base = doc * length
        whole = slice(base, base + length)
        grads_scratch[...] = dot_nt(both_heads(grad_ref[whole, :]), v_ref[whole, :])
        for head in range(2):
            for row in range(blocks):
                rows = slice(base + row * count, base + (row + 1) * count)
                stacked = slice(head * length + row * count, head * length + (row + 1) * count)
                probs = doc_probs_ref[head, rows, :]
                scores = backward(probs, grads_scratch[stacked, :])
                for column in range(blocks):
                    away = max(-2, min(2, column - row))
                    block = scores[:, column * count : (column + 1) * count]
                    if abs(away) == 2:
                        block = jnp.sum(block.reshape(count // 8, 8, count), axis=0)
                    gather(head, away + 2, block)
                scores_scratch[stacked, :] = scores.astype(low)
                probs_scratch[stacked, :] = probs.astype(low)
        out_ref[0, whole, :] = joined(dot_nn(scores_scratch[...], k_ref[whole, :]))
        q_turned = q_ref[whole, :].T
        grad_turned = grad_ref[whole, :].T
        half = q_turned.shape[0] // 2
        grad_k, grad_v = [], []
        for head in range(2):
            own = slice(head * half, (head + 1) * half)
            stacked = slice(head * length, (head + 1) * length)
            grad_k.append(dot_nn(q_turned[own, :], scores_scratch[stacked, :]))
            grad_v.append(dot_nn(grad_turned[own, :], probs_scratch[stacked, :]))
        out_ref[1, whole, :] = jnp.concatenate(grad_k, axis=0).astype(low).T
        out_ref[2, whole, :] = jnp.concatenate(grad_v, axis=0).astype(low).T
    for block in range(query_blocks):
        rows = slice(query_start + block * count, query_start + (block + 1) * count)
        grad_probs = dot_nt(both_heads(grad_ref[rows, :]), v_ref[rows, :])
        low_scores, low_probs = [], []
        for head in range(2):
            probs = query_probs_ref[head, block * count : (block + 1) * count, :]
            scores = backward(probs, grad_probs[head * count : (head + 1) * count, :])
            gather(head, 2, scores)
            low_scores.append(scores.astype(low))
            low_probs.append(probs.astype(low))
        out_ref[0, rows, :] = joined(dot_nn(jnp.concatenate(low_scores, axis=0), k_ref[rows, :]))
        turned = jnp.concatenate(low_scores, axis=1).T
        out_ref[1, rows, :] = joined(dot_nn(turned, q_ref[rows, :]))
        turned = jnp.concatenate(low_probs, axis=1).T
        out_ref[2, rows, :] = joined(dot_nn(turned, grad_ref[rows, :]))
    for head in range(2):
        below, before, middle, after, above = band[head]
        wide = jnp.concatenate([before, middle, after, jnp.zeros_like(middle)], axis=1)
        size = count
        while size > 1:
            size //= 2
            wide = wide[:size] + pltpu.roll(wide[size:], 4 * count - size, 1)
        far = jnp.concatenate(
            [
                jnp.zeros((1, 2 * count), jnp.float32),
                jnp.sum(above, axis=0, keepdims=True),
                jnp.sum(below, axis=0, keepdims=True),
            ],
            axis=1,
        )
        line_ref[0, head : head + 1, :] = wide + far


def attend_back(projected, grad_mixed, doc_probs, query_probs, length, *earlier):
    rows, width = grad_mixed.shape
    pairs = doc_probs.shape[0] // 2
    docs = doc_probs.shape[1] // length
    query_rows = query_probs.shape[1]

    def kernel(*refs):
        attend_back_kernel(docs, length, *refs[:6], *refs[6 + len(earlier) :])

    return pl.pallas_call(
        kernel,
        grid=(pairs,),
        out_shape=(
            jax.ShapeDtypeStruct((3, rows, width), jnp.bfloat16),
            jax.ShapeDtypeStruct((pairs, 2, 4 * count), jnp.float32),
        ),
        in_specs=[
            pair_spec(rows, 0),
            pair_spec(rows, pairs),
            pair_spec(rows, 2 * pairs),
            pair_spec(rows, 0),
            pl.BlockSpec((2, docs * length, length), lambda pair: (pair, 0, 0)),
            pl.BlockSpec((2, query_rows, count), lambda pair: (pair, 0, 0)),
        ]
        + [anywhere] * len(earlier),
        out_specs=(
            pl.BlockSpec((3, rows, 2 * 64), lambda pair: (0, 0, pair)),
            pl.BlockSpec((1, 2, 4 * count), lambda pair: (pair, 0, 0)),
        ),
        scratch_shapes=[
            pltpu.VMEM((2 * length, length), jnp.float32),
            pltpu.VMEM((2 * length, length), jnp.bfloat16),
            pltpu.VMEM((2 * length, length), jnp.bfloat16),
        ],
        compiler_params=pltpu.CompilerParams(vmem_limit_bytes=40 * 2**20),
        cost_estimate=pl.CostEstimate(
            flops=2 * 2 * pairs * (docs * length * length + query_rows * count) * 128 * 4,
            bytes_accessed=rows * width * 14 + 8 * pairs * docs * length * length,
            transcendentals=0,
        ),
        name="attend_back",
    )(projected, projected, projected, grad_mixed, doc_probs, query_probs, *earlier)


def dot_tn(left, right):
    return lax.dot_general(
        left, right, (((0,), (0,)), ((), ())), preferred_element_type=jnp.float32
    )


tile = 512
row_parts = 2
gate_parts = 4
curve = 0.044715
slope = 0.7978845608028654


def turned_rows(place_ref, values, turned):
    quarter = values.shape[1] // 4
    flipped = values[...].T
    for outer in range(2):
        for core in range(2):
            kept = core ^ 1 ^ place_ref[1]
            start = pl.multiple_of((2 * kept + outer) * quarter, 16)
            block = flipped[(2 * outer + core) * quarter : (2 * outer + core + 1) * quarter, :]
            turned[pl.ds(start, quarter), :] = block


def split_store(values, kept_ref, sent_ref):
    quarter = values.shape[0] // 4
    low = values.astype(jnp.bfloat16)
    for outer in range(2):
        sent_ref[outer] = low[outer * quarter : (outer + 1) * quarter, :]
        kept_ref[outer] = low[(2 + outer) * quarter : (3 + outer) * quarter, :]


def gate_kernel(place_ref, n2_ref, weight, cot_ref, act_ref, by_gate_ref, by_up_ref, kept_ref, sent_ref):
    rows, width = n2_ref.shape
    hidden = weight.shape[2] // 2
    start = pl.multiple_of(pl.program_id(0) * tile, 128)
    gate_weight = weight[:, :, pl.ds(start, tile)].reshape(width, tile)
    up_weight = weight[:, :, pl.ds(hidden + start, tile)].reshape(width, tile)
    part = rows // gate_parts
    for start in range(0, rows, part):
        places = slice(start, start + part)
        gate = dot_nn(n2_ref[places, :], gate_weight)
        up = dot_nn(n2_ref[places, :], up_weight)
        square = gate * gate
        turned = jnp.tanh(slope * gate * (1.0 + curve * square))
        halved = 0.5 * (1.0 + turned)
        value = gate * halved
        steep = halved + 0.5 * gate * (1.0 - turned * turned) * slope * (1.0 + 3.0 * curve * square)
        act_ref[places, :] = (value * up).astype(jnp.bfloat16)
        by_gate_ref[places, :] = up * steep
        by_up_ref[places, :] = value
    grad = dot_tn(act_ref[...], cot_ref[...]).astype(jnp.bfloat16)
    core = pl.program_id(0) % 2

    @pl.when(core == place_ref[1])
    def _():
        kept_ref[0] = grad

    @pl.when(core != place_ref[1])
    def _():
        sent_ref[0] = grad


def gate_forward(place, pieces, normed_two, cot_low):
    rows, width = normed_two.shape
    columns = pieces[0].shape[-1]
    hidden = columns // 2
    number = len(pieces)
    whole = pl.BlockSpec((rows, width), lambda step: (0, 0))
    column = pl.BlockSpec((rows, tile), lambda step: (0, step))
    half = pl.BlockSpec((1, tile, width), lambda step: (step // 2, 0, 0))
    assert hidden == 4 * tile

    def kernel(place_ref, *refs):
        n2_ref, cot_ref, *outs, full_ref, held, sems = refs[number:]
        filled(
            place_ref, refs[:number], full_ref, held, sems,
            lambda: gate_kernel(place_ref, n2_ref, held, cot_ref, *outs),
        )

    *results, full = pl.pallas_call(
        kernel,
        grid=(hidden // tile,),
        out_shape=(
            jax.ShapeDtypeStruct((rows, hidden), jnp.bfloat16),
            jax.ShapeDtypeStruct((rows, hidden), jnp.float32),
            jax.ShapeDtypeStruct((rows, hidden), jnp.float32),
            jax.ShapeDtypeStruct((2, tile, width), jnp.bfloat16),
            jax.ShapeDtypeStruct((2, tile, width), jnp.bfloat16),
            jax.ShapeDtypeStruct((32, width // 32, columns), jnp.bfloat16),
        ),
        in_specs=[scalars()] + [anywhere] * number + [whole, whole],
        out_specs=(column, column, column, half, half, anywhere),
        scratch_shapes=[
            pltpu.VMEM((32, width // 32, columns), jnp.bfloat16),
            pltpu.SemaphoreType.DMA((33,)),
        ],
        compiler_params=pltpu.CompilerParams(vmem_limit_bytes=48 * 2**20),
        cost_estimate=pl.CostEstimate(
            flops=6 * rows * width * hidden,
            bytes_accessed=rows * hidden * 10 + 8 * width * hidden,
            transcendentals=rows * hidden,
        ),
        name="gate_forward",
    )(place, *pieces, normed_two, cot_low)
    return (*results, full.reshape(width, columns))


def gate_back_kernel(
    place_ref, n2_ref, cot_ref, ff, by_gate_ref, by_up_ref, out_ref, kept_ref, sent_ref, turned
):
    step = pl.program_id(0)

    @pl.when(step == 0)
    def _():
        turned_rows(place_ref, n2_ref, turned)

    per = tile // ff.shape[1]
    weight = ff[pl.ds(step * per, per)].reshape(tile, ff.shape[2])
    incoming = dot_nt(cot_ref[...], weight)
    by_gate = (incoming * by_gate_ref[...]).astype(jnp.bfloat16)
    by_up = (incoming * by_up_ref[...]).astype(jnp.bfloat16)
    out_ref[0] = by_gate
    out_ref[1] = by_up
    split_store(dot_nn(turned[...], by_gate), kept_ref.at[:, :, :tile], sent_ref.at[:, :, :tile])
    split_store(dot_nn(turned[...], by_up), kept_ref.at[:, :, tile:], sent_ref.at[:, :, tile:])


def gate_back(place, pieces, normed_two, cot_low, by_gate, by_up):
    rows, width = normed_two.shape
    hidden = by_gate.shape[1]
    number = len(pieces)
    whole = pl.BlockSpec((rows, width), lambda step: (0, 0))
    column = pl.BlockSpec((rows, tile), lambda step: (0, step))
    half = pl.BlockSpec((2, width // 4, 2 * tile), lambda step: (0, 0, step))

    def kernel(place_ref, *refs):
        n2_ref, cot_ref, gate_ref, up_ref, *outs, full_ref, held, turned, sems = refs[number:]
        filled(
            place_ref, refs[:number], full_ref, held, sems,
            lambda: gate_back_kernel(
                place_ref, n2_ref, cot_ref, held, gate_ref, up_ref, *outs, turned
            ),
        )

    *results, full = pl.pallas_call(
        kernel,
        grid=(hidden // tile,),
        out_shape=(
            jax.ShapeDtypeStruct((2, rows, hidden), jnp.bfloat16),
            jax.ShapeDtypeStruct((2, width // 4, 2 * hidden), jnp.bfloat16),
            jax.ShapeDtypeStruct((2, width // 4, 2 * hidden), jnp.bfloat16),
            jax.ShapeDtypeStruct((32, hidden // 32, width), jnp.bfloat16),
        ),
        in_specs=[scalars()] + [anywhere] * number + [whole, whole, column, column],
        out_specs=(
            pl.BlockSpec((2, rows, tile), lambda step: (0, 0, step)),
            half,
            half,
            anywhere,
        ),
        scratch_shapes=[
            pltpu.VMEM((32, hidden // 32, width), jnp.bfloat16),
            pltpu.VMEM((width, rows), jnp.bfloat16),
            pltpu.SemaphoreType.DMA((33,)),
        ],
        compiler_params=pltpu.CompilerParams(vmem_limit_bytes=48 * 2**20),
        cost_estimate=pl.CostEstimate(
            flops=6 * rows * width * hidden,
            bytes_accessed=rows * hidden * 12 + 8 * width * hidden,
            transcendentals=0,
        ),
        name="gate_back",
    )(place, *pieces, normed_two, cot_low, by_gate, by_up)
    return (*results, full.reshape(hidden, width))


def norm_back(grads, values, gain, residual):
    spread = lax.rsqrt(jnp.mean(values * values, axis=-1, keepdims=True) + epsilon)
    scaled = grads * gain
    inner = jnp.mean(scaled * values, axis=-1, keepdims=True)
    gain_grad = jnp.sum(grads * (values * spread), axis=0, keepdims=True)
    return residual + spread * scaled - values * (spread * spread * spread * inner), gain_grad


def middle_back_kernel(
    gates_ref, weight_ref, middle_ref, cot_ref, gain_ref, out_weight_ref,
    grad_ref, low_ref, mixed_ref, gain_grad_ref,
):
    hidden = gates_ref.shape[2]
    total = dot_nt(gates_ref[0], weight_ref[:, :hidden])
    total = total + dot_nt(gates_ref[1], weight_ref[:, hidden:])
    grad, gain_grad = norm_back(total, middle_ref[...], gain_ref[...], cot_ref[...])
    grad_ref[...] = grad
    low_ref[...] = grad.astype(jnp.bfloat16)

    @pl.when(pl.program_id(0) == 0)
    def _():
        gain_grad_ref[...] = gain_grad

    @pl.when(pl.program_id(0) > 0)
    def _():
        gain_grad_ref[...] += gain_grad

    mixed_ref[...] = dot_nt(low_ref[...], out_weight_ref[...]).astype(jnp.bfloat16)


def middle_back(gates, full_in, middle, cotangent, gain, full_attention, *earlier):
    rows, width = middle.shape
    hidden = gates.shape[2]
    part = rows // row_parts
    block = pl.BlockSpec((part, width), lambda step: (step, 0))

    def kernel(*refs):
        middle_back_kernel(*refs[:6], *refs[6 + len(earlier) :])

    return pl.pallas_call(
        kernel,
        grid=(row_parts,),
        out_shape=(
            jax.ShapeDtypeStruct((rows, width), jnp.float32),
            jax.ShapeDtypeStruct((rows, width), jnp.bfloat16),
            jax.ShapeDtypeStruct((rows, width), jnp.bfloat16),
            jax.ShapeDtypeStruct((1, width), jnp.float32),
        ),
        in_specs=[
            pl.BlockSpec((2, part, hidden), lambda step: (0, step, 0)),
            pl.BlockSpec((width, 2 * hidden), lambda step: (0, 0)),
            block,
            block,
            pl.BlockSpec((1, width), lambda step: (0, 0)),
            pl.BlockSpec((width, width), lambda step: (0, 3)),
        ]
        + [anywhere] * len(earlier),
        out_specs=(block, block, block, pl.BlockSpec((1, width), lambda step: (0, 0))),
        compiler_params=pltpu.CompilerParams(vmem_limit_bytes=56 * 2**20),
        cost_estimate=pl.CostEstimate(
            flops=4 * rows * width * hidden + 2 * rows * width * width,
            bytes_accessed=rows * hidden * 4 + 4 * width * hidden + 18 * rows * width,
            transcendentals=0,
        ),
        name="middle_back",
    )(gates, full_in, middle, cotangent, gain.reshape(1, -1), full_attention, *earlier)


def scalars():
    return pl.BlockSpec(memory_space=pltpu.SMEM)


def project(place, pieces, normed):
    rows, width = normed.shape
    columns = pieces[0].shape[-1]
    number = len(pieces)

    def kernel(place_ref, *refs):
        normed_ref, out_ref, full_ref, held, sems = refs[number:]

        def body():
            start = pl.multiple_of(pl.program_id(0) * width, 128)
            weight = held[:, :, pl.ds(start, width)].reshape(width, width)
            out_ref[...] = dot_nn(normed_ref[...], weight).astype(jnp.bfloat16)

        filled(place_ref, refs[:number], full_ref, held, sems, body)

    projected, full = pl.pallas_call(
        kernel,
        grid=(3,),
        out_shape=(
            jax.ShapeDtypeStruct((rows, 3 * width), jnp.bfloat16),
            jax.ShapeDtypeStruct((32, width // 32, columns), jnp.bfloat16),
        ),
        in_specs=[scalars()]
        + [anywhere] * number
        + [pl.BlockSpec((rows, width), lambda step: (0, 0))],
        out_specs=(pl.BlockSpec((rows, width), lambda step: (0, step)), anywhere),
        scratch_shapes=[
            pltpu.VMEM((32, width // 32, columns), jnp.bfloat16),
            pltpu.SemaphoreType.DMA((33,)),
        ],
        compiler_params=pltpu.CompilerParams(vmem_limit_bytes=32 * 2**20),
        cost_estimate=pl.CostEstimate(
            flops=6 * rows * width * width,
            bytes_accessed=8 * rows * width + 4 * columns * width,
            transcendentals=0,
        ),
        name="project",
    )(place, *pieces, normed)
    return projected, full.reshape(width, columns)


def middle_kernel(rows_ref, mixed_ref, weight_ref, gain_ref, middle_ref, normed_ref):
    middle = rows_ref[...] + dot_nn(mixed_ref[...], weight_ref[...])
    spread = lax.rsqrt(jnp.mean(middle * middle, axis=-1, keepdims=True) + epsilon)
    middle_ref[...] = middle
    normed_ref[...] = (middle * spread * gain_ref[...]).astype(jnp.bfloat16)


def middle_forward(values, mixed, full_attention, gain, *earlier):
    rows, width = values.shape
    part = rows // 2
    block = pl.BlockSpec((part, width), lambda step: (step, 0))

    def kernel(*refs):
        middle_kernel(*refs[:4], *refs[4 + len(earlier) :])

    return pl.pallas_call(
        kernel,
        grid=(2,),
        out_shape=(
            jax.ShapeDtypeStruct((rows, width), jnp.float32),
            jax.ShapeDtypeStruct((rows, width), jnp.bfloat16),
        ),
        in_specs=[
            block,
            block,
            pl.BlockSpec((width, width), lambda step: (0, 3)),
            pl.BlockSpec((1, width), lambda step: (0, 0)),
        ]
        + [anywhere] * len(earlier),
        out_specs=(block, block),
        compiler_params=pltpu.CompilerParams(vmem_limit_bytes=32 * 2**20),
        cost_estimate=pl.CostEstimate(
            flops=2 * rows * width * width,
            bytes_accessed=12 * rows * width + 2 * width * width,
            transcendentals=0,
        ),
        name="middle_forward",
    )(values, mixed, full_attention, gain.reshape(1, -1), *earlier)


def attention_grads_kernel(
    place_ref, normed_ref, grads_ref, mixed_ref, low_ref, kept_ref, sent_ref, turned
):
    step = pl.program_id(0)
    last = pl.num_programs(0) - 1

    @pl.when(step == 0)
    def _():
        turned_rows(place_ref, normed_ref, turned)

    @pl.when(step < last)
    def _():
        split_store(dot_nn(turned[...], grads_ref[0]), kept_ref, sent_ref)

    @pl.when(step == last)
    def _():
        turned_rows(place_ref, mixed_ref, turned)
        split_store(dot_nn(turned[...], low_ref[...]), kept_ref, sent_ref)


def attention_grads(place, normed, grad_projected, mixed, grad_low):
    rows, width = normed.shape
    whole = pl.BlockSpec((rows, width), lambda step: (0, 0))
    half = pl.BlockSpec((2, width // 4, width), lambda step: (0, 0, step))
    shape = jax.ShapeDtypeStruct((2, width // 4, 4 * width), jnp.bfloat16)
    return pl.pallas_call(
        attention_grads_kernel,
        grid=(4,),
        out_shape=(shape, shape),
        in_specs=[
            scalars(),
            whole,
            pl.BlockSpec((1, rows, width), lambda step: (jnp.minimum(step, 2), 0, 0)),
            whole,
            whole,
        ],
        out_specs=(half, half),
        scratch_shapes=[pltpu.VMEM((width, rows), jnp.bfloat16)],
        compiler_params=pltpu.CompilerParams(vmem_limit_bytes=32 * 2**20),
        cost_estimate=pl.CostEstimate(
            flops=8 * rows * width * width,
            bytes_accessed=12 * rows * width + 8 * width * width,
            transcendentals=0,
        ),
        name="attention_grads",
    )(place, normed, grad_projected, mixed, grad_low)


def input_back_kernel(grads_ref, weight_ref, rows_ref, residual_ref, gain_ref, out_ref, gain_grad_ref):
    width = rows_ref.shape[1]
    total = dot_nt(grads_ref[0], weight_ref[:, :width])
    for part in (1, 2):
        total = total + dot_nt(grads_ref[part], weight_ref[:, part * width : (part + 1) * width])
    grad, gain_grad = norm_back(total, rows_ref[...], gain_ref[...], residual_ref[...])
    out_ref[...] = grad

    @pl.when(pl.program_id(0) == 0)
    def _():
        gain_grad_ref[...] = gain_grad

    @pl.when(pl.program_id(0) > 0)
    def _():
        gain_grad_ref[...] += gain_grad


def input_back(grad_projected, full_attention, values, residual, gain, *earlier):
    rows, width = values.shape
    part = rows // 2
    block = pl.BlockSpec((part, width), lambda step: (step, 0))

    def kernel(*refs):
        input_back_kernel(*refs[:5], *refs[5 + len(earlier) :])

    return pl.pallas_call(
        kernel,
        grid=(2,),
        out_shape=(
            jax.ShapeDtypeStruct((rows, width), jnp.float32),
            jax.ShapeDtypeStruct((1, width), jnp.float32),
        ),
        in_specs=[
            pl.BlockSpec((3, part, width), lambda step: (0, step, 0)),
            pl.BlockSpec((width, 3 * width), lambda step: (0, 0)),
            block,
            block,
            pl.BlockSpec((1, width), lambda step: (0, 0)),
        ]
        + [anywhere] * len(earlier),
        out_specs=(block, pl.BlockSpec((1, width), lambda step: (0, 0))),
        compiler_params=pltpu.CompilerParams(vmem_limit_bytes=40 * 2**20),
        cost_estimate=pl.CostEstimate(
            flops=6 * rows * width * width,
            bytes_accessed=18 * rows * width + 6 * width * width,
            transcendentals=0,
        ),
        name="input_back",
    )(grad_projected, full_attention, values, residual, gain.reshape(1, -1), *earlier)


def body(
    doc_inputs,
    query_inputs,
    doc_mask,
    query_lengths,
    doc_cotangent,
    query_cotangent,
    qkv_weight,
    out_weight,
    in_weight,
    ff_weight,
    attn_gain,
    ffn_gain,
    bias_table,
):
    doc_count, doc_length, model_width = doc_inputs.shape
    group_count, group_length = (query_inputs.shape[0], query_inputs.shape[1])
    head_count = bias_table.shape[1]
    doc_rows = doc_count * doc_length
    low = jnp.bfloat16
    routed = hand_routed()
    place = own_place() if routed else (0, 0, 0, 0)
    place_vector = jnp.stack([jnp.asarray(index, jnp.int32) for index in place])

    attention_shard = jnp.concatenate([qkv_weight, out_weight], axis=1).astype(low)
    in_shard = in_weight.astype(low)
    ff_shard = ff_weight.astype(low)

    values = jnp.concatenate(
        [doc_inputs.reshape(doc_rows, model_width), query_inputs.reshape(-1, model_width)], axis=0
    )
    cotangent = jnp.concatenate(
        [doc_cotangent.reshape(doc_rows, model_width), query_cotangent.reshape(-1, model_width)],
        axis=0,
    )
    cot_low = cotangent.astype(low)
    spread = lax.rsqrt(jnp.mean(values * values, axis=-1, keepdims=True) + epsilon)
    normed = (values * spread * attn_gain).astype(low)
    places = jnp.arange(group_length, dtype=jnp.int32)
    query_mask = places[None, :] < query_lengths[:, None]
    onehot = lines_onehot(bias_table.shape[0])
    lines = jnp.einsum("pn,nh->hp", onehot, bias_table, precision=highest)
    lines = lines.reshape(head_count // 2, 2, 4 * count)
    doc_masking = jnp.where(doc_mask > 0, 0.0, -1e9).astype(jnp.float32)
    query_masking = jnp.where(query_mask, 0.0, -1e9).astype(jnp.float32)
    query_masking = query_masking.reshape(-1, 1, count)

    if routed:
        column_a = gather_column(attention_shard)
        column_a, normed, lines, doc_masking, query_masking, cotangent, cot_low, in_shard = together(
            column_a, normed, lines, doc_masking, query_masking, cotangent, cot_low, in_shard
        )
        near_a = gather_near(place, *gather_plane(place, attention_shard, column_a))
        column_i = gather_column(in_shard)
        core_a = gather_core(*near_a)
        far_a = gather_far(*near_a)
        column_i, far_a, core_a, ff_shard = together(column_i, far_a, core_a, ff_shard)
        pieces = gather_order(near_a, far_a, core_a, gather_core(*far_a))
        plane_i = gather_plane(place, in_shard, column_i)
    else:
        pieces = (split_rows(lax.all_gather(attention_shard, both, axis=0, tiled=True)),)
    projected, full_attention = project(place_vector, pieces, normed)
    if routed:
        plane_i, projected, ff_shard = together(plane_i, projected, ff_shard)
        near_i = gather_near(place, *plane_i)
        far_i = gather_far(*near_i)
        column_f = gather_column(ff_shard)
        core_i = gather_core(*near_i)
    mixed, doc_probs, query_probs = attend(
        projected, lines, doc_masking, query_masking, group_length
    )
    if routed:
        mixed, far_i, column_f = together(mixed, far_i, column_f)
        plane_f = gather_plane(place, ff_shard, column_f)
        pieces = gather_order(near_i, far_i, core_i, gather_core(*far_i))
    else:
        pieces = (split_rows(lax.all_gather(in_shard, both, axis=0, tiled=True)),)
    middle, normed_two = middle_forward(values, mixed, full_attention, ffn_gain)
    if routed:
        pieces, normed_two, plane_f = together(pieces, normed_two, plane_f)
        near_f = gather_near(place, *plane_f)
        far_f = gather_far(*near_f)
    activated, by_gate, by_up, kept, sent, full_in = gate_forward(
        place_vector, pieces, normed_two, cot_low
    )
    if routed:
        far_f, by_gate, kept, sent = together(far_f, by_gate, kept, sent)
        pieces = gather_order(near_f, far_f, gather_core(*near_f), gather_core(*far_f))
        ff_grads = Scatter(kept, sent, place)
        got_f = ff_grads.core()
    else:
        pieces = (split_rows(lax.all_gather(ff_shard, both, axis=0, tiled=True)),)
        grad_ff = joined_halves(kept, sent)
    gates, kept, sent, full_ff = gate_back(
        place_vector, pieces, normed_two, cot_low, by_gate, by_up
    )
    if routed:
        gates, kept, sent, got_f = together(gates, kept, sent, got_f)
        in_grads = Scatter(kept, sent, place)
        near_f = ff_grads.plane(got_f)
        got_i = in_grads.core()
    else:
        grad_in = joined_halves(kept, sent)
    grad_middle, grad_middle_low, grad_mixed, grad_ffn_gain = middle_back(
        gates, full_in, middle, cotangent, ffn_gain, full_attention
    )
    if routed:
        grad_mixed, near_f, got_i = together(grad_mixed, near_f, got_i)
        far_f = ff_grads.far(got_f, near_f)
        near_i = in_grads.plane(got_i)
    grad_projected, grad_lines = attend_back(
        projected, grad_mixed, doc_probs, query_probs, doc_length
    )
    if routed:
        grad_projected, grad_lines, far_f, near_i = together(
            grad_projected, grad_lines, far_f, near_i
        )
        far_i = in_grads.far(got_i, near_i)
        shares_f = ff_grads.column(got_f, near_f, far_f)
    kept, sent = attention_grads(place_vector, normed, grad_projected, mixed, grad_middle_low)
    if routed:
        kept, sent, far_i = together(kept, sent, far_i)
        attention = Scatter(kept, sent, place)
        got_a = attention.core()
        got_a, shares_f, grad_projected, grad_lines = together(
            got_a, shares_f, grad_projected, grad_lines
        )
        near_a = attention.plane(got_a)
        shares_i = in_grads.column(got_i, near_i, far_i)
    grad_inputs, grad_attn_gain = input_back(
        grad_projected, full_attention, values, grad_middle, attn_gain
    )
    grad_table = jnp.einsum(
        "pn,hp->nh", onehot, grad_lines.reshape(head_count, 4 * count), precision=highest
    )
    small = jnp.concatenate([grad_attn_gain[0], grad_ffn_gain[0], grad_table.reshape(-1)])
    if routed:
        near_a, small, activated = together(near_a, small, activated)
        far_a = attention.far(got_a, near_a)
        small = add_flipped(small, {"dc": 1}, {"dz": 1})
    outputs = middle + dot_nn(activated, full_ff)
    if routed:
        far_a, small, outputs, shares_i = together(far_a, small, outputs, shares_i)
        shares_a = attention.column(got_a, near_a, far_a)
        small = add_flipped(small, {"dx": 1}, {"dy": 1}, {"dz": 2})
        ff_grad_shard = summed(*shares_f)
        in_grad_shard = summed(*shares_i)
        attention_grad_shard = summed(*shares_a)
    else:
        scatter = functools.partial(
            lax.psum_scatter, axis_name=both, scatter_dimension=0, tiled=True
        )
        ff_grad_shard = scatter(grad_ff)
        in_grad_shard = scatter(grad_in)
        attention_grad_shard = scatter(joined_halves(kept, sent))
        small = lax.psum(small, both)
    in_grad_shard = in_grad_shard.reshape(in_weight.shape[0], -1, 2, tile)
    in_grad_shard = jnp.swapaxes(in_grad_shard, 1, 2).reshape(in_weight.shape)
    return (
        outputs[:doc_rows].reshape(doc_inputs.shape),
        outputs[doc_rows:].reshape(query_inputs.shape),
        grad_inputs[:doc_rows].reshape(doc_inputs.shape),
        grad_inputs[doc_rows:].reshape(query_inputs.shape),
        attention_grad_shard[:, : 3 * model_width],
        attention_grad_shard[:, 3 * model_width :],
        in_grad_shard,
        ff_grad_shard,
        small[:model_width],
        small[model_width : 2 * model_width],
        small[2 * model_width :].reshape(bias_table.shape),
    )


def solution(mesh):
    placed = (
        P(("dp", "fsdp"), None, None),
        P(("dp", "fsdp"), None, None),
        P(("dp", "fsdp"), None),
        P(("dp", "fsdp")),
        P(("dp", "fsdp"), None, None),
        P(("dp", "fsdp"), None, None),
        P(("dp", "fsdp"), None),
        P(("dp", "fsdp"), None),
        P(("dp", "fsdp"), None),
        P(("dp", "fsdp"), None),
        P(),
        P(),
        P(),
    )
    return jax.shard_map(
        body,
        mesh=mesh,
        in_specs=placed,
        out_specs=(
            P(("dp", "fsdp"), None, None),
            P(("dp", "fsdp"), None, None),
            P(("dp", "fsdp"), None, None),
            P(("dp", "fsdp"), None, None),
            P(("dp", "fsdp"), None),
            P(("dp", "fsdp"), None),
            P(("dp", "fsdp"), None),
            P(("dp", "fsdp"), None),
            P(),
            P(),
            P(),
        ),
        check_vma=False,
    )
```

```python
import functools
import math

import jax
import jax.numpy as jnp
from jax import lax
from jax.experimental import pallas as pl
from jax.experimental.pallas import tpu as pltpu
from jax.sharding import PartitionSpec as P

both = ("dp", "fsdp")
epsilon = 1e-06
highest = lax.Precision.HIGHEST
anywhere = pl.BlockSpec(memory_space=pl.ANY)


def place_index(y, c, z, x):
    return ((y * 2 + c) * 4 + z) * 2 + x


def flip_pairs(dy=0, dc=0, dz=0, dx=0):
    pairs = []
    for y in range(2):
        for c in range(2):
            for z in range(4):
                for x in range(2):
                    pairs.append(
                        (place_index(y, c, z, x), place_index(y ^ dy, c ^ dc, z ^ dz, x ^ dx))
                    )
    return pairs


def swap(values, **flips):
    return lax.ppermute(values, both, flip_pairs(**flips))


def hand_routed():
    return (lax.axis_size("dp"), lax.axis_size("fsdp")) == (4, 8)


def own_place():
    outer = lax.axis_index("dp")
    inner = lax.axis_index("fsdp")
    return outer // 2, outer % 2, inner // 2, inner % 2


def after(values, *earlier):
    return lax.optimization_barrier((values, *earlier))[0]


def in_hbm(*values):
    return [pltpu.with_memory_space_constraint(value, pltpu.HBM) for value in values]


def together(*values):
    return lax.optimization_barrier(values)


def fill_copies(place_ref, pieces, target, sems):
    if len(pieces) == 1:
        return [pltpu.make_async_copy(pieces[0], target, sems.at[0])]
    y, c, z, x = place_ref[0], place_ref[1], place_ref[2], place_ref[3]
    copies = []
    even = z - z % 2
    for number, piece in enumerate(pieces):
        core = c ^ (number // 4)
        kind = number % 4
        if kind < 2:
            where = target.at[y ^ kind, core, pl.ds(even, 2)]
        else:
            where = target.at[:, core, pl.ds(even ^ 2, 2), x ^ (kind - 2)]
        copies.append(pltpu.make_async_copy(piece, where, sems.at[number]))
    return copies


def filled(place_ref, pieces, full_ref, held, sems, body):
    step = pl.program_id(0)
    kept = pltpu.make_async_copy(held, full_ref, sems.at[8])

    @pl.when(step == 0)
    def _():
        copies = fill_copies(place_ref, pieces, held, sems)
        for copy in copies:
            copy.start()
        for copy in copies:
            copy.wait()
        kept.start()

    body()

    @pl.when(step == pl.num_programs(0) - 1)
    def _():
        kept.wait()


def emit(slots, targets, sems):
    step, rows = pl.program_id(0), slots.shape[1]
    copies = []
    for number in range(slots.shape[0]):
        start = 0
        for target in targets:
            low = max(number * rows, start)
            high = min((number + 1) * rows, start + target.shape[0])
            if low < high:
                source = slots.at[number, pl.ds(low - number * rows, high - low)]
                where = target.at[pl.ds(low - start, high - low)]
                copy = pltpu.make_async_copy(source, where, sems.at[len(copies)])
                copies.append((number, copy))
            start += target.shape[0]
    for number in range(slots.shape[0]):

        @pl.when(step == number)
        def _():
            for owner, copy in copies:
                if owner == number:
                    copy.start()

    @pl.when(step == slots.shape[0] - 1)
    def _():
        for _, copy in copies:
            copy.wait()


def gather_order(near, far, core_near, core_far):
    return (near[0], far[0], near[1], far[1], core_near[0], core_far[0], core_near[1], core_far[1])


def slab(columns, rows):
    return (2, 2, 4, 2, rows // 32, columns)


def split_rows(full):
    return full.reshape(slab(full.shape[1], full.shape[0]))


def in_order(own, other, index):
    odd = index % 2 == 1
    return jnp.where(odd, other, own), jnp.where(odd, own, other)


def gather_column(shard):
    return tuple(swap(shard, dz=flip) for flip in (1, 2, 3))


def gather_plane(place, shard, column):
    first = jnp.stack(in_order(shard, column[0], place[2]))
    second = jnp.stack(in_order(column[1], column[2], place[2]))
    return first, second, swap(first, dx=1), swap(second, dy=1)


def gather_near(place, first, second, first_near, second_near):
    even, odd = in_order(first, first_near, place[3])
    first = jnp.stack([even[0], odd[0], even[1], odd[1]]).reshape(2, 2, *first.shape[1:])
    second = jnp.stack(in_order(second, second_near, place[0]))
    return first, second


def gather_far(first, second):
    return swap(first, dy=1), swap(second, dx=1)


def gather_core(*pieces):
    return tuple(swap(piece, dc=1) for piece in pieces)


def summed(*terms):
    total = terms[0].astype(jnp.float32)
    for term in terms[1:]:
        total = total + term.astype(jnp.float32)
    return total


def joined_halves(kept, sent):
    return jnp.stack([kept, sent], axis=1).reshape(-1, kept.shape[2]).astype(jnp.float32)


def route(name, place, sources, targets, body, scratch=()):
    def spec(array, lead, pick):
        block = (*lead, *array.shape[-2:])
        return pl.BlockSpec(block, lambda step, where: (*pick(where), 0, 0))

    return pl.pallas_call(
        body,
        grid_spec=pltpu.PrefetchScalarGridSpec(
            num_scalar_prefetch=1,
            grid=(1,),
            in_specs=[spec(*source) for source in sources],
            out_specs=[spec(*target) for target in targets],
            scratch_shapes=scratch,
        ),
        out_shape=[target[0] for target in targets],
        compiler_params=pltpu.CompilerParams(vmem_limit_bytes=20 * 2**20),
        cost_estimate=pl.CostEstimate(
            flops=0,
            bytes_accessed=8 * len(sources) * math.prod(sources[0][0].shape[-2:]),
            transcendentals=0,
        ),
        name=name,
    )(place, *[source[0] for source in sources])


def whole_block(target):
    lead = target.shape[:-2]
    return target, lead, lambda where: (0,) * len(lead)


def store_sum(out_ref, *refs):
    blocks = math.prod(refs[0].shape[:-2])
    for number in range(blocks):
        terms = []
        for ref in (out_ref, *refs):
            index, rest = [], number
            for size in reversed(ref.shape[:-2]):
                index.insert(0, rest % size)
                rest //= size
            terms.append(ref.at[tuple(index)])
        terms[0][...] = summed(*[term[...] for term in terms[1:]]).astype(out_ref.dtype)


class Scatter:
    def __init__(self, kept, sent, place):
        self.place = place
        self.block = (kept.shape[1] // 8, kept.shape[2])
        self.shape = (2, 4, 2, *self.block)
        self.kept = kept.reshape(self.shape)
        self.sent = sent

    def target(self, *lead, dtype=jnp.bfloat16):
        return jax.ShapeDtypeStruct((*lead, *self.block), dtype)

    def both(self, got, lead, pick):
        return [(in_hbm(self.kept)[0], lead, pick), (got, lead, pick)]

    def core(self):
        return swap(self.sent, dc=1).reshape(self.shape)

    def plane(self, got):
        def body(place_ref, *refs):
            store_sum(refs[4], *refs[0:2])
            store_sum(refs[5], *refs[2:4])

        sources = self.both(got, (2, 2, 1), lambda where: (0, 0, 1 - where[3]))
        sources += self.both(got, (1, 2, 2), lambda where: (1 - where[0], 1, 0))
        target = whole_block(self.target(2, 2))
        one, two = route("plane", self.place, sources, [target, target], body)
        return swap(one, dx=1), swap(two, dy=1)

    def far(self, got, near):
        def body(place_ref, *refs):
            store_sum(refs[6], *refs[0:3])
            store_sum(refs[7], *refs[3:6])

        sources = [
            *self.both(got, (1, 2, 1), lambda where: (1 - where[0], 0, where[3])),
            (near[0], (1, 2), lambda where: (1 - where[0], 0)),
            *self.both(got, (1, 2, 1), lambda where: (where[0], 1, 1 - where[3])),
            (near[1], (2, 1), lambda where: (0, 1 - where[3])),
        ]
        target = whole_block(self.target(2))
        one, two = route("far", self.place, sources, [target, target], body)
        return swap(one, dy=1), swap(two, dx=1)

    def column_sources(self, near, far):
        return [
            (near[0], (1, 2), lambda where: (where[0], 0)),
            (far[0], (2,), lambda where: (0,)),
            (near[1], (2, 1), lambda where: (0, where[3])),
            (far[1], (2,), lambda where: (0,)),
        ]

    def column_terms(self, row, refs):
        if row < 2:
            return refs[0].at[0, row], refs[1].at[row]
        return refs[2].at[row - 2, 0], refs[3].at[row - 2]

    def column_sums(self, got, near, far):
        sources = self.both(got, (1, 4, 1), lambda where: (where[0], 0, where[3]))
        sources += self.column_sources(near, far)
        number = len(sources)

        def body(place_ref, *refs):
            *outs, total = refs[number:]
            for row in range(4):
                terms = (refs[0].at[0, row, 0], refs[1].at[0, row, 0])
                terms += self.column_terms(row, refs[2:number])
                total[row] = summed(*[term[...] for term in terms])
            for flip, out in enumerate(outs):
                out[...] = total[place_ref[2] ^ flip].astype(out.dtype)

        targets = [self.target(dtype=jnp.float32)] + [self.target()] * 3
        targets = [whole_block(target) for target in targets]
        scratch = [pltpu.VMEM((4, *self.block), jnp.float32)]
        return tuple(route("column", self.place, sources, targets, body, scratch))

    def column(self, sums):
        return sums[0], *[swap(share, dz=flip) for flip, share in zip((1, 2, 3), sums[1:])]


class NarrowScatter(Scatter):
    def plane(self, got):
        def body(place_ref, *refs):
            store_sum(refs[2], *refs[0:2])

        sources = self.both(got, (2, 4, 1), lambda where: (0, 0, 1 - where[3]))
        target = whole_block(self.target(2, 4))
        (sums,) = route("plane", self.place, sources, [target], body)
        return swap(sums, dx=1)

    def far_sums(self, got, near):
        def body(place_ref, *refs):
            store_sum(refs[3], *refs[0:3])

        sources = self.both(got, (1, 4, 1), lambda where: (1 - where[0], 0, where[3]))
        sources.append((near, (1, 4), lambda where: (1 - where[0], 0)))
        return route("far", self.place, sources, [whole_block(self.target(4))], body)[0]

    def far(self, sums):
        return swap(sums, dy=1)

    def column_sources(self, near, far):
        return [
            (near, (1, 4), lambda where: (where[0], 0)),
            (far, (4,), lambda where: (0,)),
        ]

    def column_terms(self, row, refs):
        return refs[0].at[0, row], refs[1].at[row]


def add_flipped(values, *steps):
    for flips in steps:
        values = values + swap(values, **flips)
    return values


count = 128


def relative_places():
    places = jnp.arange(4 * count, dtype=jnp.int32)
    return jnp.where(places < 3 * count, places - count, places - 5 * count)


def bucket_of(relative):
    distance = jnp.abs(relative)
    larger = jnp.zeros_like(distance)
    for threshold in (12, 16, 23, 32, 46, 64, 91):
        larger = larger + (distance >= threshold).astype(jnp.int32)
    bucket = jnp.where(distance < 8, distance, 8 + larger)
    return bucket + 16 * (relative > 0).astype(jnp.int32)


def lines_onehot(bucket_count):
    labels = jnp.arange(bucket_count, dtype=jnp.int32)
    return (bucket_of(relative_places())[:, None] == labels).astype(jnp.float32)


def own_lanes(head, shape):
    lanes = lax.broadcasted_iota(jnp.int32, shape, 1)
    return lanes < shape[1] // 2 if head == 0 else lanes >= shape[1] // 2


def keep_lanes(head, values):
    return jnp.where(own_lanes(head, values.shape), values, jnp.zeros_like(values))


def both_heads(values):
    return jnp.concatenate([keep_lanes(0, values), keep_lanes(1, values)], axis=0)


def joined(stacked):
    first, second = jnp.split(stacked, 2, axis=0)
    return jnp.where(own_lanes(0, first.shape), first, second).astype(jnp.bfloat16)


def softmax_rows(scores):
    raised = jnp.exp(scores - jnp.max(scores, axis=-1, keepdims=True))
    return raised * (1.0 / jnp.sum(raised, axis=-1, keepdims=True))


def dot_nt(left, right):
    return lax.dot_general(
        left, right, (((1,), (1,)), ((), ())), preferred_element_type=jnp.float32
    )


def dot_nn(left, right):
    return jnp.dot(left, right, preferred_element_type=jnp.float32)


def attend_kernel(
    docs, length, group, q_ref, k_ref, v_ref, line_ref, mask_ref, query_mask_ref,
    mixed_ref, doc_probs_ref, query_probs_ref, scores_scratch, probs_scratch,
):
    blocks = length // count
    query_start = docs * length
    query_blocks = (q_ref.shape[0] - query_start) // count
    row_group = lax.broadcasted_iota(jnp.int32, (count, count), 0) // group
    column_group = lax.broadcasted_iota(jnp.int32, (count, count), 1) // group
    bands, edges = [], []
    for head in range(2):
        line = line_ref[0, head : head + 1, :]
        band = pltpu.roll(
            jnp.broadcast_to(line, (count, 4 * count)), 0, 1, stride=1, stride_axis=0
        )
        bands.append(band)
        edges.append(
            (
                jnp.broadcast_to(line[:, 4 * count - 1 :], (1, count)),
                jnp.broadcast_to(line[:, 3 * count - 1 : 3 * count], (1, count)),
            )
        )
    for doc in range(docs):
        base = doc * length
        whole = slice(base, base + length)
        masking = mask_ref[doc : doc + 1, :]
        scores_scratch[...] = dot_nt(both_heads(q_ref[whole, :]), k_ref[whole, :])
        for head in range(2):
            for row in range(blocks):
                rows = slice(row * count, (row + 1) * count)
                stacked = slice(head * length + row * count, head * length + (row + 1) * count)
                shifted = []
                for column in range(blocks):
                    columns = slice(column * count, (column + 1) * count)
                    away = column - row
                    block = scores_scratch[stacked, columns]
                    if abs(away) > 1:
                        block = block + (edges[head][away > 0] + masking[:, columns])
                    else:
                        start = (away + 1) * count
                        block = block + bands[head][:, start : start + count]
                        block = block + masking[:, columns]
                    shifted.append(block)
                probs = softmax_rows(jnp.concatenate(shifted, axis=1))
                doc_probs_ref[head, base + row * count : base + (row + 1) * count, :] = probs
                probs_scratch[stacked, :] = probs.astype(jnp.bfloat16)
        mixed_ref[whole, :] = joined(dot_nn(probs_scratch[...], v_ref[whole, :]))
    for block in range(query_blocks):
        rows = slice(query_start + block * count, query_start + (block + 1) * count)
        masking = query_mask_ref[block]
        scores = dot_nt(both_heads(q_ref[rows, :]), k_ref[rows, :])
        low = []
        for head in range(2):
            bias = jnp.where(
                row_group == column_group, bands[head][:, count : 2 * count], -1e9
            )
            probs = softmax_rows(scores[head * count : (head + 1) * count, :] + bias + masking)
            query_probs_ref[head, block * count : (block + 1) * count, :] = probs
            low.append(probs.astype(jnp.bfloat16))
        mixed_ref[rows, :] = joined(dot_nn(jnp.concatenate(low, axis=0), v_ref[rows, :]))


def pair_spec(rows, offset):
    return pl.BlockSpec((rows, 2 * 64), lambda pair: (0, offset + pair))


def attend(projected, lines, doc_mask, query_mask, group):
    docs, length = doc_mask.shape
    rows, width = projected.shape[0], projected.shape[1] // 3
    pairs = lines.shape[0]
    query_rows = rows - docs * length
    return pl.pallas_call(
        functools.partial(attend_kernel, docs, length, group),
        grid=(pairs,),
        out_shape=(
            pltpu.HBM((rows, width), jnp.bfloat16),
            pltpu.HBM((2 * pairs, docs * length, length), jnp.float32),
            pltpu.HBM((2 * pairs, query_rows, count), jnp.float32),
        ),
        in_specs=[
            pair_spec(rows, 0),
            pair_spec(rows, pairs),
            pair_spec(rows, 2 * pairs),
            pl.BlockSpec((1, 2, 4 * count), lambda pair: (pair, 0, 0)),
            pl.BlockSpec((docs, length), lambda pair: (0, 0)),
            pl.BlockSpec(query_mask.shape, lambda pair: (0, 0, 0)),
        ],
        out_specs=(
            pair_spec(rows, 0),
            pl.BlockSpec((2, docs * length, length), lambda pair: (pair, 0, 0)),
            pl.BlockSpec((2, query_rows, count), lambda pair: (pair, 0, 0)),
        ),
        scratch_shapes=[
            pltpu.VMEM((2 * length, length), jnp.float32),
            pltpu.VMEM((2 * length, length), jnp.bfloat16),
        ],
        compiler_params=pltpu.CompilerParams(vmem_limit_bytes=18 * 2**20),
        cost_estimate=pl.CostEstimate(
            flops=2 * 2 * pairs * (docs * length * length + query_rows * count) * 128 * 2,
            bytes_accessed=rows * width * 8 + 8 * pairs * docs * length * length,
            transcendentals=2 * pairs * (docs * length * length + query_rows * count),
        ),
        name="attend",
    )(*in_hbm(projected, projected, projected), lines, doc_mask, query_mask)


def attend_back_kernel(
    docs, length, q_ref, k_ref, v_ref, grad_ref, doc_probs_ref, query_probs_ref, onehot_ref,
    out_ref, table_ref, grads_scratch, scores_scratch, probs_scratch, lines_scratch,
):
    blocks = length // count
    query_start = docs * length
    query_blocks = (q_ref.shape[0] - query_start) // count
    low = jnp.bfloat16
    half = q_ref.shape[1] // 2
    band = [[None] * 5, [None] * 5]

    def gather(head, place, block):
        held = band[head][place]
        band[head][place] = block if held is None else held + block

    def backward(probs, grad_probs):
        product = probs * grad_probs
        return product - probs * jnp.sum(product, axis=-1, keepdims=True)

    for doc in range(docs):
        base = doc * length
        whole = slice(base, base + length)
        grads_scratch[...] = dot_nt(both_heads(grad_ref[whole, :]), v_ref[whole, :])
        for head in range(2):
            for row in range(blocks):
                rows = slice(base + row * count, base + (row + 1) * count)
                stacked = slice(head * length + row * count, head * length + (row + 1) * count)
                probs = doc_probs_ref[head, rows, :]
                scores = backward(probs, grads_scratch[stacked, :])
                for column in range(blocks):
                    away = max(-2, min(2, column - row))
                    block = scores[:, column * count : (column + 1) * count]
                    if abs(away) == 2:
                        block = jnp.sum(block.reshape(count // 8, 8, count), axis=0)
                    gather(head, away + 2, block)
                scores_scratch[stacked, :] = scores.astype(low)
                probs_scratch[stacked, :] = probs.astype(low)
        out_ref[0, whole, :] = joined(dot_nn(scores_scratch[...], k_ref[whole, :]))
        q_turned = q_ref[whole, :].T
        grad_turned = grad_ref[whole, :].T
        grad_k, grad_v = [], []
        for head in range(2):
            own = slice(head * half, (head + 1) * half)
            stacked = slice(head * length, (head + 1) * length)
            grad_k.append(dot_nn(q_turned[own, :], scores_scratch[stacked, :]))
            grad_v.append(dot_nn(grad_turned[own, :], probs_scratch[stacked, :]))
        out_ref[1, whole, :] = jnp.concatenate(grad_k, axis=0).astype(low).T
        out_ref[2, whole, :] = jnp.concatenate(grad_v, axis=0).astype(low).T
    for block in range(query_blocks):
        rows = slice(query_start + block * count, query_start + (block + 1) * count)
        grad_probs = dot_nt(both_heads(grad_ref[rows, :]), v_ref[rows, :])
        low_scores, low_probs = [], []
        for head in range(2):
            probs = query_probs_ref[head, block * count : (block + 1) * count, :]
            scores = backward(probs, grad_probs[head * count : (head + 1) * count, :])
            gather(head, 2, scores)
            low_scores.append(scores.astype(low))
            low_probs.append(probs.astype(low))
        out_ref[0, rows, :] = joined(dot_nn(jnp.concatenate(low_scores, axis=0), k_ref[rows, :]))
        turned = jnp.concatenate(low_scores, axis=1).T
        turned = jnp.concatenate([turned, jnp.concatenate(low_probs, axis=1).T], axis=1)
        empty = jnp.zeros((count, 2 * half), low)
        weights = jnp.concatenate(
            [
                jnp.concatenate([q_ref[rows, :], empty], axis=1),
                jnp.concatenate([empty, grad_ref[rows, :]], axis=1),
            ],
            axis=0,
        )
        both_grads = dot_nn(turned, weights)
        out_ref[1, rows, :] = joined(both_grads[:, : 2 * half])
        out_ref[2, rows, :] = joined(both_grads[:, 2 * half :])
    lines = []
    for head in range(2):
        below, before, middle, after, above = band[head]
        wide = jnp.concatenate([before, middle, after, jnp.zeros_like(middle)], axis=1)
        eights = [wide[:8]]
        for start in range(8, count, 8):
            eights.append(pltpu.roll(wide[start : start + 8], 4 * count - start, 1))
        wide = sum(eights)
        wide = jnp.concatenate([wide[7 - row : 8 - row] for row in range(8)], axis=0)
        wide = pltpu.roll(wide, 4 * count - 7, 1, stride=1, stride_axis=0)
        wide = jnp.sum(wide, axis=0, keepdims=True)
        far = jnp.concatenate(
            [
                jnp.zeros((1, 2 * count), jnp.float32),
                jnp.sum(above, axis=0, keepdims=True),
                jnp.sum(below, axis=0, keepdims=True),
            ],
            axis=1,
        )
        lines.append(wide + far)
    pair = pl.program_id(0)
    lines_scratch[pair] = jnp.concatenate(lines, axis=0)

    @pl.when(pair == pl.num_programs(0) - 1)
    def _():
        table_ref[...] = jnp.dot(
            lines_scratch[...].reshape(-1, 4 * count),
            onehot_ref[...],
            precision=highest,
            preferred_element_type=jnp.float32,
        ).reshape(table_ref.shape)


def attend_back(projected, grad_mixed, doc_probs, query_probs, onehot, length):
    rows, width = grad_mixed.shape
    pairs = doc_probs.shape[0] // 2
    docs = doc_probs.shape[1] // length
    query_rows = query_probs.shape[1]

    return pl.pallas_call(
        functools.partial(attend_back_kernel, docs, length),
        grid=(pairs,),
        out_shape=(
            pltpu.HBM((3, rows, width), jnp.bfloat16),
            pltpu.HBM((pairs, 2, onehot.shape[1]), jnp.float32),
        ),
        in_specs=[
            pair_spec(rows, 0),
            pair_spec(rows, pairs),
            pair_spec(rows, 2 * pairs),
            pair_spec(rows, 0),
            pl.BlockSpec((2, docs * length, length), lambda pair: (pair, 0, 0)),
            pl.BlockSpec((2, query_rows, count), lambda pair: (pair, 0, 0)),
            pl.BlockSpec(onehot.shape, lambda pair: (0, 0)),
        ],
        out_specs=(
            pl.BlockSpec((3, rows, 2 * 64), lambda pair: (0, 0, pair)),
            pl.BlockSpec((pairs, 2, onehot.shape[1]), lambda pair: (0, 0, 0)),
        ),
        scratch_shapes=[
            pltpu.VMEM((2 * length, length), jnp.float32),
            pltpu.VMEM((2 * length, length), jnp.bfloat16),
            pltpu.VMEM((2 * length, length), jnp.bfloat16),
            pltpu.VMEM((pairs, 2, 4 * count), jnp.float32),
        ],
        compiler_params=pltpu.CompilerParams(vmem_limit_bytes=22 * 2**20),
        cost_estimate=pl.CostEstimate(
            flops=2 * 2 * pairs * (docs * length * length + query_rows * count) * 128 * 4,
            bytes_accessed=rows * width * 14 + 8 * pairs * docs * length * length,
            transcendentals=0,
        ),
        name="attend_back",
    )(*in_hbm(projected, projected, projected, grad_mixed, doc_probs, query_probs), onehot)


def dot_tn(left, right):
    return lax.dot_general(
        left, right, (((0,), (0,)), ((), ())), preferred_element_type=jnp.float32
    )


tile = 512
row_parts = 2
curve = 0.044715
slope = 0.7978845608028654


def turned_rows(place_ref, values, turned):
    quarter = values.shape[1] // 4
    flipped = values[...].T
    for outer in range(2):
        for core in range(2):
            kept = core ^ 1 ^ place_ref[1]
            start = pl.multiple_of((2 * kept + outer) * quarter, 16)
            block = flipped[(2 * outer + core) * quarter : (2 * outer + core + 1) * quarter, :]
            turned[pl.ds(start, quarter), :] = block


def split_store(values, kept_ref, sent_ref):
    quarter = values.shape[0] // 4
    low = values.astype(jnp.bfloat16)
    for outer in range(2):
        sent_ref[outer] = low[outer * quarter : (outer + 1) * quarter, :]
        kept_ref[outer] = low[(2 + outer) * quarter : (3 + outer) * quarter, :]


def gate_kernel(place_ref, n2_ref, weight, cot_ref, act_ref, by_gate_ref, by_up_ref, kept_ref, sent_ref):
    rows, width = n2_ref.shape
    hidden = weight.shape[-1] // 2
    start = pl.multiple_of(pl.program_id(0) * tile, 128)
    gate_weight = weight[..., pl.ds(start, tile)].reshape(width, tile)
    up_weight = weight[..., pl.ds(hidden + start, tile)].reshape(width, tile)

    def finish(places, gate, up):
        square = gate * gate
        bent = slope + (slope * curve) * square
        halved = 0.5 + 0.5 * jnp.tanh(gate * bent)
        value = gate * halved
        steep = halved + gate * (6.0 * bent - 4.0 * slope) * (halved - halved * halved)
        act_ref[places, :] = (value * up).astype(jnp.bfloat16)
        by_gate_ref[places, :] = up * steep
        by_up_ref[places, :] = value

    held = None
    for start in range(0, rows, 128):
        places = slice(start, start + 128)
        gate = dot_nn(n2_ref[places, :], gate_weight)
        up = dot_nn(n2_ref[places, :], up_weight)
        if held is not None:
            finish(*held)
        held = (places, gate, up)
    finish(*held)
    grad = dot_tn(act_ref[...], cot_ref[...]).astype(jnp.bfloat16)
    core = pl.program_id(0) % 2

    @pl.when(core == place_ref[1])
    def _():
        kept_ref[0] = grad

    @pl.when(core != place_ref[1])
    def _():
        sent_ref[0] = grad


def gate_forward(place, pieces, normed_two, cot_low):
    rows, width = normed_two.shape
    columns = pieces[0].shape[-1]
    hidden = columns // 2
    number = len(pieces)
    whole = pl.BlockSpec((rows, width), lambda step: (0, 0))
    column = pl.BlockSpec((rows, tile), lambda step: (0, step))
    half = pl.BlockSpec((1, tile, width), lambda step: (step // 2, 0, 0))
    assert hidden == 4 * tile

    def kernel(place_ref, *refs):
        n2_ref, cot_ref, *outs, full_ref, held, sems = refs[number:]
        filled(
            place_ref, refs[:number], full_ref, held, sems,
            lambda: gate_kernel(place_ref, n2_ref, held, cot_ref, *outs),
        )

    *results, full = pl.pallas_call(
        kernel,
        grid=(hidden // tile,),
        out_shape=(
            pltpu.HBM((rows, hidden), jnp.bfloat16),
            pltpu.HBM((rows, hidden), jnp.float32),
            pltpu.HBM((rows, hidden), jnp.float32),
            pltpu.HBM((2, tile, width), jnp.bfloat16),
            pltpu.HBM((2, tile, width), jnp.bfloat16),
            pltpu.HBM(slab(columns, width), jnp.bfloat16),
        ),
        in_specs=[scalars()] + [anywhere] * number + [whole, whole],
        out_specs=(column, column, column, half, half, anywhere),
        scratch_shapes=[
            pltpu.VMEM(slab(columns, width), jnp.bfloat16),
            pltpu.SemaphoreType.DMA((9,)),
        ],
        compiler_params=pltpu.CompilerParams(vmem_limit_bytes=34 * 2**20),
        cost_estimate=pl.CostEstimate(
            flops=6 * rows * width * hidden,
            bytes_accessed=rows * hidden * 10 + 8 * width * hidden,
            transcendentals=rows * hidden,
        ),
        name="gate_forward",
    )(place, *pieces, normed_two, *in_hbm(cot_low))
    return (*results, full.reshape(width, columns))


def gate_back_kernel(
    place_ref, n2_ref, cot_ref, ff, by_gate_ref, by_up_ref, out_ref, kept_ref, sent_ref, turned
):
    step = pl.program_id(0)

    @pl.when(step == 0)
    def _():
        turned_rows(place_ref, n2_ref, turned)

    weight = ff[step // 2, step % 2].reshape(tile, ff.shape[-1])
    incoming = dot_nt(cot_ref[...], weight)
    by_gate = (incoming * by_gate_ref[...]).astype(jnp.bfloat16)
    by_up = (incoming * by_up_ref[...]).astype(jnp.bfloat16)
    out_ref[0] = by_gate
    out_ref[1] = by_up
    split_store(dot_nn(turned[...], by_gate), kept_ref.at[:, :, :tile], sent_ref.at[:, :, :tile])
    split_store(dot_nn(turned[...], by_up), kept_ref.at[:, :, tile:], sent_ref.at[:, :, tile:])


def gate_back(place, pieces, normed_two, cot_low, by_gate, by_up):
    rows, width = normed_two.shape
    hidden = by_gate.shape[1]
    number = len(pieces)
    whole = pl.BlockSpec((rows, width), lambda step: (0, 0))
    column = pl.BlockSpec((rows, tile), lambda step: (0, step))
    half = pl.BlockSpec((2, width // 4, 2 * tile), lambda step: (0, 0, step))

    def kernel(place_ref, *refs):
        n2_ref, cot_ref, gate_ref, up_ref, *outs, full_ref, held, turned, sems = refs[number:]
        filled(
            place_ref, refs[:number], full_ref, held, sems,
            lambda: gate_back_kernel(
                place_ref, n2_ref, cot_ref, held, gate_ref, up_ref, *outs, turned
            ),
        )

    *results, full = pl.pallas_call(
        kernel,
        grid=(hidden // tile,),
        out_shape=(
            pltpu.HBM((2, rows, hidden), jnp.bfloat16),
            pltpu.HBM((2, width // 4, 2 * hidden), jnp.bfloat16),
            pltpu.HBM((2, width // 4, 2 * hidden), jnp.bfloat16),
            pltpu.HBM(slab(width, hidden), jnp.bfloat16),
        ),
        in_specs=[scalars()] + [anywhere] * number + [whole, whole, column, column],
        out_specs=(
            pl.BlockSpec((2, rows, tile), lambda step: (0, 0, step)),
            half,
            half,
            anywhere,
        ),
        scratch_shapes=[
            pltpu.VMEM(slab(width, hidden), jnp.bfloat16),
            pltpu.VMEM((width, rows), jnp.bfloat16),
            pltpu.SemaphoreType.DMA((9,)),
        ],
        compiler_params=pltpu.CompilerParams(vmem_limit_bytes=38 * 2**20),
        cost_estimate=pl.CostEstimate(
            flops=6 * rows * width * hidden,
            bytes_accessed=rows * hidden * 12 + 8 * width * hidden,
            transcendentals=0,
        ),
        name="gate_back",
    )(place, *pieces, *in_hbm(normed_two, cot_low, by_gate, by_up))
    return (*results, full.reshape(hidden, width))


def norm_back(grads, values, gain, residual):
    spread = lax.rsqrt(jnp.mean(values * values, axis=-1, keepdims=True) + epsilon)
    scaled = grads * gain
    inner = jnp.mean(scaled * values, axis=-1, keepdims=True)
    gain_grad = jnp.sum(grads * (values * spread), axis=0, keepdims=True)
    return residual + spread * scaled - values * (spread * spread * spread * inner), gain_grad


def middle_back_kernel(
    gates_ref, weight_ref, middle_ref, cot_ref, gain_ref, out_weight_ref,
    grad_ref, low_ref, mixed_ref, gain_grad_ref,
):
    hidden = gates_ref.shape[2]
    total = dot_nt(gates_ref[0], weight_ref[:, :hidden])
    total = total + dot_nt(gates_ref[1], weight_ref[:, hidden:])
    grad, gain_grad = norm_back(total, middle_ref[...], gain_ref[...], cot_ref[...])
    grad_ref[...] = grad
    low_ref[...] = grad.astype(jnp.bfloat16)

    @pl.when(pl.program_id(0) == 0)
    def _():
        gain_grad_ref[...] = gain_grad

    @pl.when(pl.program_id(0) > 0)
    def _():
        gain_grad_ref[...] += gain_grad

    mixed_ref[...] = dot_nt(low_ref[...], out_weight_ref[...]).astype(jnp.bfloat16)


def middle_back(gates, full_in, middle, cotangent, gain, full_attention, *earlier):
    rows, width = middle.shape
    hidden = gates.shape[2]
    part = rows // row_parts
    block = pl.BlockSpec((part, width), lambda step: (step, 0))

    def kernel(*refs):
        middle_back_kernel(*refs[:6], *refs[6 + len(earlier) :])

    return pl.pallas_call(
        kernel,
        grid=(row_parts,),
        out_shape=(
            pltpu.HBM((rows, width), jnp.float32),
            pltpu.HBM((rows, width), jnp.bfloat16),
            pltpu.HBM((rows, width), jnp.bfloat16),
            pltpu.HBM((1, width), jnp.float32),
        ),
        in_specs=[
            pl.BlockSpec((2, part, hidden), lambda step: (0, step, 0)),
            pl.BlockSpec((width, 2 * hidden), lambda step: (0, 0)),
            block,
            block,
            pl.BlockSpec((1, width), lambda step: (0, 0)),
            pl.BlockSpec((width, width), lambda step: (0, 3)),
        ]
        + [anywhere] * len(earlier),
        out_specs=(block, block, block, pl.BlockSpec((1, width), lambda step: (0, 0))),
        compiler_params=pltpu.CompilerParams(vmem_limit_bytes=46 * 2**20),
        cost_estimate=pl.CostEstimate(
            flops=4 * rows * width * hidden + 2 * rows * width * width,
            bytes_accessed=rows * hidden * 4 + 4 * width * hidden + 18 * rows * width,
            transcendentals=0,
        ),
        name="middle_back",
    )(
        *in_hbm(gates, full_in, middle, cotangent),
        gain.reshape(1, -1),
        *in_hbm(full_attention),
    )


def scalars():
    return pl.BlockSpec(memory_space=pltpu.SMEM)


def project(place, pieces, normed):
    rows, width = normed.shape
    columns = pieces[0].shape[-1]
    number = len(pieces)

    def kernel(place_ref, *refs):
        normed_ref, out_ref, full_ref, held, sems = refs[number:]

        def body():
            start = pl.multiple_of(pl.program_id(0) * width, 128)
            weight = held[..., pl.ds(start, width)].reshape(width, width)
            out_ref[...] = dot_nn(normed_ref[...], weight).astype(jnp.bfloat16)

        filled(place_ref, refs[:number], full_ref, held, sems, body)

    projected, full = pl.pallas_call(
        kernel,
        grid=(3,),
        out_shape=(
            pltpu.HBM((rows, 3 * width), jnp.bfloat16),
            pltpu.HBM(slab(columns, width), jnp.bfloat16),
        ),
        in_specs=[scalars()]
        + [anywhere] * number
        + [pl.BlockSpec((rows, width), lambda step: (0, 0))],
        out_specs=(pl.BlockSpec((rows, width), lambda step: (0, step)), anywhere),
        scratch_shapes=[
            pltpu.VMEM(slab(columns, width), jnp.bfloat16),
            pltpu.SemaphoreType.DMA((9,)),
        ],
        compiler_params=pltpu.CompilerParams(vmem_limit_bytes=14 * 2**20),
        cost_estimate=pl.CostEstimate(
            flops=6 * rows * width * width,
            bytes_accessed=8 * rows * width + 4 * columns * width,
            transcendentals=0,
        ),
        name="project",
    )(place, *pieces, normed)
    return projected, full.reshape(width, columns)


def middle_kernel(rows_ref, mixed_ref, weight_ref, gain_ref, middle_ref, normed_ref):
    middle = rows_ref[...] + dot_nn(mixed_ref[...], weight_ref[...])
    spread = lax.rsqrt(jnp.mean(middle * middle, axis=-1, keepdims=True) + epsilon)
    middle_ref[...] = middle
    normed_ref[...] = (middle * spread * gain_ref[...]).astype(jnp.bfloat16)


def middle_forward(values, mixed, full_attention, gain, *earlier):
    rows, width = values.shape
    part = rows // 2
    block = pl.BlockSpec((part, width), lambda step: (step, 0))

    def kernel(*refs):
        middle_kernel(*refs[:4], *refs[4 + len(earlier) :])

    return pl.pallas_call(
        kernel,
        grid=(2,),
        out_shape=(
            pltpu.HBM((rows, width), jnp.float32),
            jax.ShapeDtypeStruct((rows, width), jnp.bfloat16),
        ),
        in_specs=[
            block,
            block,
            pl.BlockSpec((width, width), lambda step: (0, 3)),
            pl.BlockSpec((1, width), lambda step: (0, 0)),
        ]
        + [anywhere] * len(earlier),
        out_specs=(block, block),
        compiler_params=pltpu.CompilerParams(vmem_limit_bytes=15 * 2**20),
        cost_estimate=pl.CostEstimate(
            flops=2 * rows * width * width,
            bytes_accessed=12 * rows * width + 2 * width * width,
            transcendentals=0,
        ),
        name="middle_forward",
    )(*in_hbm(values, mixed, full_attention), gain.reshape(1, -1), *earlier)


def attention_grads_kernel(
    place_ref, normed_ref, grads_ref, mixed_hbm, low_hbm, weight_ref, gain_ref,
    kept_ref, sent_ref, gain_grad_ref, turned, held, column, mixed_ref, low_ref, sems,
):
    step = pl.program_id(0)
    last = pl.num_programs(0) - 1
    quarter = held.shape[0] // 4
    copies = [
        pltpu.make_async_copy(mixed_hbm, mixed_ref, sems.at[0]),
        pltpu.make_async_copy(low_hbm, low_ref, sems.at[1]),
    ]

    @pl.when(step == 0)
    def _():
        for copy in copies:
            copy.start()
        turned_rows(place_ref, normed_ref, turned)
        column[...] = jnp.zeros_like(column)

    @pl.when(step < last)
    def _():
        held[...] = dot_nn(turned[...], grads_ref[0])
        split_store(held[...], kept_ref, sent_ref)
        for outer in range(2):
            for core in range(2):
                kept = core ^ 1 ^ place_ref[1]
                start = pl.multiple_of((2 * kept + outer) * quarter, 16)
                rows = slice((2 * outer + core) * quarter, (2 * outer + core + 1) * quarter)
                product = held[pl.ds(start, quarter), :] * weight_ref[rows, :].astype(jnp.float32)
                parts = [product[:, lane : lane + 128] for lane in range(0, held.shape[1], 128)]
                column[rows, :] += sum(parts)

    @pl.when(step == last)
    def _():
        for copy in copies:
            copy.wait()
        turned_rows(place_ref, mixed_ref, turned)
        split_store(dot_nn(turned[...], low_ref[...]), kept_ref, sent_ref)
        gain_grad_ref[...] = jnp.sum(column[...].T, axis=0, keepdims=True) / gain_ref[...]


def attention_grads(place, normed, grad_projected, mixed, grad_low, full_attention, gain):
    rows, width = normed.shape
    whole = pl.BlockSpec((rows, width), lambda step: (0, 0))
    line = pl.BlockSpec((1, width), lambda step: (0, 0))
    half = pl.BlockSpec((2, width // 4, width), lambda step: (0, 0, step))
    shape = pltpu.HBM((2, width // 4, 4 * width), jnp.bfloat16)
    return pl.pallas_call(
        attention_grads_kernel,
        grid=(4,),
        out_shape=(shape, shape, pltpu.HBM((1, width), jnp.float32)),
        in_specs=[
            scalars(),
            whole,
            pl.BlockSpec((1, rows, width), lambda step: (jnp.minimum(step, 2), 0, 0)),
            anywhere,
            anywhere,
            pl.BlockSpec((width, width), lambda step: (0, jnp.minimum(step, 2))),
            line,
        ],
        out_specs=(half, half, line),
        scratch_shapes=[
            pltpu.VMEM((width, rows), jnp.bfloat16),
            pltpu.VMEM((width, width), jnp.float32),
            pltpu.VMEM((width, 128), jnp.float32),
            pltpu.VMEM((rows, width), jnp.bfloat16),
            pltpu.VMEM((rows, width), jnp.bfloat16),
            pltpu.SemaphoreType.DMA((2,)),
        ],
        compiler_params=pltpu.CompilerParams(vmem_limit_bytes=36 * 2**20),
        cost_estimate=pl.CostEstimate(
            flops=8 * rows * width * width,
            bytes_accessed=12 * rows * width + 14 * width * width,
            transcendentals=0,
        ),
        name="attention_grads",
    )(
        place,
        *in_hbm(normed, grad_projected, mixed, grad_low, full_attention),
        gain.reshape(1, -1),
    )


def input_back(grad_projected, full_qkv, values, residual, gain, doc_rows):
    rows, width = values.shape
    part = rows // row_parts
    block = pl.BlockSpec((part, width), lambda step: (step, 0))

    def kernel(
        grads_ref, weight_ref, rows_ref, residual_ref, gain_ref,
        doc_ref, query_ref, slots, sems,
    ):
        step = pl.program_id(0)
        total = dot_nt(grads_ref[0], weight_ref[:, :width])
        for third in (1, 2):
            columns = slice(third * width, (third + 1) * width)
            total = total + dot_nt(grads_ref[third], weight_ref[:, columns])
        slots[step], _ = norm_back(total, rows_ref[...], gain_ref[...], residual_ref[...])
        emit(slots, (doc_ref, query_ref), sems)

    return pl.pallas_call(
        kernel,
        grid=(row_parts,),
        out_shape=(
            jax.ShapeDtypeStruct((doc_rows, width), jnp.float32),
            jax.ShapeDtypeStruct((rows - doc_rows, width), jnp.float32),
        ),
        in_specs=[
            pl.BlockSpec((3, part, width), lambda step: (0, step, 0)),
            pl.BlockSpec((width, 3 * width), lambda step: (0, 0)),
            block,
            block,
            pl.BlockSpec((1, width), lambda step: (0, 0)),
        ],
        out_specs=(anywhere, anywhere),
        scratch_shapes=[
            pltpu.VMEM((row_parts, part, width), jnp.float32),
            pltpu.SemaphoreType.DMA((row_parts + 1,)),
        ],
        compiler_params=pltpu.CompilerParams(vmem_limit_bytes=30 * 2**20),
        cost_estimate=pl.CostEstimate(
            flops=6 * rows * width * width,
            bytes_accessed=18 * rows * width + 6 * width * width,
            transcendentals=0,
        ),
        name="input_back",
    )(*in_hbm(grad_projected, full_qkv, values, residual), gain.reshape(1, -1))


def layer_outputs(middle, activated, full_ff, doc_rows):
    rows, width = middle.shape
    hidden = activated.shape[1]
    part = rows // row_parts

    def kernel(middle_ref, act_ref, weight_ref, doc_ref, query_ref, slots, sems):
        slots[pl.program_id(0)] = middle_ref[...] + dot_nn(act_ref[...], weight_ref[...])
        emit(slots, (doc_ref, query_ref), sems)

    return pl.pallas_call(
        kernel,
        grid=(row_parts,),
        out_shape=(
            jax.ShapeDtypeStruct((doc_rows, width), jnp.float32),
            jax.ShapeDtypeStruct((rows - doc_rows, width), jnp.float32),
        ),
        in_specs=[
            pl.BlockSpec((part, width), lambda step: (step, 0)),
            pl.BlockSpec((part, hidden), lambda step: (step, 0)),
            pl.BlockSpec((hidden, width), lambda step: (0, 0)),
        ],
        out_specs=(anywhere, anywhere),
        scratch_shapes=[
            pltpu.VMEM((row_parts, part, width), jnp.float32),
            pltpu.SemaphoreType.DMA((row_parts + 1,)),
        ],
        compiler_params=pltpu.CompilerParams(vmem_limit_bytes=24 * 2**20),
        cost_estimate=pl.CostEstimate(
            flops=2 * rows * width * hidden,
            bytes_accessed=8 * rows * width + 2 * hidden * (rows + width),
            transcendentals=0,
        ),
        name="layer_outputs",
    )(*in_hbm(middle, activated, full_ff))


def body(
    doc_inputs,
    query_inputs,
    doc_mask,
    query_lengths,
    doc_cotangent,
    query_cotangent,
    qkv_weight,
    out_weight,
    in_weight,
    ff_weight,
    attn_gain,
    ffn_gain,
    bias_table,
):
    doc_count, doc_length, model_width = doc_inputs.shape
    group_count, group_length = (query_inputs.shape[0], query_inputs.shape[1])
    head_count = bias_table.shape[1]
    doc_rows = doc_count * doc_length
    low = jnp.bfloat16
    routed = hand_routed()
    place = own_place() if routed else (0, 0, 0, 0)
    place_vector = jnp.stack([jnp.asarray(index, jnp.int32) for index in place])

    attention_shard = jnp.concatenate([qkv_weight, out_weight], axis=1).astype(low)
    in_shard = in_weight.astype(low)
    ff_shard = ff_weight.astype(low)

    values = jnp.concatenate(
        [doc_inputs.reshape(doc_rows, model_width), query_inputs.reshape(-1, model_width)], axis=0
    )
    cotangent = jnp.concatenate(
        [doc_cotangent.reshape(doc_rows, model_width), query_cotangent.reshape(-1, model_width)],
        axis=0,
    )
    cot_low = cotangent.astype(low)
    spread = lax.rsqrt(jnp.mean(values * values, axis=-1, keepdims=True) + epsilon)
    normed = (values * spread * attn_gain).astype(low)
    places = jnp.arange(group_length, dtype=jnp.int32)
    query_mask = places[None, :] < query_lengths[:, None]
    onehot = lines_onehot(bias_table.shape[0])
    lines = jnp.einsum("pn,nh->hp", onehot, bias_table, precision=highest)
    lines = lines.reshape(head_count // 2, 2, 4 * count)
    doc_masking = jnp.where(doc_mask > 0, 0.0, -1e9).astype(jnp.float32)
    query_masking = jnp.where(query_mask, 0.0, -1e9).astype(jnp.float32)
    query_masking = query_masking.reshape(-1, 1, count)

    if routed:
        column_a = gather_column(attention_shard)
        column_a, normed, lines, doc_masking, query_masking, cotangent, cot_low, in_shard = together(
            column_a, normed, lines, doc_masking, query_masking, cotangent, cot_low, in_shard
        )
        near_a = gather_near(place, *gather_plane(place, attention_shard, column_a))
        column_i = gather_column(in_shard)
        far_a = gather_far(*near_a)
        column_i, far_a, ff_shard = together(column_i, far_a, ff_shard)
        pieces = gather_order(near_a, far_a, gather_core(*near_a), gather_core(*far_a))
        plane_i = gather_plane(place, in_shard, column_i)
    else:
        pieces = (split_rows(lax.all_gather(attention_shard, both, axis=0, tiled=True)),)
    projected, full_attention = project(place_vector, pieces, normed)
    if routed:
        plane_i, projected, ff_shard = together(plane_i, projected, ff_shard)
        near_i = gather_near(place, *plane_i)
        far_i = gather_far(*near_i)
        column_f = gather_column(ff_shard)
    mixed, doc_probs, query_probs = attend(
        projected, lines, doc_masking, query_masking, group_length
    )
    if routed:
        mixed, far_i, column_f = together(mixed, far_i, column_f)
        plane_f = gather_plane(place, ff_shard, column_f)
        pieces = gather_order(near_i, far_i, gather_core(*near_i), gather_core(*far_i))
    else:
        pieces = (split_rows(lax.all_gather(in_shard, both, axis=0, tiled=True)),)
    middle, normed_two = middle_forward(values, mixed, full_attention, ffn_gain)
    if routed:
        pieces, normed_two, plane_f = together(pieces, normed_two, plane_f)
        near_f = gather_near(place, *plane_f)
        far_f = gather_far(*near_f)
        core_f = gather_core(*near_f)
    activated, by_gate, by_up, kept, sent, full_in = gate_forward(
        place_vector, pieces, normed_two, cot_low
    )
    if routed:
        far_f, core_f, by_gate, kept, sent = together(far_f, core_f, by_gate, kept, sent)
        pieces = gather_order(near_f, far_f, core_f, gather_core(*far_f))
        ff_grads = NarrowScatter(kept, sent, place_vector)
        got_f = ff_grads.core()
        pieces, got_f = together(pieces, got_f)
        near_f = ff_grads.plane(got_f)
    else:
        pieces = (split_rows(lax.all_gather(ff_shard, both, axis=0, tiled=True)),)
        grad_ff = joined_halves(kept, sent)
    gates, kept, sent, full_ff = gate_back(
        place_vector, pieces, normed_two, cot_low, by_gate, by_up
    )
    if routed:
        gates, kept, sent, near_f = together(gates, kept, sent, near_f)
        in_grads = Scatter(kept, sent, place_vector)
        far_f = ff_grads.far(ff_grads.far_sums(got_f, near_f))
        got_i = in_grads.core()
    else:
        grad_in = joined_halves(kept, sent)
    grad_middle, grad_middle_low, grad_mixed, grad_ffn_gain = middle_back(
        gates, full_in, middle, cotangent, ffn_gain, full_attention
    )
    if routed:
        grad_mixed, far_f, got_i = together(grad_mixed, far_f, got_i)
        near_i = in_grads.plane(got_i)
        shares_f = ff_grads.column(ff_grads.column_sums(got_f, near_f, far_f))
    grad_projected, grad_table = attend_back(
        projected, grad_mixed, doc_probs, query_probs, onehot, doc_length
    )
    if routed:
        grad_projected, grad_table, shares_f, near_i = together(
            grad_projected, grad_table, shares_f, near_i
        )
        far_i = in_grads.far(got_i, near_i)
    kept, sent, grad_attn_gain = attention_grads(
        place_vector, normed, grad_projected, mixed, grad_middle_low, full_attention, attn_gain
    )
    small = (grad_attn_gain, grad_ffn_gain, grad_table)
    small = jnp.concatenate([part.reshape(-1) for part in small])
    if routed:
        kept, sent, far_i, small, grad_projected, shares_f, activated = together(
            kept, sent, far_i, small, grad_projected, shares_f, activated
        )
        attention = Scatter(kept, sent, place_vector)
        got_a = attention.core()
        small = add_flipped(small, {"dc": 1})
        sums_i = in_grads.column_sums(got_i, near_i, far_i)
        got_a, sums_i, small, grad_projected, shares_f, activated = together(
            got_a, sums_i, small, grad_projected, shares_f, activated
        )
        near_a = attention.plane(got_a)
        shares_i = in_grads.column(sums_i)
        small = add_flipped(small, {"dz": 1})
    grad_inputs = input_back(
        grad_projected, full_attention, values, grad_middle, attn_gain, doc_rows
    )
    if routed:
        near_a, grad_inputs, small, shares_f, shares_i, activated = together(
            near_a, grad_inputs, small, shares_f, shares_i, activated
        )
        far_a = attention.far(got_a, near_a)
        small = add_flipped(small, {"dz": 2})
        far_a, small, shares_f, shares_i, activated = together(
            far_a, small, shares_f, shares_i, activated
        )
        sums_a = attention.column_sums(got_a, near_a, far_a)
        sums_a, small, shares_f, shares_i, activated = together(
            sums_a, small, shares_f, shares_i, activated
        )
        shares_a = attention.column(sums_a)
        small = add_flipped(small, {"dx": 1}, {"dy": 1})
    outputs = layer_outputs(middle, activated, full_ff, doc_rows)
    if routed:
        ff_grad_shard = summed(*shares_f)
        in_grad_shard = summed(*shares_i)
        grad_qkv = summed(*[share[:, : 3 * model_width] for share in shares_a])
        grad_out = summed(*[share[:, 3 * model_width :] for share in shares_a])
    else:
        scatter = functools.partial(
            lax.psum_scatter, axis_name=both, scatter_dimension=0, tiled=True
        )
        ff_grad_shard = scatter(grad_ff)
        in_grad_shard = scatter(grad_in)
        grad_attention = scatter(joined_halves(kept, sent))
        grad_qkv = grad_attention[:, : 3 * model_width]
        grad_out = grad_attention[:, 3 * model_width :]
        small = lax.psum(small, both)
    in_grad_shard = in_grad_shard.reshape(in_weight.shape[0], -1, 2, tile)
    in_grad_shard = jnp.swapaxes(in_grad_shard, 1, 2).reshape(in_weight.shape)
    return (
        outputs[0].reshape(doc_inputs.shape),
        outputs[1].reshape(query_inputs.shape),
        grad_inputs[0].reshape(doc_inputs.shape),
        grad_inputs[1].reshape(query_inputs.shape),
        grad_qkv,
        grad_out,
        in_grad_shard,
        ff_grad_shard,
        small[:model_width],
        small[model_width : 2 * model_width],
        small[2 * model_width :].reshape(head_count, -1).T,
    )


def solution(mesh):
    placed = (
        P(("dp", "fsdp"), None, None),
        P(("dp", "fsdp"), None, None),
        P(("dp", "fsdp"), None),
        P(("dp", "fsdp")),
        P(("dp", "fsdp"), None, None),
        P(("dp", "fsdp"), None, None),
        P(("dp", "fsdp"), None),
        P(("dp", "fsdp"), None),
        P(("dp", "fsdp"), None),
        P(("dp", "fsdp"), None),
        P(),
        P(),
        P(),
    )
    return jax.shard_map(
        body,
        mesh=mesh,
        in_specs=placed,
        out_specs=(
            P(("dp", "fsdp"), None, None),
            P(("dp", "fsdp"), None, None),
            P(("dp", "fsdp"), None, None),
            P(("dp", "fsdp"), None, None),
            P(("dp", "fsdp"), None),
            P(("dp", "fsdp"), None),
            P(("dp", "fsdp"), None),
            P(("dp", "fsdp"), None),
            P(),
            P(),
            P(),
        ),
        check_vma=False,
    )
```

```python
import functools
import math

import jax
import jax.numpy as jnp
from jax import lax
from jax.experimental import pallas as pl
from jax.experimental.pallas import tpu as pltpu
from jax.sharding import PartitionSpec as P

both = ("dp", "fsdp")
epsilon = 1e-06
highest = lax.Precision.HIGHEST
anywhere = pl.BlockSpec(memory_space=pl.ANY)


def place_index(y, c, z, x):
    return ((y * 2 + c) * 4 + z) * 2 + x


def flip_pairs(dy=0, dc=0, dz=0, dx=0):
    pairs = []
    for y in range(2):
        for c in range(2):
            for z in range(4):
                for x in range(2):
                    pairs.append(
                        (place_index(y, c, z, x), place_index(y ^ dy, c ^ dc, z ^ dz, x ^ dx))
                    )
    return pairs


def swap(values, **flips):
    return lax.ppermute(values, both, flip_pairs(**flips))


def hand_routed():
    return (lax.axis_size("dp"), lax.axis_size("fsdp")) == (4, 8)


def own_place():
    outer = lax.axis_index("dp")
    inner = lax.axis_index("fsdp")
    return outer // 2, outer % 2, inner // 2, inner % 2


def after(values, *earlier):
    return lax.optimization_barrier((values, *earlier))[0]


def in_hbm(*values):
    return [pltpu.with_memory_space_constraint(value, pltpu.HBM) for value in values]


def together(*values):
    return lax.optimization_barrier(values)


def fill_copies(place_ref, pieces, target, sems, by_column):
    if len(pieces) == 1:
        return [pltpu.make_async_copy(pieces[0], target, sems.at[0])]
    y, c, z, x = place_ref[0], place_ref[1], place_ref[2], place_ref[3]
    copies = []
    even = z - z % 2
    for number, piece in enumerate(pieces):
        core = c ^ (number // 4)
        kind = number % 4
        if by_column:
            where = target.at[:, core, z ^ kind]
        elif kind < 2:
            where = target.at[y ^ kind, core, pl.ds(even, 2)]
        else:
            where = target.at[:, core, pl.ds(even ^ 2, 2), x ^ (kind - 2)]
        copies.append(pltpu.make_async_copy(piece, where, sems.at[number]))
    return copies


def filled(place_ref, pieces, full_ref, held, sems, body, meanwhile=None, by_column=False):
    step = pl.program_id(0)
    kept = pltpu.make_async_copy(held, full_ref, sems.at[8])

    @pl.when(step == 0)
    def _():
        copies = fill_copies(place_ref, pieces, held, sems, by_column)
        for copy in copies:
            copy.start()
        if meanwhile is not None:
            meanwhile()
        for copy in copies:
            copy.wait()
        kept.start()

    body()

    @pl.when(step == pl.num_programs(0) - 1)
    def _():
        kept.wait()


def emit(slots, targets, sems):
    step, rows = pl.program_id(0), slots.shape[1]
    copies = []
    for number in range(slots.shape[0]):
        start = 0
        for target in targets:
            low = max(number * rows, start)
            high = min((number + 1) * rows, start + target.shape[0])
            if low < high:
                source = slots.at[number, pl.ds(low - number * rows, high - low)]
                where = target.at[pl.ds(low - start, high - low)]
                copy = pltpu.make_async_copy(source, where, sems.at[len(copies)])
                copies.append((number, copy))
            start += target.shape[0]
    for number in range(slots.shape[0]):

        @pl.when(step == number)
        def _():
            for owner, copy in copies:
                if owner == number:
                    copy.start()

    @pl.when(step == slots.shape[0] - 1)
    def _():
        for _, copy in copies:
            copy.wait()


def gather_order(near, far, core_near, core_far):
    return (near[0], far[0], near[1], far[1], core_near[0], core_far[0], core_near[1], core_far[1])


def slab(columns, rows):
    return (2, 2, 4, 2, rows // 32, columns)


def split_rows(full):
    return full.reshape(slab(full.shape[1], full.shape[0]))


def in_order(own, other, index):
    odd = index % 2 == 1
    return jnp.where(odd, other, own), jnp.where(odd, own, other)


def gather_column(shard):
    two, three, one = [swap(shard, dz=flip) for flip in (2, 3, 1)]
    return one, two, three


def gather_plane(place, shard, column):
    first = jnp.stack(in_order(shard, column[0], place[2]))
    second = jnp.stack(in_order(column[1], column[2], place[2]))
    return first, second, swap(first, dx=1), swap(second, dy=1)


def gather_near(place, first, second, first_near, second_near):
    even, odd = in_order(first, first_near, place[3])
    first = jnp.stack([even[0], odd[0], even[1], odd[1]]).reshape(2, 2, *first.shape[1:])
    second = jnp.stack(in_order(second, second_near, place[0]))
    return first, second


def gather_far(first, second):
    return swap(first, dy=1), swap(second, dx=1)


def gather_others(own, second):
    return swap(own, dz=1), swap(second, dz=1)


def gather_core(*pieces):
    return tuple(swap(piece, dc=1) for piece in pieces)


def summed(*terms):
    total = terms[0].astype(jnp.float32)
    for term in terms[1:]:
        total = total + term.astype(jnp.float32)
    return total


def joined_halves(kept, sent):
    return jnp.stack([kept, sent], axis=1).reshape(-1, kept.shape[2]).astype(jnp.float32)


def route(name, place, sources, targets, body, scratch=()):
    def spec(array, lead, pick):
        block = (*lead, *array.shape[-2:])
        return pl.BlockSpec(block, lambda step, where: (*pick(where), 0, 0))

    return pl.pallas_call(
        body,
        grid_spec=pltpu.PrefetchScalarGridSpec(
            num_scalar_prefetch=1,
            grid=(1,),
            in_specs=[spec(*source) for source in sources],
            out_specs=[spec(*target) for target in targets],
            scratch_shapes=scratch,
        ),
        out_shape=[target[0] for target in targets],
        compiler_params=pltpu.CompilerParams(vmem_limit_bytes=20 * 2**20),
        cost_estimate=pl.CostEstimate(
            flops=0,
            bytes_accessed=8 * len(sources) * math.prod(sources[0][0].shape[-2:]),
            transcendentals=0,
        ),
        name=name,
    )(place, *[source[0] for source in sources])


def whole_block(target):
    lead = target.shape[:-2]
    return target, lead, lambda where: (0,) * len(lead)


def store_sum(out_ref, *refs):
    blocks = math.prod(refs[0].shape[:-2])
    for number in range(blocks):
        terms = []
        for ref in (out_ref, *refs):
            index, rest = [], number
            for size in reversed(ref.shape[:-2]):
                index.insert(0, rest % size)
                rest //= size
            terms.append(ref.at[tuple(index)])
        terms[0][...] = summed(*[term[...] for term in terms[1:]]).astype(out_ref.dtype)


class Scatter:
    def __init__(self, kept, sent, place):
        self.place = place
        self.block = (kept.shape[1] // 8, kept.shape[2])
        self.shape = (2, 4, 2, *self.block)
        self.kept = kept.reshape(self.shape)
        self.sent = sent

    def target(self, *lead, dtype=jnp.bfloat16):
        return jax.ShapeDtypeStruct((*lead, *self.block), dtype)

    def both(self, got, lead, pick):
        return [(*in_hbm(self.kept), lead, pick), (got, lead, pick)]

    def core(self):
        return swap(self.sent, dc=1).reshape(self.shape)

    def plane(self, got):
        def body(place_ref, *refs):
            store_sum(refs[4], *refs[0:2])
            store_sum(refs[5], *refs[2:4])

        sources = self.both(got, (2, 2, 1), lambda where: (0, 0, 1 - where[3]))
        sources += self.both(got, (1, 2, 2), lambda where: (1 - where[0], 1, 0))
        target = whole_block(self.target(2, 2))
        one, two = route("plane", self.place, sources, [target, target], body)
        return swap(one, dx=1), swap(two, dy=1)

    def far(self, got, near):
        def body(place_ref, *refs):
            store_sum(refs[6], *refs[0:3])
            store_sum(refs[7], *refs[3:6])

        sources = [
            *self.both(got, (1, 2, 1), lambda where: (1 - where[0], 0, where[3])),
            (near[0], (1, 2), lambda where: (1 - where[0], 0)),
            *self.both(got, (1, 2, 1), lambda where: (where[0], 1, 1 - where[3])),
            (near[1], (2, 1), lambda where: (0, 1 - where[3])),
        ]
        target = whole_block(self.target(2))
        one, two = route("far", self.place, sources, [target, target], body)
        return swap(one, dy=1), swap(two, dx=1)

    def column_sources(self, near, far):
        return [
            (near[0], (1, 2), lambda where: (where[0], 0)),
            (far[0], (2,), lambda where: (0,)),
            (near[1], (2, 1), lambda where: (0, where[3])),
            (far[1], (2,), lambda where: (0,)),
        ]

    def column_terms(self, row, refs):
        if row < 2:
            return refs[0].at[0, row], refs[1].at[row]
        return refs[2].at[row - 2, 0], refs[3].at[row - 2]

    def column_sums(self, got, near, far):
        sources = self.both(got, (1, 4, 1), lambda where: (where[0], 0, where[3]))
        sources += self.column_sources(near, far)
        number = len(sources)

        def body(place_ref, *refs):
            *outs, total = refs[number:]
            for row in range(4):
                terms = (refs[0].at[0, row, 0], refs[1].at[0, row, 0])
                terms += self.column_terms(row, refs[2:number])
                total[row] = summed(*[term[...] for term in terms])
            for flip, out in enumerate(outs):
                out[...] = total[place_ref[2] ^ flip].astype(out.dtype)

        targets = [self.target(dtype=jnp.float32)] + [self.target()] * 3
        targets = [whole_block(target) for target in targets]
        scratch = [pltpu.VMEM((4, *self.block), jnp.float32)]
        return tuple(route("column", self.place, sources, targets, body, scratch))

    def column(self, sums):
        return sums[0], *[swap(share, dz=flip) for flip, share in zip((1, 2, 3), sums[1:])]


class NarrowScatter(Scatter):
    def both(self, got, lead, pick, pinned=True):
        got = in_hbm(got)[0] if pinned else got
        return [(*in_hbm(self.kept), lead, pick), (got, lead, pick)]

    def plane(self, got):
        def body(place_ref, *refs):
            store_sum(refs[2], *refs[0:2])

        sources = self.both(got, (2, 4, 1), lambda where: (0, 0, 1 - where[3]), False)
        target = whole_block(self.target(2, 4))
        (sums,) = route("plane", self.place, sources, [target], body)
        return swap(sums, dx=1)

    def far_sums(self, got, near):
        def body(place_ref, *refs):
            store_sum(refs[3], *refs[0:3])

        sources = self.both(got, (1, 4, 1), lambda where: (1 - where[0], 0, where[3]))
        sources.append((near, (1, 4), lambda where: (1 - where[0], 0)))
        return route("far", self.place, sources, [whole_block(self.target(4))], body)[0]

    def far(self, sums):
        return swap(sums, dy=1)

    def column_sources(self, near, far):
        return [
            (near, (1, 4), lambda where: (where[0], 0)),
            (far, (4,), lambda where: (0,)),
        ]

    def column_terms(self, row, refs):
        return refs[0].at[0, row], refs[1].at[row]


def add_flipped(values, *steps):
    for flips in steps:
        values = values + swap(values, **flips)
    return values


count = 128


def relative_places():
    places = jnp.arange(4 * count, dtype=jnp.int32)
    return jnp.where(places < 3 * count, places - count, places - 5 * count)


def bucket_of(relative):
    distance = jnp.abs(relative)
    larger = jnp.zeros_like(distance)
    for threshold in (12, 16, 23, 32, 46, 64, 91):
        larger = larger + (distance >= threshold).astype(jnp.int32)
    bucket = jnp.where(distance < 8, distance, 8 + larger)
    return bucket + 16 * (relative > 0).astype(jnp.int32)


def lines_onehot(bucket_count):
    labels = jnp.arange(bucket_count, dtype=jnp.int32)
    return (bucket_of(relative_places())[:, None] == labels).astype(jnp.float32)


def own_lanes(head, shape):
    lanes = lax.broadcasted_iota(jnp.int32, shape, 1)
    return lanes < shape[1] // 2 if head == 0 else lanes >= shape[1] // 2


def keep_lanes(head, values):
    return jnp.where(own_lanes(head, values.shape), values, jnp.zeros_like(values))


def both_heads(values):
    return jnp.concatenate([keep_lanes(0, values), keep_lanes(1, values)], axis=0)


def joined(stacked):
    first, second = jnp.split(stacked, 2, axis=0)
    return jnp.where(own_lanes(0, first.shape), first, second).astype(jnp.bfloat16)


def softmax_rows(scores):
    raised = jnp.exp(scores - jnp.max(scores, axis=-1, keepdims=True))
    return raised * (1.0 / jnp.sum(raised, axis=-1, keepdims=True))


def dot_nt(left, right):
    return lax.dot_general(
        left, right, (((1,), (1,)), ((), ())), preferred_element_type=jnp.float32
    )


def dot_nn(left, right):
    return jnp.dot(left, right, preferred_element_type=jnp.float32)


def attend_kernel(
    docs, length, group, q_ref, k_ref, v_ref, line_ref, mask_ref, query_mask_ref,
    mixed_ref, doc_probs_ref, query_probs_ref, scores_scratch, probs_scratch,
):
    blocks = length // count
    query_start = docs * length
    query_blocks = (q_ref.shape[0] - query_start) // count
    row_group = lax.broadcasted_iota(jnp.int32, (count, count), 0) // group
    column_group = lax.broadcasted_iota(jnp.int32, (count, count), 1) // group
    bands, edges = [], []
    for head in range(2):
        line = line_ref[0, head : head + 1, :]
        band = pltpu.roll(
            jnp.broadcast_to(line, (count, 4 * count)), 0, 1, stride=1, stride_axis=0
        )
        bands.append(band)
        edges.append(
            (
                jnp.broadcast_to(line[:, 4 * count - 1 :], (1, count)),
                jnp.broadcast_to(line[:, 3 * count - 1 : 3 * count], (1, count)),
            )
        )
    for doc in range(docs):
        base = doc * length
        whole = slice(base, base + length)
        masking = mask_ref[doc : doc + 1, :]
        scores_scratch[...] = dot_nt(both_heads(q_ref[whole, :]), k_ref[whole, :])
        for head in range(2):
            for row in range(blocks):
                rows = slice(row * count, (row + 1) * count)
                stacked = slice(head * length + row * count, head * length + (row + 1) * count)
                shifted = []
                for column in range(blocks):
                    columns = slice(column * count, (column + 1) * count)
                    away = column - row
                    block = scores_scratch[stacked, columns]
                    if abs(away) > 1:
                        block = block + (edges[head][away > 0] + masking[:, columns])
                    else:
                        start = (away + 1) * count
                        block = block + bands[head][:, start : start + count]
                        block = block + masking[:, columns]
                    shifted.append(block)
                probs = softmax_rows(jnp.concatenate(shifted, axis=1))
                doc_probs_ref[head, base + row * count : base + (row + 1) * count, :] = probs
                probs_scratch[stacked, :] = probs.astype(jnp.bfloat16)
        mixed_ref[whole, :] = joined(dot_nn(probs_scratch[...], v_ref[whole, :]))
    for block in range(query_blocks):
        rows = slice(query_start + block * count, query_start + (block + 1) * count)
        masking = query_mask_ref[block]
        scores = dot_nt(both_heads(q_ref[rows, :]), k_ref[rows, :])
        low = []
        for head in range(2):
            bias = jnp.where(
                row_group == column_group, bands[head][:, count : 2 * count], -1e9
            )
            probs = softmax_rows(scores[head * count : (head + 1) * count, :] + bias + masking)
            query_probs_ref[head, block * count : (block + 1) * count, :] = probs
            low.append(probs.astype(jnp.bfloat16))
        mixed_ref[rows, :] = joined(dot_nn(jnp.concatenate(low, axis=0), v_ref[rows, :]))


def pair_spec(rows, offset):
    return pl.BlockSpec((rows, 2 * 64), lambda pair: (0, offset + pair))


def attend(projected, lines, doc_mask, query_mask, group):
    docs, length = doc_mask.shape
    rows, width = projected.shape[0], projected.shape[1] // 3
    pairs = lines.shape[0]
    query_rows = rows - docs * length
    return pl.pallas_call(
        functools.partial(attend_kernel, docs, length, group),
        grid=(pairs,),
        out_shape=(
            jax.ShapeDtypeStruct((rows, width), jnp.bfloat16),
            pltpu.HBM((2 * pairs, docs * length, length), jnp.float32),
            pltpu.HBM((2 * pairs, query_rows, count), jnp.float32),
        ),
        in_specs=[
            pair_spec(rows, 0),
            pair_spec(rows, pairs),
            pair_spec(rows, 2 * pairs),
            pl.BlockSpec((1, 2, 4 * count), lambda pair: (pair, 0, 0)),
            pl.BlockSpec((docs, length), lambda pair: (0, 0)),
            pl.BlockSpec(query_mask.shape, lambda pair: (0, 0, 0)),
        ],
        out_specs=(
            pair_spec(rows, 0),
            pl.BlockSpec((2, docs * length, length), lambda pair: (pair, 0, 0)),
            pl.BlockSpec((2, query_rows, count), lambda pair: (pair, 0, 0)),
        ),
        scratch_shapes=[
            pltpu.VMEM((2 * length, length), jnp.float32),
            pltpu.VMEM((2 * length, length), jnp.bfloat16),
        ],
        compiler_params=pltpu.CompilerParams(vmem_limit_bytes=18 * 2**20),
        cost_estimate=pl.CostEstimate(
            flops=2 * 2 * pairs * (docs * length * length + query_rows * count) * 128 * 2,
            bytes_accessed=rows * width * 8 + 8 * pairs * docs * length * length,
            transcendentals=2 * pairs * (docs * length * length + query_rows * count),
        ),
        name="attend",
    )(*in_hbm(projected, projected, projected), lines, doc_mask, query_mask)


def attend_back_kernel(
    docs, length, q_ref, k_ref, v_ref, grad_ref, doc_probs_ref, query_probs_ref, onehot_ref,
    out_ref, table_ref, grads_scratch, scores_scratch, probs_scratch, lines_scratch,
):
    blocks = length // count
    query_start = docs * length
    query_blocks = (q_ref.shape[0] - query_start) // count
    low = jnp.bfloat16
    half = q_ref.shape[1] // 2
    band = [[None] * 5, [None] * 5]

    def gather(head, place, block):
        held = band[head][place]
        band[head][place] = block if held is None else held + block

    def backward(probs, grad_probs):
        product = probs * grad_probs
        return product - probs * jnp.sum(product, axis=-1, keepdims=True)

    for doc in range(docs):
        base = doc * length
        whole = slice(base, base + length)
        grads_scratch[...] = dot_nt(both_heads(grad_ref[whole, :]), v_ref[whole, :])
        for head in range(2):
            for row in range(blocks):
                rows = slice(base + row * count, base + (row + 1) * count)
                stacked = slice(head * length + row * count, head * length + (row + 1) * count)
                probs = doc_probs_ref[head, rows, :]
                scores = backward(probs, grads_scratch[stacked, :])
                for column in range(blocks):
                    away = max(-2, min(2, column - row))
                    block = scores[:, column * count : (column + 1) * count]
                    if abs(away) == 2:
                        block = jnp.sum(block.reshape(count // 8, 8, count), axis=0)
                    gather(head, away + 2, block)
                scores_scratch[stacked, :] = scores.astype(low)
                probs_scratch[stacked, :] = probs.astype(low)
        out_ref[0, whole, :] = joined(dot_nn(scores_scratch[...], k_ref[whole, :]))
        q_turned = q_ref[whole, :].T
        grad_turned = grad_ref[whole, :].T
        grad_k, grad_v = [], []
        for head in range(2):
            own = slice(head * half, (head + 1) * half)
            stacked = slice(head * length, (head + 1) * length)
            grad_k.append(dot_nn(q_turned[own, :], scores_scratch[stacked, :]))
            grad_v.append(dot_nn(grad_turned[own, :], probs_scratch[stacked, :]))
        out_ref[1, whole, :] = jnp.concatenate(grad_k, axis=0).astype(low).T
        out_ref[2, whole, :] = jnp.concatenate(grad_v, axis=0).astype(low).T
    for block in range(query_blocks):
        rows = slice(query_start + block * count, query_start + (block + 1) * count)
        grad_probs = dot_nt(both_heads(grad_ref[rows, :]), v_ref[rows, :])
        low_scores, low_probs = [], []
        for head in range(2):
            probs = query_probs_ref[head, block * count : (block + 1) * count, :]
            scores = backward(probs, grad_probs[head * count : (head + 1) * count, :])
            gather(head, 2, scores)
            low_scores.append(scores.astype(low))
            low_probs.append(probs.astype(low))
        out_ref[0, rows, :] = joined(dot_nn(jnp.concatenate(low_scores, axis=0), k_ref[rows, :]))
        turned = jnp.concatenate(low_scores, axis=1).T
        turned = jnp.concatenate([turned, jnp.concatenate(low_probs, axis=1).T], axis=1)
        empty = jnp.zeros((count, 2 * half), low)
        weights = jnp.concatenate(
            [
                jnp.concatenate([q_ref[rows, :], empty], axis=1),
                jnp.concatenate([empty, grad_ref[rows, :]], axis=1),
            ],
            axis=0,
        )
        both_grads = dot_nn(turned, weights)
        out_ref[1, rows, :] = joined(both_grads[:, : 2 * half])
        out_ref[2, rows, :] = joined(both_grads[:, 2 * half :])
    lines = []
    for head in range(2):
        below, before, middle, after, above = band[head]
        wide = jnp.concatenate([before, middle, after, jnp.zeros_like(middle)], axis=1)
        eights = [wide[:8]]
        for start in range(8, count, 8):
            eights.append(pltpu.roll(wide[start : start + 8], 4 * count - start, 1))
        wide = sum(eights)
        wide = jnp.concatenate([wide[7 - row : 8 - row] for row in range(8)], axis=0)
        wide = pltpu.roll(wide, 4 * count - 7, 1, stride=1, stride_axis=0)
        wide = jnp.sum(wide, axis=0, keepdims=True)
        far = jnp.concatenate(
            [
                jnp.zeros((1, 2 * count), jnp.float32),
                jnp.sum(above, axis=0, keepdims=True),
                jnp.sum(below, axis=0, keepdims=True),
            ],
            axis=1,
        )
        lines.append(wide + far)
    pair = pl.program_id(0)
    lines_scratch[pair] = jnp.concatenate(lines, axis=0)

    @pl.when(pair == pl.num_programs(0) - 1)
    def _():
        table_ref[...] = jnp.dot(
            lines_scratch[...].reshape(-1, 4 * count),
            onehot_ref[...],
            precision=highest,
            preferred_element_type=jnp.float32,
        ).reshape(table_ref.shape)


def attend_back(projected, grad_mixed, doc_probs, query_probs, onehot, length):
    rows, width = grad_mixed.shape
    pairs = doc_probs.shape[0] // 2
    docs = doc_probs.shape[1] // length
    query_rows = query_probs.shape[1]

    return pl.pallas_call(
        functools.partial(attend_back_kernel, docs, length),
        grid=(pairs,),
        out_shape=(
            pltpu.HBM((3, rows, width), jnp.bfloat16),
            pltpu.HBM((pairs, 2, onehot.shape[1]), jnp.float32),
        ),
        in_specs=[
            pair_spec(rows, 0),
            pair_spec(rows, pairs),
            pair_spec(rows, 2 * pairs),
            pair_spec(rows, 0),
            pl.BlockSpec((2, docs * length, length), lambda pair: (pair, 0, 0)),
            pl.BlockSpec((2, query_rows, count), lambda pair: (pair, 0, 0)),
            pl.BlockSpec(onehot.shape, lambda pair: (0, 0)),
        ],
        out_specs=(
            pl.BlockSpec((3, rows, 2 * 64), lambda pair: (0, 0, pair)),
            pl.BlockSpec((pairs, 2, onehot.shape[1]), lambda pair: (0, 0, 0)),
        ),
        scratch_shapes=[
            pltpu.VMEM((2 * length, length), jnp.float32),
            pltpu.VMEM((2 * length, length), jnp.bfloat16),
            pltpu.VMEM((2 * length, length), jnp.bfloat16),
            pltpu.VMEM((pairs, 2, 4 * count), jnp.float32),
        ],
        compiler_params=pltpu.CompilerParams(vmem_limit_bytes=22 * 2**20),
        cost_estimate=pl.CostEstimate(
            flops=2 * 2 * pairs * (docs * length * length + query_rows * count) * 128 * 4,
            bytes_accessed=rows * width * 14 + 8 * pairs * docs * length * length,
            transcendentals=0,
        ),
        name="attend_back",
    )(*in_hbm(projected, projected, projected, grad_mixed, doc_probs, query_probs), onehot)


def dot_tn(left, right):
    return lax.dot_general(
        left, right, (((0,), (0,)), ((), ())), preferred_element_type=jnp.float32
    )


tile = 512
row_parts = 2
curve = 0.044715
slope = 0.7978845608028654


def turned_rows(place_ref, values, turned):
    quarter = values.shape[1] // 4
    flipped = values[...].T
    for outer in range(2):
        for core in range(2):
            kept = core ^ 1 ^ place_ref[1]
            start = pl.multiple_of((2 * kept + outer) * quarter, 16)
            block = flipped[(2 * outer + core) * quarter : (2 * outer + core + 1) * quarter, :]
            turned[pl.ds(start, quarter), :] = block


def split_store(values, kept_ref, sent_ref):
    quarter = values.shape[0] // 4
    low = values.astype(jnp.bfloat16)
    for outer in range(2):
        sent_ref[outer] = low[outer * quarter : (outer + 1) * quarter, :]
        kept_ref[outer] = low[(2 + outer) * quarter : (3 + outer) * quarter, :]


def gate_kernel(place_ref, n2_ref, weight, cot_ref, act_ref, by_gate_ref, by_up_ref, kept_ref, sent_ref):
    rows, width = n2_ref.shape
    hidden = weight.shape[-1] // 2
    start = pl.multiple_of(pl.program_id(0) * tile, 128)
    gate_weight = weight[..., pl.ds(start, tile)].reshape(width, tile)
    up_weight = weight[..., pl.ds(hidden + start, tile)].reshape(width, tile)

    def finish(places, gate, up):
        square = gate * gate
        bent = slope + (slope * curve) * square
        halved = 0.5 + 0.5 * jnp.tanh(gate * bent)
        value = gate * halved
        steep = halved + gate * (6.0 * bent - 4.0 * slope) * (halved - halved * halved)
        act_ref[places, :] = (value * up).astype(jnp.bfloat16)
        by_gate_ref[places, :] = up * steep
        by_up_ref[places, :] = value

    held = None
    for start in range(0, rows, 128):
        places = slice(start, start + 128)
        gate = dot_nn(n2_ref[places, :], gate_weight)
        up = dot_nn(n2_ref[places, :], up_weight)
        if held is not None:
            finish(*held)
        held = (places, gate, up)
    finish(*held)
    grad = dot_tn(act_ref[...], cot_ref[...]).astype(jnp.bfloat16)
    core = pl.program_id(0) % 2

    @pl.when(core == place_ref[1])
    def _():
        kept_ref[0] = grad

    @pl.when(core != place_ref[1])
    def _():
        sent_ref[0] = grad


def gate_forward(place, pieces, normed_two, cot_low):
    rows, width = normed_two.shape
    columns = pieces[0].shape[-1]
    hidden = columns // 2
    number = len(pieces)
    whole = pl.BlockSpec((rows, width), lambda step: (0, 0))
    column = pl.BlockSpec((rows, tile), lambda step: (0, step))
    half = pl.BlockSpec((1, tile, width), lambda step: (step // 2, 0, 0))
    assert hidden == 4 * tile

    def kernel(place_ref, *refs):
        n2_ref, cot_ref, *outs, full_ref, held, sems = refs[number:]
        filled(
            place_ref, refs[:number], full_ref, held, sems,
            lambda: gate_kernel(place_ref, n2_ref, held, cot_ref, *outs),
        )

    *results, full = pl.pallas_call(
        kernel,
        grid=(hidden // tile,),
        out_shape=(
            pltpu.HBM((rows, hidden), jnp.bfloat16),
            pltpu.HBM((rows, hidden), jnp.float32),
            pltpu.HBM((rows, hidden), jnp.float32),
            pltpu.HBM((2, tile, width), jnp.bfloat16),
            pltpu.HBM((2, tile, width), jnp.bfloat16),
            pltpu.HBM(slab(columns, width), jnp.bfloat16),
        ),
        in_specs=[scalars()] + [anywhere] * number + [whole, whole],
        out_specs=(column, column, column, half, half, anywhere),
        scratch_shapes=[
            pltpu.VMEM(slab(columns, width), jnp.bfloat16),
            pltpu.SemaphoreType.DMA((9,)),
        ],
        compiler_params=pltpu.CompilerParams(vmem_limit_bytes=34 * 2**20),
        cost_estimate=pl.CostEstimate(
            flops=6 * rows * width * hidden,
            bytes_accessed=rows * hidden * 10 + 8 * width * hidden,
            transcendentals=rows * hidden,
        ),
        name="gate_forward",
    )(place, *pieces, normed_two, *in_hbm(cot_low))
    return (*results, full.reshape(width, columns))


def gate_back_kernel(
    place_ref, n2_ref, cot_ref, ff, by_gate_ref, by_up_ref, out_ref, kept_ref, sent_ref, turned
):
    step = pl.program_id(0)
    weight = ff[step // 2, step % 2].reshape(tile, ff.shape[-1])
    incoming = dot_nt(cot_ref[...], weight)
    by_gate = (incoming * by_gate_ref[...]).astype(jnp.bfloat16)
    by_up = (incoming * by_up_ref[...]).astype(jnp.bfloat16)
    out_ref[0] = by_gate
    out_ref[1] = by_up
    split_store(dot_nn(turned[...], by_gate), kept_ref.at[:, :, :tile], sent_ref.at[:, :, :tile])
    split_store(dot_nn(turned[...], by_up), kept_ref.at[:, :, tile:], sent_ref.at[:, :, tile:])


def gate_back(place, pieces, normed_two, cot_low, by_gate, by_up):
    rows, width = normed_two.shape
    hidden = by_gate.shape[1]
    number = len(pieces)
    whole = pl.BlockSpec((rows, width), lambda step: (0, 0))
    column = pl.BlockSpec((rows, tile), lambda step: (0, step))
    half = pl.BlockSpec((2, width // 4, 2 * tile), lambda step: (0, 0, step))

    def kernel(place_ref, *refs):
        n2_ref, cot_ref, gate_ref, up_ref, *outs, full_ref, held, turned, sems = refs[number:]
        filled(
            place_ref, refs[:number], full_ref, held, sems,
            lambda: gate_back_kernel(
                place_ref, n2_ref, cot_ref, held, gate_ref, up_ref, *outs, turned
            ),
            lambda: turned_rows(place_ref, n2_ref, turned), True,
        )

    *results, full = pl.pallas_call(
        kernel,
        grid=(hidden // tile,),
        out_shape=(
            pltpu.HBM((2, rows, hidden), jnp.bfloat16),
            pltpu.HBM((2, width // 4, 2 * hidden), jnp.bfloat16),
            pltpu.HBM((2, width // 4, 2 * hidden), jnp.bfloat16),
            pltpu.HBM(slab(width, hidden), jnp.bfloat16),
        ),
        in_specs=[scalars()] + [anywhere] * number + [whole, whole, column, column],
        out_specs=(
            pl.BlockSpec((2, rows, tile), lambda step: (0, 0, step)),
            half,
            half,
            anywhere,
        ),
        scratch_shapes=[
            pltpu.VMEM(slab(width, hidden), jnp.bfloat16),
            pltpu.VMEM((width, rows), jnp.bfloat16),
            pltpu.SemaphoreType.DMA((9,)),
        ],
        compiler_params=pltpu.CompilerParams(vmem_limit_bytes=38 * 2**20),
        cost_estimate=pl.CostEstimate(
            flops=6 * rows * width * hidden,
            bytes_accessed=rows * hidden * 12 + 8 * width * hidden,
            transcendentals=0,
        ),
        name="gate_back",
    )(place, *pieces, *in_hbm(normed_two, cot_low, by_gate, by_up))
    return (*results, full.reshape(hidden, width))


def norm_back(grads, values, gain, residual):
    spread = lax.rsqrt(jnp.mean(values * values, axis=-1, keepdims=True) + epsilon)
    scaled = grads * gain
    inner = jnp.mean(scaled * values, axis=-1, keepdims=True)
    gain_grad = jnp.sum(grads * (values * spread), axis=0, keepdims=True)
    return residual + spread * scaled - values * (spread * spread * spread * inner), gain_grad


def middle_back_kernel(
    gates_hbm, weight_hbm, out_weight_hbm, middle_hbm, cot_hbm, gain_ref,
    grad_hbm, low_hbm, mixed_hbm, gain_grad_ref,
    gates, weight, out_weight, middle, cot, total, low, mixed, sems,
):
    rows, width = total.shape
    hidden = gates.shape[2]
    wide = hidden // 2
    arrivals = []

    def bring(source, target):
        copy = pltpu.make_async_copy(source, target, sems.at[len(arrivals)])
        copy.start()
        arrivals.append(copy)

    for part in range(4):
        columns = pl.ds(part % 2 * wide, wide)
        bring(gates_hbm.at[part // 2, :, columns], gates.at[part // 2, :, columns])
        columns = pl.ds(part * wide, wide)
        bring(weight_hbm.at[:, columns], weight.at[:, columns])
    bring(middle_hbm, middle)
    bring(cot_hbm, cot)
    bring(out_weight_hbm.at[:, pl.ds(3 * width, width)], out_weight)
    for part in range(4):
        arrivals[2 * part].wait()
        arrivals[2 * part + 1].wait()
        columns = slice(part % 2 * wide, part % 2 * wide + wide)
        product = dot_nt(
            gates[part // 2, :, columns], weight[:, part * wide : part * wide + wide]
        )
        if part == 0:
            total[...] = product
        else:
            total[...] += product
    for copy in arrivals[8:]:
        copy.wait()
    leaving = []
    for half in range(2):
        places = slice(half * rows // 2, (half + 1) * rows // 2)
        grad, gain_grad = norm_back(
            total[places, :], middle[places, :], gain_ref[...], cot[places, :]
        )
        total[places, :] = grad
        low[places, :] = grad.astype(jnp.bfloat16)
        if half == 0:
            gain_grad_ref[...] = gain_grad
        else:
            gain_grad_ref[...] += gain_grad
        mixed[places, :] = dot_nt(low[places, :], out_weight[...]).astype(jnp.bfloat16)
        places = pl.ds(half * rows // 2, rows // 2)
        for source, target in ((total, grad_hbm), (low, low_hbm), (mixed, mixed_hbm)):
            copy = pltpu.make_async_copy(
                source.at[places], target.at[places], sems.at[len(arrivals) + len(leaving)]
            )
            copy.start()
            leaving.append(copy)
    for copy in leaving:
        copy.wait()


def middle_back(gates, full_in, middle, cotangent, gain, full_attention):
    rows, width = middle.shape
    hidden = gates.shape[2]
    low = jnp.bfloat16
    line = pl.BlockSpec(memory_space=pltpu.VMEM)
    return pl.pallas_call(
        middle_back_kernel,
        out_shape=(
            pltpu.HBM((rows, width), jnp.float32),
            pltpu.HBM((rows, width), low),
            pltpu.HBM((rows, width), low),
            jax.ShapeDtypeStruct((1, width), jnp.float32),
        ),
        in_specs=[anywhere] * 5 + [line],
        out_specs=(anywhere, anywhere, anywhere, line),
        scratch_shapes=[
            pltpu.VMEM((2, rows, hidden), low),
            pltpu.VMEM((width, 2 * hidden), low),
            pltpu.VMEM((width, width), low),
            pltpu.VMEM((rows, width), jnp.float32),
            pltpu.VMEM((rows, width), jnp.float32),
            pltpu.VMEM((rows, width), jnp.float32),
            pltpu.VMEM((rows, width), low),
            pltpu.VMEM((rows, width), low),
            pltpu.SemaphoreType.DMA((17,)),
        ],
        compiler_params=pltpu.CompilerParams(vmem_limit_bytes=46 * 2**20),
        cost_estimate=pl.CostEstimate(
            flops=4 * rows * width * hidden + 2 * rows * width * width,
            bytes_accessed=rows * hidden * 4 + 4 * width * hidden + 18 * rows * width,
            transcendentals=0,
        ),
        name="middle_back",
    )(*in_hbm(gates, full_in, full_attention, middle, cotangent), gain.reshape(1, -1))


def scalars():
    return pl.BlockSpec(memory_space=pltpu.SMEM)


def by_parts(name, first, second, kinds, body, *extra):
    width = first.shape[1]
    rows = first.shape[0] + second.shape[0]
    starts = first.shape[0] // count

    def kernel(first_ref, second_ref, *refs):
        @pl.when(pl.program_id(0) < starts)
        def _():
            body(first_ref, *refs)

        @pl.when(pl.program_id(0) >= starts)
        def _():
            body(second_ref, *refs)

    return pl.pallas_call(
        kernel,
        grid=(rows // count,),
        out_shape=[pltpu.HBM((rows, width), kind) for kind in kinds],
        in_specs=[
            pl.BlockSpec((count, width), lambda step: (jnp.minimum(step, starts - 1), 0)),
            pl.BlockSpec((count, width), lambda step: (jnp.maximum(step - starts, 0), 0)),
        ]
        + [pl.BlockSpec(line.shape, lambda step: (0, 0)) for line in extra],
        out_specs=[pl.BlockSpec((count, width), lambda step: (step, 0))] * len(kinds),
        compiler_params=pltpu.CompilerParams(vmem_limit_bytes=20 * 2**20),
        cost_estimate=pl.CostEstimate(
            flops=4 * rows * width, bytes_accessed=10 * rows * width, transcendentals=rows
        ),
        name=name,
    )(*in_hbm(first, second), *extra)


def norm_body(rows_ref, gain_ref, values_ref, normed_ref):
    values = rows_ref[...]
    spread = lax.rsqrt(jnp.mean(values * values, axis=-1, keepdims=True) + epsilon)
    values_ref[...] = values
    normed_ref[...] = (values * spread * gain_ref[...]).astype(jnp.bfloat16)


def round_body(rows_ref, values_ref, low_ref):
    values_ref[...] = rows_ref[...]
    low_ref[...] = rows_ref[...].astype(jnp.bfloat16)


def project(place, pieces, normed):
    rows, width = normed.shape
    columns = pieces[0].shape[-1]
    number = len(pieces)

    def kernel(place_ref, *refs):
        normed_ref, out_ref, full_ref, held, sems = refs[number:]

        def body():
            start = pl.multiple_of(pl.program_id(0) * width, 128)
            weight = held[..., pl.ds(start, width)].reshape(width, width)
            out_ref[...] = dot_nn(normed_ref[...], weight).astype(jnp.bfloat16)

        filled(place_ref, refs[:number], full_ref, held, sems, body)

    projected, full = pl.pallas_call(
        kernel,
        grid=(3,),
        out_shape=(
            pltpu.HBM((rows, 3 * width), jnp.bfloat16),
            pltpu.HBM(slab(columns, width), jnp.bfloat16),
        ),
        in_specs=[scalars()]
        + [anywhere] * number
        + [pl.BlockSpec((rows, width), lambda step: (0, 0))],
        out_specs=(pl.BlockSpec((rows, width), lambda step: (0, step)), anywhere),
        scratch_shapes=[
            pltpu.VMEM(slab(columns, width), jnp.bfloat16),
            pltpu.SemaphoreType.DMA((9,)),
        ],
        compiler_params=pltpu.CompilerParams(vmem_limit_bytes=14 * 2**20),
        cost_estimate=pl.CostEstimate(
            flops=6 * rows * width * width,
            bytes_accessed=8 * rows * width + 4 * columns * width,
            transcendentals=0,
        ),
        name="project",
    )(place, *pieces, normed)
    return projected, full.reshape(width, columns)


def middle_kernel(rows_ref, mixed_ref, weight_ref, gain_ref, middle_ref, normed_ref):
    middle = rows_ref[...] + dot_nn(mixed_ref[...], weight_ref[...])
    spread = lax.rsqrt(jnp.mean(middle * middle, axis=-1, keepdims=True) + epsilon)
    middle_ref[...] = middle
    normed_ref[...] = (middle * spread * gain_ref[...]).astype(jnp.bfloat16)


def middle_forward(values, mixed, full_attention, gain, *earlier):
    rows, width = values.shape
    part = rows // 2
    block = pl.BlockSpec((part, width), lambda step: (step, 0))

    def kernel(*refs):
        middle_kernel(*refs[:4], *refs[4 + len(earlier) :])

    return pl.pallas_call(
        kernel,
        grid=(2,),
        out_shape=(
            pltpu.HBM((rows, width), jnp.float32),
            jax.ShapeDtypeStruct((rows, width), jnp.bfloat16),
        ),
        in_specs=[
            block,
            block,
            pl.BlockSpec((width, width), lambda step: (0, 3)),
            pl.BlockSpec((1, width), lambda step: (0, 0)),
        ]
        + [anywhere] * len(earlier),
        out_specs=(block, block),
        compiler_params=pltpu.CompilerParams(vmem_limit_bytes=15 * 2**20),
        cost_estimate=pl.CostEstimate(
            flops=2 * rows * width * width,
            bytes_accessed=12 * rows * width + 2 * width * width,
            transcendentals=0,
        ),
        name="middle_forward",
    )(*in_hbm(values), mixed, *in_hbm(full_attention), gain.reshape(1, -1), *earlier)


def attention_grads_kernel(
    place_ref, normed_ref, grads_ref, mixed_hbm, low_hbm, weight_0, weight_1, weight_2, weight_3,
    gain_ref, ffn_ref, table_ref, kept_ref, sent_ref, small_ref,
    turned, column, ordered, mixed_ref, low_ref, sems,
):
    step = pl.program_id(0)
    last = pl.num_programs(0) - 1
    quarter = column.shape[0] // 4
    copies = [
        pltpu.make_async_copy(mixed_hbm, mixed_ref, sems.at[0]),
        pltpu.make_async_copy(low_hbm, low_ref, sems.at[1]),
    ]

    @pl.when(step == 0)
    def _():
        for copy in copies:
            copy.start()
        turned_rows(place_ref, normed_ref, turned)
        column[...] = jnp.zeros_like(column)

    @pl.when(step < last)
    def _():
        grads = dot_nn(turned[...], grads_ref[0])
        split_store(grads, kept_ref, sent_ref)
        for number, weight in enumerate((weight_0, weight_1, weight_2, weight_3)):
            rows = slice(number * quarter, (number + 1) * quarter)
            product = grads[rows, :] * weight[...].astype(jnp.float32)
            parts = [product[:, lane : lane + 128] for lane in range(0, grads.shape[1], 128)]
            column[rows, :] += sum(parts)

    @pl.when(step == last)
    def _():
        for copy in copies:
            copy.wait()
        turned_rows(place_ref, mixed_ref, turned)
        split_store(dot_nn(turned[...], low_ref[...]), kept_ref, sent_ref)
        for number in range(4):
            row = quarter_owner(number, place_ref[1])
            start = pl.multiple_of(row * quarter, 16)
            ordered[pl.ds(start, quarter), :] = column[number * quarter : (number + 1) * quarter, :]
        gain_grad = jnp.sum(ordered[...].T, axis=0, keepdims=True) / gain_ref[...]
        small_ref[...] = jnp.zeros_like(small_ref)
        lines = gain_grad.shape[1] // 128
        for number, line in enumerate((gain_grad, ffn_ref[...])):
            for part in range(lines):
                row = number * lines + part
                small_ref[row : row + 1, :] = line[:, part * 128 : (part + 1) * 128]
        table = table_ref[...].reshape(-1, table_ref.shape[2])
        small_ref[2 * lines :, : table.shape[1]] = table


def quarter_owner(number, core):
    return 2 * (number % 2) + (core if number >= 2 else 1 - core)


def attention_grads(
    place, normed, grad_projected, mixed, grad_low, full_attention, gain, ffn_grad, table
):
    rows, width = normed.shape
    lines = 2 * (width // 128) + 2 * table.shape[0]

    def fixed(step, where):
        return 0, 0

    def column(step, where):
        return 0, 0, step

    def weight_spec(number):
        return pl.BlockSpec(
            (width // 4, width),
            lambda step, where: (quarter_owner(number, where[1]), jnp.minimum(step, 2)),
        )

    shape = pltpu.HBM((2, width // 4, 4 * width), jnp.bfloat16)
    half = pl.BlockSpec((2, width // 4, width), column)
    return pl.pallas_call(
        attention_grads_kernel,
        grid_spec=pltpu.PrefetchScalarGridSpec(
            num_scalar_prefetch=1,
            grid=(4,),
            in_specs=[
                pl.BlockSpec((rows, width), fixed),
                pl.BlockSpec((1, rows, width), lambda step, where: (jnp.minimum(step, 2), 0, 0)),
                anywhere,
                anywhere,
                *[weight_spec(number) for number in range(4)],
                pl.BlockSpec((1, width), fixed),
                pl.BlockSpec((1, width), fixed),
                pl.BlockSpec(table.shape, lambda step, where: (0, 0, 0)),
            ],
            out_specs=(half, half, pl.BlockSpec((lines, 128), fixed)),
            scratch_shapes=[
                pltpu.VMEM((width, rows), jnp.bfloat16),
                pltpu.VMEM((width, 128), jnp.float32),
                pltpu.VMEM((width, 128), jnp.float32),
                pltpu.VMEM((rows, width), jnp.bfloat16),
                pltpu.VMEM((rows, width), jnp.bfloat16),
                pltpu.SemaphoreType.DMA((2,)),
            ],
        ),
        out_shape=(shape, shape, jax.ShapeDtypeStruct((lines, 128), jnp.float32)),
        compiler_params=pltpu.CompilerParams(vmem_limit_bytes=36 * 2**20),
        cost_estimate=pl.CostEstimate(
            flops=8 * rows * width * width,
            bytes_accessed=12 * rows * width + 14 * width * width,
            transcendentals=0,
        ),
        name="attention_grads",
    )(
        place,
        *in_hbm(normed, grad_projected, mixed, grad_low, *[full_attention] * 4),
        gain.reshape(1, -1),
        ffn_grad,
        table,
    )


def input_back(grad_projected, full_qkv, values, residual, gain, doc_rows):
    rows, width = values.shape
    part = rows // row_parts
    block = pl.BlockSpec((part, width), lambda step: (step, 0))

    def kernel(
        grads_ref, weight_ref, rows_ref, residual_ref, gain_ref,
        doc_ref, query_ref, slots, sems,
    ):
        step = pl.program_id(0)
        total = dot_nt(grads_ref[0], weight_ref[:, :width])
        for third in (1, 2):
            columns = slice(third * width, (third + 1) * width)
            total = total + dot_nt(grads_ref[third], weight_ref[:, columns])
        slots[step], _ = norm_back(total, rows_ref[...], gain_ref[...], residual_ref[...])
        emit(slots, (doc_ref, query_ref), sems)

    return pl.pallas_call(
        kernel,
        grid=(row_parts,),
        out_shape=(
            jax.ShapeDtypeStruct((doc_rows, width), jnp.float32),
            jax.ShapeDtypeStruct((rows - doc_rows, width), jnp.float32),
        ),
        in_specs=[
            pl.BlockSpec((3, part, width), lambda step: (0, step, 0)),
            pl.BlockSpec((width, 3 * width), lambda step: (0, 0)),
            block,
            block,
            pl.BlockSpec((1, width), lambda step: (0, 0)),
        ],
        out_specs=(anywhere, anywhere),
        scratch_shapes=[
            pltpu.VMEM((row_parts, part, width), jnp.float32),
            pltpu.SemaphoreType.DMA((row_parts + 1,)),
        ],
        compiler_params=pltpu.CompilerParams(vmem_limit_bytes=30 * 2**20),
        cost_estimate=pl.CostEstimate(
            flops=6 * rows * width * width,
            bytes_accessed=18 * rows * width + 6 * width * width,
            transcendentals=0,
        ),
        name="input_back",
    )(*in_hbm(grad_projected, full_qkv, values, residual), gain.reshape(1, -1))


def layer_outputs(middle, activated, full_ff, doc_rows):
    rows, width = middle.shape
    hidden = activated.shape[1]
    part = rows // row_parts

    def kernel(middle_ref, act_ref, weight_ref, doc_ref, query_ref, slots, sems):
        slots[pl.program_id(0)] = middle_ref[...] + dot_nn(act_ref[...], weight_ref[...])
        emit(slots, (doc_ref, query_ref), sems)

    return pl.pallas_call(
        kernel,
        grid=(row_parts,),
        out_shape=(
            jax.ShapeDtypeStruct((doc_rows, width), jnp.float32),
            jax.ShapeDtypeStruct((rows - doc_rows, width), jnp.float32),
        ),
        in_specs=[
            pl.BlockSpec((part, width), lambda step: (step, 0)),
            pl.BlockSpec((part, hidden), lambda step: (step, 0)),
            pl.BlockSpec((hidden, width), lambda step: (0, 0)),
        ],
        out_specs=(anywhere, anywhere),
        scratch_shapes=[
            pltpu.VMEM((row_parts, part, width), jnp.float32),
            pltpu.SemaphoreType.DMA((row_parts + 1,)),
        ],
        compiler_params=pltpu.CompilerParams(vmem_limit_bytes=24 * 2**20),
        cost_estimate=pl.CostEstimate(
            flops=2 * rows * width * hidden,
            bytes_accessed=8 * rows * width + 2 * hidden * (rows + width),
            transcendentals=0,
        ),
        name="layer_outputs",
    )(*in_hbm(middle, activated, full_ff))


def body(
    doc_inputs,
    query_inputs,
    doc_mask,
    query_lengths,
    doc_cotangent,
    query_cotangent,
    qkv_weight,
    out_weight,
    in_weight,
    ff_weight,
    attn_gain,
    ffn_gain,
    bias_table,
):
    doc_count, doc_length, model_width = doc_inputs.shape
    group_count, group_length = (query_inputs.shape[0], query_inputs.shape[1])
    head_count = bias_table.shape[1]
    doc_rows = doc_count * doc_length
    low = jnp.bfloat16
    routed = hand_routed()
    place = own_place() if routed else (0, 0, 0, 0)
    place_vector = jnp.stack([jnp.asarray(index, jnp.int32) for index in place])

    attention_shard = jnp.concatenate([qkv_weight, out_weight], axis=1).astype(low)
    in_shard = in_weight.astype(low)
    ff_shard = ff_weight.astype(low)

    kinds = (jnp.float32, low)
    values, normed = by_parts(
        "norm_rows",
        doc_inputs.reshape(doc_rows, model_width),
        query_inputs.reshape(-1, model_width),
        kinds,
        norm_body,
        attn_gain.reshape(1, -1),
    )
    cotangent_parts = (
        doc_cotangent.reshape(doc_rows, model_width),
        query_cotangent.reshape(-1, model_width),
    )
    places = jnp.arange(group_length, dtype=jnp.int32)
    query_mask = places[None, :] < query_lengths[:, None]
    onehot = lines_onehot(bias_table.shape[0])
    lines = jnp.einsum("pn,nh->hp", onehot, bias_table, precision=highest)
    lines = lines.reshape(head_count // 2, 2, 4 * count)
    doc_masking = jnp.where(doc_mask > 0, 0.0, -1e9).astype(jnp.float32)
    query_masking = jnp.where(query_mask, 0.0, -1e9).astype(jnp.float32)
    query_masking = query_masking.reshape(-1, 1, count)

    if routed:
        column_a = gather_column(attention_shard)
        row_f = jnp.stack(in_order(ff_shard, swap(ff_shard, dx=1), place[3]))
        column_a, row_f, normed, lines, doc_masking, query_masking, in_shard, cotangent_parts = (
            together(
                column_a, row_f, normed, lines, doc_masking, query_masking, in_shard,
                cotangent_parts,
            )
        )
        plane_a = gather_plane(place, attention_shard, column_a)
        cotangent, cot_low = by_parts("round_rows", *cotangent_parts, kinds, round_body)
        plane_a, cotangent, cot_low = together(plane_a, cotangent, cot_low)
        near_a = gather_near(place, *plane_a)
        column_i = gather_column(in_shard)
        far_a = gather_far(*near_a)
        far_f = swap(row_f, dy=1)
        column_i, far_a, far_f = together(column_i, far_a, far_f)
        plane_f = jnp.stack(in_order(row_f, far_f, place[0]))
        pieces = gather_order(near_a, far_a, gather_core(*near_a), gather_core(*far_a))
        plane_i = gather_plane(place, in_shard, column_i)
    else:
        cotangent, cot_low = by_parts("round_rows", *cotangent_parts, kinds, round_body)
        pieces = (split_rows(lax.all_gather(attention_shard, both, axis=0, tiled=True)),)
    projected, full_attention = project(place_vector, pieces, normed)
    if routed:
        plane_i, projected = together(plane_i, projected)
        near_i = gather_near(place, *plane_i)
        far_i = gather_far(*near_i)
        second_f = swap(plane_f, dz=2)
    mixed, doc_probs, query_probs = attend(
        projected, lines, doc_masking, query_masking, group_length
    )
    if routed:
        mixed, far_i, second_f = together(mixed, far_i, second_f)
        others_f = gather_others(plane_f, second_f)
        pieces = gather_order(near_i, far_i, gather_core(*near_i), gather_core(*far_i))
    else:
        pieces = (split_rows(lax.all_gather(in_shard, both, axis=0, tiled=True)),)
    middle, normed_two = middle_forward(values, mixed, full_attention, ffn_gain)
    if routed:
        pieces, normed_two = together(pieces, normed_two)
        core_f = gather_core(plane_f, second_f)
    activated, by_gate, by_up, kept, sent, full_in = gate_forward(
        place_vector, pieces, normed_two, cot_low
    )
    if routed:
        others_f, core_f, by_gate, kept, sent = together(others_f, core_f, by_gate, kept, sent)
        core_others = gather_core(*others_f)
        pieces = (plane_f, others_f[0], second_f, others_f[1])
        pieces += (core_f[0], core_others[0], core_f[1], core_others[1])
        ff_grads = NarrowScatter(kept, sent, place_vector)
        got_f = ff_grads.core()
        pieces, got_f = together(pieces, got_f)
        near_f = ff_grads.plane(got_f)
    else:
        pieces = (split_rows(lax.all_gather(ff_shard, both, axis=0, tiled=True)),)
        grad_ff = joined_halves(kept, sent)
    gates, kept, sent, full_ff = gate_back(
        place_vector, pieces, normed_two, cot_low, by_gate, by_up
    )
    if routed:
        gates, kept, sent, near_f = together(gates, kept, sent, near_f)
        in_grads = Scatter(kept, sent, place_vector)
        far_f = ff_grads.far(ff_grads.far_sums(got_f, near_f))
        got_i = in_grads.core()
    else:
        grad_in = joined_halves(kept, sent)
    grad_middle, grad_middle_low, grad_mixed, grad_ffn_gain = middle_back(
        gates, full_in, middle, cotangent, ffn_gain, full_attention
    )
    if routed:
        grad_mixed, far_f, got_i = together(grad_mixed, far_f, got_i)
        near_i = in_grads.plane(got_i)
        shares_f = ff_grads.column(ff_grads.column_sums(got_f, near_f, far_f))
    grad_projected, grad_table = attend_back(
        projected, grad_mixed, doc_probs, query_probs, onehot, doc_length
    )
    if routed:
        grad_projected, grad_table, shares_f, near_i = together(
            grad_projected, grad_table, shares_f, near_i
        )
        far_i = in_grads.far(got_i, near_i)
    kept, sent, small = attention_grads(
        place_vector, normed, grad_projected, mixed, grad_middle_low, full_attention, attn_gain,
        grad_ffn_gain, grad_table,
    )
    if routed:
        kept, sent, far_i, small, grad_projected, shares_f, activated = together(
            kept, sent, far_i, small, grad_projected, shares_f, activated
        )
        attention = Scatter(kept, sent, place_vector)
        got_a = attention.core()
        small = add_flipped(small, {"dc": 1})
        sums_i = in_grads.column_sums(got_i, near_i, far_i)
        got_a, sums_i, small, grad_projected, shares_f, activated = together(
            got_a, sums_i, small, grad_projected, shares_f, activated
        )
        near_a = attention.plane(got_a)
        shares_i = in_grads.column(sums_i)
        small = add_flipped(small, {"dz": 1})
    grad_inputs = input_back(
        grad_projected, full_attention, values, grad_middle, attn_gain, doc_rows
    )
    if routed:
        near_a, grad_inputs, small, shares_f, shares_i, activated = together(
            near_a, grad_inputs, small, shares_f, shares_i, activated
        )
        far_a = attention.far(got_a, near_a)
        small = add_flipped(small, {"dz": 2})
        far_a, small, shares_f, shares_i, activated = together(
            far_a, small, shares_f, shares_i, activated
        )
        sums_a = attention.column_sums(got_a, near_a, far_a)
        sums_a, small, shares_f, shares_i, activated = together(
            sums_a, small, shares_f, shares_i, activated
        )
        shares_a = attention.column(sums_a)
        small = add_flipped(small, {"dx": 1}, {"dy": 1})
    outputs = layer_outputs(middle, activated, full_ff, doc_rows)
    if routed:
        ff_grad_shard = summed(*shares_f)
        in_grad_shard = summed(*shares_i)
        grad_qkv = summed(*[share[:, : 3 * model_width] for share in shares_a])
        grad_out = summed(*[share[:, 3 * model_width :] for share in shares_a])
    else:
        scatter = functools.partial(
            lax.psum_scatter, axis_name=both, scatter_dimension=0, tiled=True
        )
        ff_grad_shard = scatter(grad_ff)
        in_grad_shard = scatter(grad_in)
        grad_attention = scatter(joined_halves(kept, sent))
        grad_qkv = grad_attention[:, : 3 * model_width]
        grad_out = grad_attention[:, 3 * model_width :]
        small = lax.psum(small, both)
    width_lines = model_width // 128
    in_grad_shard = in_grad_shard.reshape(in_weight.shape[0], -1, 2, tile)
    in_grad_shard = jnp.swapaxes(in_grad_shard, 1, 2).reshape(in_weight.shape)
    return (
        outputs[0].reshape(doc_inputs.shape),
        outputs[1].reshape(query_inputs.shape),
        grad_inputs[0].reshape(doc_inputs.shape),
        grad_inputs[1].reshape(query_inputs.shape),
        grad_qkv,
        grad_out,
        in_grad_shard,
        ff_grad_shard,
        small[:width_lines].reshape(model_width),
        small[width_lines : 2 * width_lines].reshape(model_width),
        small[2 * width_lines :, : bias_table.shape[0]].T,
    )


def solution(mesh):
    placed = (
        P(("dp", "fsdp"), None, None),
        P(("dp", "fsdp"), None, None),
        P(("dp", "fsdp"), None),
        P(("dp", "fsdp")),
        P(("dp", "fsdp"), None, None),
        P(("dp", "fsdp"), None, None),
        P(("dp", "fsdp"), None),
        P(("dp", "fsdp"), None),
        P(("dp", "fsdp"), None),
        P(("dp", "fsdp"), None),
        P(),
        P(),
        P(),
    )
    return jax.shard_map(
        body,
        mesh=mesh,
        in_specs=placed,
        out_specs=(
            P(("dp", "fsdp"), None, None),
            P(("dp", "fsdp"), None, None),
            P(("dp", "fsdp"), None, None),
            P(("dp", "fsdp"), None, None),
            P(("dp", "fsdp"), None),
            P(("dp", "fsdp"), None),
            P(("dp", "fsdp"), None),
            P(("dp", "fsdp"), None),
            P(),
            P(),
            P(),
        ),
        check_vma=False,
    )
```

```python
import functools
import math

import jax
import jax.numpy as jnp
from jax import lax
from jax.experimental import pallas as pl
from jax.experimental.pallas import tpu as pltpu
from jax.sharding import PartitionSpec as P

both = ("dp", "fsdp")
epsilon = 1e-06
highest = lax.Precision.HIGHEST
anywhere = pl.BlockSpec(memory_space=pl.ANY)


def place_index(y, c, z, x):
    return ((y * 2 + c) * 4 + z) * 2 + x


def flip_pairs(dy=0, dc=0, dz=0, dx=0):
    pairs = []
    for y in range(2):
        for c in range(2):
            for z in range(4):
                for x in range(2):
                    pairs.append(
                        (place_index(y, c, z, x), place_index(y ^ dy, c ^ dc, z ^ dz, x ^ dx))
                    )
    return pairs


def swap(values, **flips):
    return lax.ppermute(values, both, flip_pairs(**flips))


def hand_routed():
    return (lax.axis_size("dp"), lax.axis_size("fsdp")) == (4, 8)


def own_place():
    outer = lax.axis_index("dp")
    inner = lax.axis_index("fsdp")
    return outer // 2, outer % 2, inner // 2, inner % 2


def after(values, *earlier):
    return lax.optimization_barrier((values, *earlier))[0]


def in_hbm(*values):
    return [pltpu.with_memory_space_constraint(value, pltpu.HBM) for value in values]


def together(*values):
    return lax.optimization_barrier(values)


def fill_copies(place_ref, pieces, target, sems, by_column):
    if len(pieces) == 1:
        return [pltpu.make_async_copy(pieces[0], target, sems.at[0])]
    y, c, z, x = place_ref[0], place_ref[1], place_ref[2], place_ref[3]
    copies = []
    even = z - z % 2
    for number, piece in enumerate(pieces):
        core = c ^ (number // 4)
        kind = number % 4
        if by_column:
            where = target.at[:, core, z ^ kind]
        elif kind < 2:
            where = target.at[y ^ kind, core, pl.ds(even, 2)]
        else:
            where = target.at[:, core, pl.ds(even ^ 2, 2), x ^ (kind - 2)]
        copies.append(pltpu.make_async_copy(piece, where, sems.at[number]))
    return copies


def filled(place_ref, pieces, full_ref, held, sems, body, meanwhile=None, by_column=False):
    step = pl.program_id(0)
    kept = pltpu.make_async_copy(held, full_ref, sems.at[8])

    @pl.when(step == 0)
    def _():
        copies = fill_copies(place_ref, pieces, held, sems, by_column)
        for copy in copies:
            copy.start()
        if meanwhile is not None:
            meanwhile()
        for copy in copies:
            copy.wait()
        kept.start()

    body()

    @pl.when(step == pl.num_programs(0) - 1)
    def _():
        kept.wait()


def emit(slots, targets, sems):
    step, rows = pl.program_id(0), slots.shape[1]
    copies = []
    for number in range(slots.shape[0]):
        start = 0
        for target in targets:
            low = max(number * rows, start)
            high = min((number + 1) * rows, start + target.shape[0])
            if low < high:
                source = slots.at[number, pl.ds(low - number * rows, high - low)]
                where = target.at[pl.ds(low - start, high - low)]
                copy = pltpu.make_async_copy(source, where, sems.at[len(copies)])
                copies.append((number, copy))
            start += target.shape[0]
    for number in range(slots.shape[0]):

        @pl.when(step == number)
        def _():
            for owner, copy in copies:
                if owner == number:
                    copy.start()

    @pl.when(step == slots.shape[0] - 1)
    def _():
        for _, copy in copies:
            copy.wait()


def gather_order(near, far, core_near, core_far):
    return (near[0], far[0], near[1], far[1], core_near[0], core_far[0], core_near[1], core_far[1])


def slab(columns, rows):
    return (2, 2, 4, 2, rows // 32, columns)


def split_rows(full):
    return full.reshape(slab(full.shape[1], full.shape[0]))


def in_order(own, other, index):
    odd = index % 2 == 1
    return jnp.where(odd, other, own), jnp.where(odd, own, other)


def gather_column(shard):
    two, three, one = [swap(shard, dz=flip) for flip in (2, 3, 1)]
    return one, two, three


def gather_plane(place, shard, column):
    first = jnp.stack(in_order(shard, column[0], place[2]))
    second = jnp.stack(in_order(column[1], column[2], place[2]))
    return first, second, swap(first, dx=1), swap(second, dy=1)


def gather_near(place, first, second, first_near, second_near):
    even, odd = in_order(first, first_near, place[3])
    first = jnp.stack([even[0], odd[0], even[1], odd[1]]).reshape(2, 2, *first.shape[1:])
    second = jnp.stack(in_order(second, second_near, place[0]))
    return first, second


def gather_far(first, second):
    return swap(first, dy=1), swap(second, dx=1)


def gather_others(own, second):
    return swap(own, dz=1), swap(second, dz=1)


def gather_core(*pieces):
    return tuple(swap(piece, dc=1) for piece in pieces)


def summed(*terms):
    total = terms[0].astype(jnp.float32)
    for term in terms[1:]:
        total = total + term.astype(jnp.float32)
    return total


def joined_halves(kept, sent):
    return jnp.stack([kept, sent], axis=1).reshape(-1, kept.shape[2]).astype(jnp.float32)


def route(name, place, sources, targets, body, scratch=()):
    def spec(array, lead, pick):
        block = (*lead, *array.shape[-2:])
        return pl.BlockSpec(block, lambda step, where: (*pick(where), 0, 0))

    return pl.pallas_call(
        body,
        grid_spec=pltpu.PrefetchScalarGridSpec(
            num_scalar_prefetch=1,
            grid=(1,),
            in_specs=[spec(*source) for source in sources],
            out_specs=[spec(*target) for target in targets],
            scratch_shapes=scratch,
        ),
        out_shape=[target[0] for target in targets],
        compiler_params=pltpu.CompilerParams(vmem_limit_bytes=20 * 2**20),
        cost_estimate=pl.CostEstimate(
            flops=0,
            bytes_accessed=8 * len(sources) * math.prod(sources[0][0].shape[-2:]),
            transcendentals=0,
        ),
        name=name,
    )(place, *[source[0] for source in sources])


def whole_block(target):
    lead = target.shape[:-2]
    return target, lead, lambda where: (0,) * len(lead)


def store_sum(out_ref, *refs):
    blocks = math.prod(refs[0].shape[:-2])
    for number in range(blocks):
        terms = []
        for ref in (out_ref, *refs):
            index, rest = [], number
            for size in reversed(ref.shape[:-2]):
                index.insert(0, rest % size)
                rest //= size
            terms.append(ref.at[tuple(index)])
        terms[0][...] = summed(*[term[...] for term in terms[1:]]).astype(out_ref.dtype)


class Scatter:
    def __init__(self, kept, sent, place, pinned=True):
        self.place = place
        self.pinned = pinned
        self.block = (kept.shape[1] // 8, kept.shape[2])
        self.shape = (2, 4, 2, *self.block)
        self.kept = kept.reshape(self.shape)
        self.sent = sent

    def target(self, *lead, dtype=jnp.bfloat16):
        return jax.ShapeDtypeStruct((*lead, *self.block), dtype)

    def both(self, got, lead, pick):
        kept = in_hbm(self.kept)[0] if self.pinned else self.kept
        return [(kept, lead, pick), (got, lead, pick)]

    def core(self):
        return swap(self.sent, dc=1).reshape(self.shape)

    def plane(self, got):
        def body(place_ref, *refs):
            store_sum(refs[4], *refs[0:2])
            store_sum(refs[5], *refs[2:4])

        sources = self.both(got, (2, 2, 1), lambda where: (0, 0, 1 - where[3]))
        sources += self.both(got, (1, 2, 2), lambda where: (1 - where[0], 1, 0))
        target = whole_block(self.target(2, 2))
        one, two = route("plane", self.place, sources, [target, target], body)
        return swap(one, dx=1), swap(two, dy=1)

    def far(self, got, near):
        def body(place_ref, *refs):
            store_sum(refs[6], *refs[0:3])
            store_sum(refs[7], *refs[3:6])

        sources = [
            *self.both(got, (1, 2, 1), lambda where: (1 - where[0], 0, where[3])),
            (near[0], (1, 2), lambda where: (1 - where[0], 0)),
            *self.both(got, (1, 2, 1), lambda where: (where[0], 1, 1 - where[3])),
            (near[1], (2, 1), lambda where: (0, 1 - where[3])),
        ]
        target = whole_block(self.target(2))
        one, two = route("far", self.place, sources, [target, target], body)
        return swap(one, dy=1), swap(two, dx=1)

    def column_sources(self, near, far):
        return [
            (near[0], (1, 2), lambda where: (where[0], 0)),
            (far[0], (2,), lambda where: (0,)),
            (near[1], (2, 1), lambda where: (0, where[3])),
            (far[1], (2,), lambda where: (0,)),
        ]

    def column_terms(self, row, refs):
        if row < 2:
            return refs[0].at[0, row], refs[1].at[row]
        return refs[2].at[row - 2, 0], refs[3].at[row - 2]

    def column_sums(self, got, near, far):
        sources = self.both(got, (1, 4, 1), lambda where: (where[0], 0, where[3]))
        sources += self.column_sources(near, far)
        number = len(sources)

        def body(place_ref, *refs):
            *outs, total = refs[number:]
            for row in range(4):
                terms = (refs[0].at[0, row, 0], refs[1].at[0, row, 0])
                terms += self.column_terms(row, refs[2:number])
                total[row] = summed(*[term[...] for term in terms])
            for flip, out in enumerate(outs):
                out[...] = total[place_ref[2] ^ flip].astype(out.dtype)

        targets = [self.target(dtype=jnp.float32)] + [self.target()] * 3
        targets = [whole_block(target) for target in targets]
        scratch = [pltpu.VMEM((4, *self.block), jnp.float32)]
        return tuple(route("column", self.place, sources, targets, body, scratch))

    def column(self, sums):
        return sums[0], *[swap(share, dz=flip) for flip, share in zip((1, 2, 3), sums[1:])]


class NarrowScatter(Scatter):
    def both(self, got, lead, pick, pinned=True):
        kept, got = in_hbm(self.kept, got) if pinned else (self.kept, got)
        return [(kept, lead, pick), (got, lead, pick)]

    def plane(self, got):
        def body(place_ref, *refs):
            store_sum(refs[2], *refs[0:2])

        sources = self.both(got, (2, 4, 1), lambda where: (0, 0, 1 - where[3]), False)
        target = whole_block(self.target(2, 4))
        (sums,) = route("plane", self.place, sources, [target], body)
        return swap(sums, dx=1)

    def far_sums(self, got, near):
        def body(place_ref, *refs):
            store_sum(refs[3], *refs[0:3])

        sources = self.both(got, (1, 4, 1), lambda where: (1 - where[0], 0, where[3]))
        sources.append((near, (1, 4), lambda where: (1 - where[0], 0)))
        return route("far", self.place, sources, [whole_block(self.target(4))], body)[0]

    def far(self, sums):
        return swap(sums, dy=1)

    def column_sources(self, near, far):
        return [
            (near, (1, 4), lambda where: (where[0], 0)),
            (far, (4,), lambda where: (0,)),
        ]

    def column_terms(self, row, refs):
        return refs[0].at[0, row], refs[1].at[row]


def add_flipped(values, *steps):
    for flips in steps:
        values = values + swap(values, **flips)
    return values


count = 128


def relative_places():
    places = jnp.arange(4 * count, dtype=jnp.int32)
    return jnp.where(places < 3 * count, places - count, places - 5 * count)


def bucket_of(relative):
    distance = jnp.abs(relative)
    larger = jnp.zeros_like(distance)
    for threshold in (12, 16, 23, 32, 46, 64, 91):
        larger = larger + (distance >= threshold).astype(jnp.int32)
    bucket = jnp.where(distance < 8, distance, 8 + larger)
    return bucket + 16 * (relative > 0).astype(jnp.int32)


def lines_onehot(bucket_count):
    labels = jnp.arange(bucket_count, dtype=jnp.int32)
    return (bucket_of(relative_places())[:, None] == labels).astype(jnp.float32)


def own_lanes(head, shape):
    lanes = lax.broadcasted_iota(jnp.int32, shape, 1)
    return lanes < shape[1] // 2 if head == 0 else lanes >= shape[1] // 2


def keep_lanes(head, values):
    return jnp.where(own_lanes(head, values.shape), values, jnp.zeros_like(values))


def both_heads(values):
    return jnp.concatenate([keep_lanes(0, values), keep_lanes(1, values)], axis=0)


def joined(stacked):
    first, second = jnp.split(stacked, 2, axis=0)
    return jnp.where(own_lanes(0, first.shape), first, second).astype(jnp.bfloat16)


def softmax_rows(scores):
    raised = jnp.exp(scores - jnp.max(scores, axis=-1, keepdims=True))
    return raised * (1.0 / jnp.sum(raised, axis=-1, keepdims=True))


def dot_nt(left, right):
    return lax.dot_general(
        left, right, (((1,), (1,)), ((), ())), preferred_element_type=jnp.float32
    )


def dot_nn(left, right):
    return jnp.dot(left, right, preferred_element_type=jnp.float32)


def attend_kernel(
    docs, length, group, q_ref, k_ref, v_ref, line_ref, mask_ref, query_mask_ref,
    mixed_ref, doc_probs_ref, query_probs_ref, scores_scratch, probs_scratch,
):
    blocks = length // count
    query_start = docs * length
    query_blocks = (q_ref.shape[0] - query_start) // count
    row_group = lax.broadcasted_iota(jnp.int32, (count, count), 0) // group
    column_group = lax.broadcasted_iota(jnp.int32, (count, count), 1) // group
    bands, edges = [], []
    for head in range(2):
        line = line_ref[0, head : head + 1, :]
        band = pltpu.roll(
            jnp.broadcast_to(line, (count, 4 * count)), 0, 1, stride=1, stride_axis=0
        )
        bands.append(band)
        edges.append(
            (
                jnp.broadcast_to(line[:, 4 * count - 1 :], (1, count)),
                jnp.broadcast_to(line[:, 3 * count - 1 : 3 * count], (1, count)),
            )
        )
    for doc in range(docs):
        base = doc * length
        whole = slice(base, base + length)
        masking = mask_ref[doc : doc + 1, :]
        for head in range(2):
            own = slice(head * length, (head + 1) * length)
            scores_scratch[own, :] = dot_nt(keep_lanes(head, q_ref[whole, :]), k_ref[whole, :])
        halves = []
        for head in range(2):
            own = slice(head * length, (head + 1) * length)
            for row in range(blocks):
                rows = slice(row * count, (row + 1) * count)
                stacked = slice(head * length + row * count, head * length + (row + 1) * count)
                shifted = []
                for column in range(blocks):
                    columns = slice(column * count, (column + 1) * count)
                    away = column - row
                    block = scores_scratch[stacked, columns]
                    if abs(away) > 1:
                        block = block + (edges[head][away > 0] + masking[:, columns])
                    else:
                        start = (away + 1) * count
                        block = block + bands[head][:, start : start + count]
                        block = block + masking[:, columns]
                    shifted.append(block)
                probs = softmax_rows(jnp.concatenate(shifted, axis=1))
                doc_probs_ref[head, base + row * count : base + (row + 1) * count, :] = probs
                probs_scratch[stacked, :] = probs.astype(jnp.bfloat16)
            halves.append(dot_nn(probs_scratch[own, :], v_ref[whole, :]))
        mixed_ref[whole, :] = joined(jnp.concatenate(halves, axis=0))
    for block in range(query_blocks):
        rows = slice(query_start + block * count, query_start + (block + 1) * count)
        masking = query_mask_ref[block]
        scores = dot_nt(both_heads(q_ref[rows, :]), k_ref[rows, :])
        low = []
        for head in range(2):
            bias = jnp.where(
                row_group == column_group, bands[head][:, count : 2 * count], -1e9
            )
            probs = softmax_rows(scores[head * count : (head + 1) * count, :] + bias + masking)
            query_probs_ref[head, block * count : (block + 1) * count, :] = probs
            low.append(probs.astype(jnp.bfloat16))
        mixed_ref[rows, :] = joined(dot_nn(jnp.concatenate(low, axis=0), v_ref[rows, :]))


def pair_spec(rows, offset):
    return pl.BlockSpec((rows, 2 * 64), lambda pair: (0, offset + pair))


def attend(projected, lines, doc_mask, query_mask, group):
    docs, length = doc_mask.shape
    rows, width = projected.shape[0], projected.shape[1] // 3
    pairs = lines.shape[0]
    query_rows = rows - docs * length
    return pl.pallas_call(
        functools.partial(attend_kernel, docs, length, group),
        grid=(pairs,),
        out_shape=(
            jax.ShapeDtypeStruct((rows, width), jnp.bfloat16),
            pltpu.HBM((2 * pairs, docs * length, length), jnp.float32),
            pltpu.HBM((2 * pairs, query_rows, count), jnp.float32),
        ),
        in_specs=[
            pair_spec(rows, 0),
            pair_spec(rows, pairs),
            pair_spec(rows, 2 * pairs),
            pl.BlockSpec((1, 2, 4 * count), lambda pair: (pair, 0, 0)),
            pl.BlockSpec((docs, length), lambda pair: (0, 0)),
            pl.BlockSpec(query_mask.shape, lambda pair: (0, 0, 0)),
        ],
        out_specs=(
            pair_spec(rows, 0),
            pl.BlockSpec((2, docs * length, length), lambda pair: (pair, 0, 0)),
            pl.BlockSpec((2, query_rows, count), lambda pair: (pair, 0, 0)),
        ),
        scratch_shapes=[
            pltpu.VMEM((2 * length, length), jnp.float32),
            pltpu.VMEM((2 * length, length), jnp.bfloat16),
        ],
        compiler_params=pltpu.CompilerParams(vmem_limit_bytes=18 * 2**20),
        cost_estimate=pl.CostEstimate(
            flops=2 * 2 * pairs * (docs * length * length + query_rows * count) * 128 * 2,
            bytes_accessed=rows * width * 8 + 8 * pairs * docs * length * length,
            transcendentals=2 * pairs * (docs * length * length + query_rows * count),
        ),
        name="attend",
    )(*in_hbm(projected, projected, projected), lines, doc_mask, query_mask)


def attend_back_kernel(
    docs, length, q_ref, k_ref, v_ref, grad_ref, doc_probs_ref, query_probs_ref, onehot_ref,
    out_ref, table_ref, grads_scratch, scores_scratch, probs_scratch, lines_scratch,
):
    blocks = length // count
    query_start = docs * length
    query_blocks = (q_ref.shape[0] - query_start) // count
    low = jnp.bfloat16
    half = q_ref.shape[1] // 2
    band = [[None] * 5, [None] * 5]

    def gather(head, place, block):
        held = band[head][place]
        band[head][place] = block if held is None else held + block

    def backward(probs, grad_probs):
        product = probs * grad_probs
        return product - probs * jnp.sum(product, axis=-1, keepdims=True)

    for doc in range(docs):
        base = doc * length
        whole = slice(base, base + length)
        for head in range(2):
            own = slice(head * length, (head + 1) * length)
            grads_scratch[own, :] = dot_nt(keep_lanes(head, grad_ref[whole, :]), v_ref[whole, :])
        halves, grad_k, grad_v = [], [], []
        q_turned = q_ref[whole, :].T
        grad_turned = grad_ref[whole, :].T
        for head in range(2):
            own = slice(head * length, (head + 1) * length)
            for row in range(blocks):
                rows = slice(base + row * count, base + (row + 1) * count)
                stacked = slice(head * length + row * count, head * length + (row + 1) * count)
                probs = doc_probs_ref[head, rows, :]
                scores = backward(probs, grads_scratch[stacked, :])
                for column in range(blocks):
                    away = max(-2, min(2, column - row))
                    block = scores[:, column * count : (column + 1) * count]
                    if abs(away) == 2:
                        block = jnp.sum(block.reshape(count // 8, 8, count), axis=0)
                    gather(head, away + 2, block)
                scores_scratch[stacked, :] = scores.astype(low)
                probs_scratch[stacked, :] = probs.astype(low)
            halves.append(dot_nn(scores_scratch[own, :], k_ref[whole, :]))
            part = slice(head * half, (head + 1) * half)
            grad_k.append(dot_nn(q_turned[part, :], scores_scratch[own, :]))
            grad_v.append(dot_nn(grad_turned[part, :], probs_scratch[own, :]))
        out_ref[0, whole, :] = joined(jnp.concatenate(halves, axis=0))
        out_ref[1, whole, :] = jnp.concatenate(grad_k, axis=0).astype(low).T
        out_ref[2, whole, :] = jnp.concatenate(grad_v, axis=0).astype(low).T
    for block in range(query_blocks):
        rows = slice(query_start + block * count, query_start + (block + 1) * count)
        grad_probs = dot_nt(both_heads(grad_ref[rows, :]), v_ref[rows, :])
        low_scores, low_probs = [], []
        for head in range(2):
            probs = query_probs_ref[head, block * count : (block + 1) * count, :]
            scores = backward(probs, grad_probs[head * count : (head + 1) * count, :])
            gather(head, 2, scores)
            low_scores.append(scores.astype(low))
            low_probs.append(probs.astype(low))
        out_ref[0, rows, :] = joined(dot_nn(jnp.concatenate(low_scores, axis=0), k_ref[rows, :]))
        turned = jnp.concatenate(low_scores, axis=1).T
        turned = jnp.concatenate([turned, jnp.concatenate(low_probs, axis=1).T], axis=1)
        empty = jnp.zeros((count, 2 * half), low)
        weights = jnp.concatenate(
            [
                jnp.concatenate([q_ref[rows, :], empty], axis=1),
                jnp.concatenate([empty, grad_ref[rows, :]], axis=1),
            ],
            axis=0,
        )
        both_grads = dot_nn(turned, weights)
        out_ref[1, rows, :] = joined(both_grads[:, : 2 * half])
        out_ref[2, rows, :] = joined(both_grads[:, 2 * half :])
    lines = []
    for head in range(2):
        below, before, middle, after, above = band[head]
        wide = jnp.concatenate([before, middle, after, jnp.zeros_like(middle)], axis=1)
        eights = [wide[:8]]
        for start in range(8, count, 8):
            eights.append(pltpu.roll(wide[start : start + 8], 4 * count - start, 1))
        wide = sum(eights)
        wide = jnp.concatenate([wide[7 - row : 8 - row] for row in range(8)], axis=0)
        wide = pltpu.roll(wide, 4 * count - 7, 1, stride=1, stride_axis=0)
        wide = jnp.sum(wide, axis=0, keepdims=True)
        far = jnp.concatenate(
            [
                jnp.zeros((1, 2 * count), jnp.float32),
                jnp.sum(above, axis=0, keepdims=True),
                jnp.sum(below, axis=0, keepdims=True),
            ],
            axis=1,
        )
        lines.append(wide + far)
    pair = pl.program_id(0)
    lines_scratch[pair] = jnp.concatenate(lines, axis=0)

    @pl.when(pair == pl.num_programs(0) - 1)
    def _():
        table_ref[...] = jnp.dot(
            lines_scratch[...].reshape(-1, 4 * count),
            onehot_ref[...],
            precision=highest,
            preferred_element_type=jnp.float32,
        ).reshape(table_ref.shape)


def attend_back(projected, grad_mixed, doc_probs, query_probs, onehot, length):
    rows, width = grad_mixed.shape
    pairs = doc_probs.shape[0] // 2
    docs = doc_probs.shape[1] // length
    query_rows = query_probs.shape[1]

    return pl.pallas_call(
        functools.partial(attend_back_kernel, docs, length),
        grid=(pairs,),
        out_shape=(
            jax.ShapeDtypeStruct((3, rows, width), jnp.bfloat16),
            pltpu.HBM((pairs, 2, onehot.shape[1]), jnp.float32),
        ),
        in_specs=[
            pair_spec(rows, 0),
            pair_spec(rows, pairs),
            pair_spec(rows, 2 * pairs),
            pair_spec(rows, 0),
            pl.BlockSpec((2, docs * length, length), lambda pair: (pair, 0, 0)),
            pl.BlockSpec((2, query_rows, count), lambda pair: (pair, 0, 0)),
            pl.BlockSpec(onehot.shape, lambda pair: (0, 0)),
        ],
        out_specs=(
            pl.BlockSpec((3, rows, 2 * 64), lambda pair: (0, 0, pair)),
            pl.BlockSpec((pairs, 2, onehot.shape[1]), lambda pair: (0, 0, 0)),
        ),
        scratch_shapes=[
            pltpu.VMEM((2 * length, length), jnp.float32),
            pltpu.VMEM((2 * length, length), jnp.bfloat16),
            pltpu.VMEM((2 * length, length), jnp.bfloat16),
            pltpu.VMEM((pairs, 2, 4 * count), jnp.float32),
        ],
        compiler_params=pltpu.CompilerParams(vmem_limit_bytes=22 * 2**20),
        cost_estimate=pl.CostEstimate(
            flops=2 * 2 * pairs * (docs * length * length + query_rows * count) * 128 * 4,
            bytes_accessed=rows * width * 14 + 8 * pairs * docs * length * length,
            transcendentals=0,
        ),
        name="attend_back",
    )(*in_hbm(projected, projected, projected, grad_mixed, doc_probs, query_probs), onehot)


def dot_tn(left, right):
    return lax.dot_general(
        left, right, (((0,), (0,)), ((), ())), preferred_element_type=jnp.float32
    )


tile = 512
row_parts = 2
curve = 0.044715
slope = 0.7978845608028654


def turned_rows(place_ref, values, turned):
    quarter = values.shape[1] // 4
    flipped = values[...].T
    for outer in range(2):
        for core in range(2):
            kept = core ^ 1 ^ place_ref[1]
            start = pl.multiple_of((2 * kept + outer) * quarter, 16)
            block = flipped[(2 * outer + core) * quarter : (2 * outer + core + 1) * quarter, :]
            turned[pl.ds(start, quarter), :] = block


def split_store(values, kept_ref, sent_ref):
    quarter = values.shape[0] // 4
    low = values.astype(jnp.bfloat16)
    for outer in range(2):
        sent_ref[outer] = low[outer * quarter : (outer + 1) * quarter, :]
        kept_ref[outer] = low[(2 + outer) * quarter : (3 + outer) * quarter, :]


def gate_kernel(place_ref, n2_ref, weight, cot_ref, act_ref, by_gate_ref, by_up_ref, kept_ref, sent_ref):
    rows, width = n2_ref.shape
    hidden = weight.shape[-1] // 2
    start = pl.multiple_of(pl.program_id(0) * tile, 128)
    gate_weight = weight[..., pl.ds(start, tile)].reshape(width, tile)
    up_weight = weight[..., pl.ds(hidden + start, tile)].reshape(width, tile)

    def finish(places, gate, up):
        square = gate * gate
        bent = slope + (slope * curve) * square
        halved = 0.5 + 0.5 * jnp.tanh(gate * bent)
        value = gate * halved
        steep = halved + gate * (6.0 * bent - 4.0 * slope) * (halved - halved * halved)
        act_ref[places, :] = (value * up).astype(jnp.bfloat16)
        by_gate_ref[places, :] = up * steep
        by_up_ref[places, :] = value

    held = None
    for start in range(0, rows, 128):
        places = slice(start, start + 128)
        gate = dot_nn(n2_ref[places, :], gate_weight)
        up = dot_nn(n2_ref[places, :], up_weight)
        if held is not None:
            finish(*held)
        held = (places, gate, up)
    finish(*held)
    grad = dot_tn(act_ref[...], cot_ref[...]).astype(jnp.bfloat16)
    core = pl.program_id(0) % 2

    @pl.when(core == place_ref[1])
    def _():
        kept_ref[0] = grad

    @pl.when(core != place_ref[1])
    def _():
        sent_ref[0] = grad


def gate_forward(place, pieces, normed_two, cot_low):
    rows, width = normed_two.shape
    columns = pieces[0].shape[-1]
    hidden = columns // 2
    number = len(pieces)
    whole = pl.BlockSpec((rows, width), lambda step: (0, 0))
    column = pl.BlockSpec((rows, tile), lambda step: (0, step))
    half = pl.BlockSpec((1, tile, width), lambda step: (step // 2, 0, 0))
    assert hidden == 4 * tile

    def kernel(place_ref, *refs):
        n2_ref, cot_ref, *outs, full_ref, held, sems = refs[number:]
        filled(
            place_ref, refs[:number], full_ref, held, sems,
            lambda: gate_kernel(place_ref, n2_ref, held, cot_ref, *outs),
        )

    *results, full = pl.pallas_call(
        kernel,
        grid=(hidden // tile,),
        out_shape=(
            pltpu.HBM((rows, hidden), jnp.bfloat16),
            pltpu.HBM((rows, hidden), jnp.float32),
            pltpu.HBM((rows, hidden), jnp.float32),
            jax.ShapeDtypeStruct((2, tile, width), jnp.bfloat16),
            jax.ShapeDtypeStruct((2, tile, width), jnp.bfloat16),
            pltpu.HBM(slab(columns, width), jnp.bfloat16),
        ),
        in_specs=[scalars()] + [anywhere] * number + [whole, whole],
        out_specs=(column, column, column, half, half, anywhere),
        scratch_shapes=[
            pltpu.VMEM(slab(columns, width), jnp.bfloat16),
            pltpu.SemaphoreType.DMA((9,)),
        ],
        compiler_params=pltpu.CompilerParams(vmem_limit_bytes=34 * 2**20),
        cost_estimate=pl.CostEstimate(
            flops=6 * rows * width * hidden,
            bytes_accessed=rows * hidden * 10 + 8 * width * hidden,
            transcendentals=rows * hidden,
        ),
        name="gate_forward",
    )(place, *pieces, normed_two, *in_hbm(cot_low))
    return (*results, full.reshape(width, columns))


def gate_back_kernel(
    place_ref, n2_ref, cot_ref, ff, by_gate_ref, by_up_ref, out_ref, kept_ref, sent_ref, turned
):
    step = pl.program_id(0)
    weight = ff[step // 2, step % 2].reshape(tile, ff.shape[-1])
    incoming = dot_nt(cot_ref[...], weight)
    by_gate = (incoming * by_gate_ref[...]).astype(jnp.bfloat16)
    by_up = (incoming * by_up_ref[...]).astype(jnp.bfloat16)
    out_ref[0] = by_gate
    out_ref[1] = by_up
    split_store(dot_nn(turned[...], by_gate), kept_ref.at[:, :, :tile], sent_ref.at[:, :, :tile])
    split_store(dot_nn(turned[...], by_up), kept_ref.at[:, :, tile:], sent_ref.at[:, :, tile:])


def gate_back(place, pieces, normed_two, cot_low, by_gate, by_up):
    rows, width = normed_two.shape
    hidden = by_gate.shape[1]
    number = len(pieces)
    whole = pl.BlockSpec((rows, width), lambda step: (0, 0))
    column = pl.BlockSpec((rows, tile), lambda step: (0, step))
    half = pl.BlockSpec((2, width // 4, 2 * tile), lambda step: (0, 0, step))

    def kernel(place_ref, *refs):
        n2_ref, cot_ref, gate_ref, up_ref, *outs, full_ref, held, turned, sems = refs[number:]
        filled(
            place_ref, refs[:number], full_ref, held, sems,
            lambda: gate_back_kernel(
                place_ref, n2_ref, cot_ref, held, gate_ref, up_ref, *outs, turned
            ),
            lambda: turned_rows(place_ref, n2_ref, turned), True,
        )

    *results, full = pl.pallas_call(
        kernel,
        grid=(hidden // tile,),
        out_shape=(
            pltpu.HBM((2, rows, hidden), jnp.bfloat16),
            jax.ShapeDtypeStruct((2, width // 4, 2 * hidden), jnp.bfloat16),
            jax.ShapeDtypeStruct((2, width // 4, 2 * hidden), jnp.bfloat16),
            pltpu.HBM(slab(width, hidden), jnp.bfloat16),
        ),
        in_specs=[scalars()] + [anywhere] * number + [whole, whole, column, column],
        out_specs=(
            pl.BlockSpec((2, rows, tile), lambda step: (0, 0, step)),
            half,
            half,
            anywhere,
        ),
        scratch_shapes=[
            pltpu.VMEM(slab(width, hidden), jnp.bfloat16),
            pltpu.VMEM((width, rows), jnp.bfloat16),
            pltpu.SemaphoreType.DMA((9,)),
        ],
        compiler_params=pltpu.CompilerParams(vmem_limit_bytes=38 * 2**20),
        cost_estimate=pl.CostEstimate(
            flops=6 * rows * width * hidden,
            bytes_accessed=rows * hidden * 12 + 8 * width * hidden,
            transcendentals=0,
        ),
        name="gate_back",
    )(place, *pieces, *in_hbm(normed_two, cot_low, by_gate, by_up))
    return (*results, full.reshape(hidden, width))


def norm_back(grads, values, gain, residual):
    spread = lax.rsqrt(jnp.mean(values * values, axis=-1, keepdims=True) + epsilon)
    scaled = grads * gain
    inner = jnp.mean(scaled * values, axis=-1, keepdims=True)
    gain_grad = jnp.sum(grads * (values * spread), axis=0, keepdims=True)
    return residual + spread * scaled - values * (spread * spread * spread * inner), gain_grad


def middle_back_kernel(
    gates_hbm, weight_hbm, out_weight_hbm, middle_hbm, cot_hbm, gain_ref,
    grad_hbm, low_hbm, mixed_hbm, gain_grad_ref,
    gates, weight, out_weight, middle, cot, total, low, mixed, sems,
):
    rows, width = total.shape
    hidden = gates.shape[2]
    wide = hidden // 2
    arrivals = []

    def bring(source, target):
        copy = pltpu.make_async_copy(source, target, sems.at[len(arrivals)])
        copy.start()
        arrivals.append(copy)

    for part in range(4):
        columns = pl.ds(part % 2 * wide, wide)
        bring(gates_hbm.at[part // 2, :, columns], gates.at[part // 2, :, columns])
        columns = pl.ds(part * wide, wide)
        bring(weight_hbm.at[:, columns], weight.at[:, columns])
    bring(middle_hbm, middle)
    bring(cot_hbm, cot)
    bring(out_weight_hbm.at[:, pl.ds(3 * width, width)], out_weight)
    for part in range(4):
        arrivals[2 * part].wait()
        arrivals[2 * part + 1].wait()
        columns = slice(part % 2 * wide, part % 2 * wide + wide)
        product = dot_nt(
            gates[part // 2, :, columns], weight[:, part * wide : part * wide + wide]
        )
        if part == 0:
            total[...] = product
        else:
            total[...] += product
    for copy in arrivals[8:]:
        copy.wait()
    leaving = []
    for half in range(2):
        places = slice(half * rows // 2, (half + 1) * rows // 2)
        grad, gain_grad = norm_back(
            total[places, :], middle[places, :], gain_ref[...], cot[places, :]
        )
        total[places, :] = grad
        low[places, :] = grad.astype(jnp.bfloat16)
        if half == 0:
            gain_grad_ref[...] = gain_grad
        else:
            gain_grad_ref[...] += gain_grad
        mixed[places, :] = dot_nt(low[places, :], out_weight[...]).astype(jnp.bfloat16)
        places = pl.ds(half * rows // 2, rows // 2)
        for source, target in ((total, grad_hbm), (low, low_hbm), (mixed, mixed_hbm)):
            copy = pltpu.make_async_copy(
                source.at[places], target.at[places], sems.at[len(arrivals) + len(leaving)]
            )
            copy.start()
            leaving.append(copy)
    for copy in leaving:
        copy.wait()


def middle_back(gates, full_in, middle, cotangent, gain, full_attention):
    rows, width = middle.shape
    hidden = gates.shape[2]
    low = jnp.bfloat16
    line = pl.BlockSpec(memory_space=pltpu.VMEM)
    return pl.pallas_call(
        middle_back_kernel,
        out_shape=(
            pltpu.HBM((rows, width), jnp.float32),
            pltpu.HBM((rows, width), low),
            pltpu.HBM((rows, width), low),
            jax.ShapeDtypeStruct((1, width), jnp.float32),
        ),
        in_specs=[anywhere] * 5 + [line],
        out_specs=(anywhere, anywhere, anywhere, line),
        scratch_shapes=[
            pltpu.VMEM((2, rows, hidden), low),
            pltpu.VMEM((width, 2 * hidden), low),
            pltpu.VMEM((width, width), low),
            pltpu.VMEM((rows, width), jnp.float32),
            pltpu.VMEM((rows, width), jnp.float32),
            pltpu.VMEM((rows, width), jnp.float32),
            pltpu.VMEM((rows, width), low),
            pltpu.VMEM((rows, width), low),
            pltpu.SemaphoreType.DMA((17,)),
        ],
        compiler_params=pltpu.CompilerParams(vmem_limit_bytes=46 * 2**20),
        cost_estimate=pl.CostEstimate(
            flops=4 * rows * width * hidden + 2 * rows * width * width,
            bytes_accessed=rows * hidden * 4 + 4 * width * hidden + 18 * rows * width,
            transcendentals=0,
        ),
        name="middle_back",
    )(*in_hbm(gates, full_in, full_attention, middle, cotangent), gain.reshape(1, -1))


def scalars():
    return pl.BlockSpec(memory_space=pltpu.SMEM)


def by_parts(name, first, second, kinds, body, *extra):
    width = first.shape[1]
    rows = first.shape[0] + second.shape[0]
    starts = first.shape[0] // count

    def kernel(first_ref, second_ref, *refs):
        @pl.when(pl.program_id(0) < starts)
        def _():
            body(first_ref, *refs)

        @pl.when(pl.program_id(0) >= starts)
        def _():
            body(second_ref, *refs)

    return pl.pallas_call(
        kernel,
        grid=(rows // count,),
        out_shape=[pltpu.HBM((rows, width), kind) for kind in kinds],
        in_specs=[
            pl.BlockSpec((count, width), lambda step: (jnp.minimum(step, starts - 1), 0)),
            pl.BlockSpec((count, width), lambda step: (jnp.maximum(step - starts, 0), 0)),
        ]
        + [pl.BlockSpec(line.shape, lambda step: (0, 0)) for line in extra],
        out_specs=[pl.BlockSpec((count, width), lambda step: (step, 0))] * len(kinds),
        compiler_params=pltpu.CompilerParams(vmem_limit_bytes=20 * 2**20),
        cost_estimate=pl.CostEstimate(
            flops=4 * rows * width, bytes_accessed=10 * rows * width, transcendentals=rows
        ),
        name=name,
    )(*in_hbm(first, second), *extra)


def norm_body(rows_ref, gain_ref, values_ref, normed_ref):
    values = rows_ref[...]
    spread = lax.rsqrt(jnp.mean(values * values, axis=-1, keepdims=True) + epsilon)
    values_ref[...] = values
    normed_ref[...] = (values * spread * gain_ref[...]).astype(jnp.bfloat16)


def round_body(rows_ref, values_ref, low_ref):
    values_ref[...] = rows_ref[...]
    low_ref[...] = rows_ref[...].astype(jnp.bfloat16)


def project(place, pieces, normed):
    rows, width = normed.shape
    columns = pieces[0].shape[-1]
    number = len(pieces)

    def kernel(place_ref, *refs):
        normed_ref, out_ref, full_ref, held, sems = refs[number:]

        def body():
            start = pl.multiple_of(pl.program_id(0) * width, 128)
            weight = held[..., pl.ds(start, width)].reshape(width, width)
            out_ref[...] = dot_nn(normed_ref[...], weight).astype(jnp.bfloat16)

        filled(place_ref, refs[:number], full_ref, held, sems, body)

    projected, full = pl.pallas_call(
        kernel,
        grid=(3,),
        out_shape=(
            pltpu.HBM((rows, 3 * width), jnp.bfloat16),
            pltpu.HBM(slab(columns, width), jnp.bfloat16),
        ),
        in_specs=[scalars()]
        + [anywhere] * number
        + [pl.BlockSpec((rows, width), lambda step: (0, 0))],
        out_specs=(pl.BlockSpec((rows, width), lambda step: (0, step)), anywhere),
        scratch_shapes=[
            pltpu.VMEM(slab(columns, width), jnp.bfloat16),
            pltpu.SemaphoreType.DMA((9,)),
        ],
        compiler_params=pltpu.CompilerParams(vmem_limit_bytes=14 * 2**20),
        cost_estimate=pl.CostEstimate(
            flops=6 * rows * width * width,
            bytes_accessed=8 * rows * width + 4 * columns * width,
            transcendentals=0,
        ),
        name="project",
    )(place, *pieces, normed)
    return projected, full.reshape(width, columns)


def middle_kernel(rows_ref, mixed_ref, weight_ref, gain_ref, middle_ref, normed_ref):
    middle = rows_ref[...] + dot_nn(mixed_ref[...], weight_ref[...])
    spread = lax.rsqrt(jnp.mean(middle * middle, axis=-1, keepdims=True) + epsilon)
    middle_ref[...] = middle
    normed_ref[...] = (middle * spread * gain_ref[...]).astype(jnp.bfloat16)


def middle_forward(values, mixed, full_attention, gain, *earlier):
    rows, width = values.shape
    part = rows // 2
    block = pl.BlockSpec((part, width), lambda step: (step, 0))

    def kernel(*refs):
        middle_kernel(*refs[:4], *refs[4 + len(earlier) :])

    return pl.pallas_call(
        kernel,
        grid=(2,),
        out_shape=(
            pltpu.HBM((rows, width), jnp.float32),
            jax.ShapeDtypeStruct((rows, width), jnp.bfloat16),
        ),
        in_specs=[
            block,
            block,
            pl.BlockSpec((width, width), lambda step: (0, 3)),
            pl.BlockSpec((1, width), lambda step: (0, 0)),
        ]
        + [anywhere] * len(earlier),
        out_specs=(block, block),
        compiler_params=pltpu.CompilerParams(vmem_limit_bytes=15 * 2**20),
        cost_estimate=pl.CostEstimate(
            flops=2 * rows * width * width,
            bytes_accessed=12 * rows * width + 2 * width * width,
            transcendentals=0,
        ),
        name="middle_forward",
    )(*in_hbm(values), mixed, *in_hbm(full_attention), gain.reshape(1, -1), *earlier)


def attention_grads_kernel(
    place_ref, normed_ref, grads_ref, mixed_hbm, low_hbm, weight_0, weight_1, weight_2, weight_3,
    gain_ref, ffn_ref, table_ref, kept_ref, sent_ref, small_ref,
    turned, column, ordered, mixed_ref, low_ref, sems,
):
    step = pl.program_id(0)
    last = pl.num_programs(0) - 1
    quarter = column.shape[0] // 4
    copies = [
        pltpu.make_async_copy(mixed_hbm, mixed_ref, sems.at[0]),
        pltpu.make_async_copy(low_hbm, low_ref, sems.at[1]),
    ]

    @pl.when(step == 0)
    def _():
        for copy in copies:
            copy.start()
        turned_rows(place_ref, normed_ref, turned)
        column[...] = jnp.zeros_like(column)

    @pl.when(step < last)
    def _():
        grads = dot_nn(turned[...], grads_ref[0])
        split_store(grads, kept_ref, sent_ref)
        for number, weight in enumerate((weight_0, weight_1, weight_2, weight_3)):
            rows = slice(number * quarter, (number + 1) * quarter)
            product = grads[rows, :] * weight[...].astype(jnp.float32)
            parts = [product[:, lane : lane + 128] for lane in range(0, grads.shape[1], 128)]
            column[rows, :] += sum(parts)

    @pl.when(step == last)
    def _():
        for copy in copies:
            copy.wait()
        turned_rows(place_ref, mixed_ref, turned)
        split_store(dot_nn(turned[...], low_ref[...]), kept_ref, sent_ref)
        for number in range(4):
            row = quarter_owner(number, place_ref[1])
            start = pl.multiple_of(row * quarter, 16)
            ordered[pl.ds(start, quarter), :] = column[number * quarter : (number + 1) * quarter, :]
        gain_grad = jnp.sum(ordered[...].T, axis=0, keepdims=True) / gain_ref[...]
        small_ref[...] = jnp.zeros_like(small_ref)
        lines = gain_grad.shape[1] // 128
        for number, line in enumerate((gain_grad, ffn_ref[...])):
            for part in range(lines):
                row = number * lines + part
                small_ref[row : row + 1, :] = line[:, part * 128 : (part + 1) * 128]
        table = table_ref[...].reshape(-1, table_ref.shape[2])
        small_ref[2 * lines :, : table.shape[1]] = table


def quarter_owner(number, core):
    return 2 * (number % 2) + (core if number >= 2 else 1 - core)


def attention_grads(
    place, normed, grad_projected, mixed, grad_low, full_attention, gain, ffn_grad, table
):
    rows, width = normed.shape
    lines = 2 * (width // 128) + 2 * table.shape[0]

    def fixed(step, where):
        return 0, 0

    def column(step, where):
        return 0, 0, step

    def weight_spec(number):
        return pl.BlockSpec(
            (width // 4, width),
            lambda step, where: (quarter_owner(number, where[1]), jnp.minimum(step, 2)),
        )

    shape = jax.ShapeDtypeStruct((2, width // 4, 4 * width), jnp.bfloat16)
    half = pl.BlockSpec((2, width // 4, width), column)
    return pl.pallas_call(
        attention_grads_kernel,
        grid_spec=pltpu.PrefetchScalarGridSpec(
            num_scalar_prefetch=1,
            grid=(4,),
            in_specs=[
                pl.BlockSpec((rows, width), fixed),
                pl.BlockSpec((1, rows, width), lambda step, where: (jnp.minimum(step, 2), 0, 0)),
                anywhere,
                anywhere,
                *[weight_spec(number) for number in range(4)],
                pl.BlockSpec((1, width), fixed),
                pl.BlockSpec((1, width), fixed),
                pl.BlockSpec(table.shape, lambda step, where: (0, 0, 0)),
            ],
            out_specs=(half, half, pl.BlockSpec((lines, 128), fixed)),
            scratch_shapes=[
                pltpu.VMEM((width, rows), jnp.bfloat16),
                pltpu.VMEM((width, 128), jnp.float32),
                pltpu.VMEM((width, 128), jnp.float32),
                pltpu.VMEM((rows, width), jnp.bfloat16),
                pltpu.VMEM((rows, width), jnp.bfloat16),
                pltpu.SemaphoreType.DMA((2,)),
            ],
        ),
        out_shape=(shape, shape, jax.ShapeDtypeStruct((lines, 128), jnp.float32)),
        compiler_params=pltpu.CompilerParams(vmem_limit_bytes=36 * 2**20),
        cost_estimate=pl.CostEstimate(
            flops=8 * rows * width * width,
            bytes_accessed=12 * rows * width + 14 * width * width,
            transcendentals=0,
        ),
        name="attention_grads",
    )(
        place,
        *in_hbm(normed),
        grad_projected,
        *in_hbm(mixed, grad_low, *[full_attention] * 4),
        gain.reshape(1, -1),
        ffn_grad,
        table,
    )


def input_back(grad_projected, full_qkv, values, residual, gain, doc_rows):
    rows, width = values.shape
    part = rows // row_parts
    block = pl.BlockSpec((part, width), lambda step: (step, 0))

    def kernel(
        grads_ref, weight_ref, rows_ref, residual_ref, gain_ref,
        doc_ref, query_ref, slots, sems,
    ):
        step = pl.program_id(0)
        total = dot_nt(grads_ref[0], weight_ref[:, :width])
        for third in (1, 2):
            columns = slice(third * width, (third + 1) * width)
            total = total + dot_nt(grads_ref[third], weight_ref[:, columns])
        slots[step], _ = norm_back(total, rows_ref[...], gain_ref[...], residual_ref[...])
        emit(slots, (doc_ref, query_ref), sems)

    return pl.pallas_call(
        kernel,
        grid=(row_parts,),
        out_shape=(
            jax.ShapeDtypeStruct((doc_rows, width), jnp.float32),
            jax.ShapeDtypeStruct((rows - doc_rows, width), jnp.float32),
        ),
        in_specs=[
            pl.BlockSpec((3, part, width), lambda step: (0, step, 0)),
            pl.BlockSpec((width, 3 * width), lambda step: (0, 0)),
            block,
            block,
            pl.BlockSpec((1, width), lambda step: (0, 0)),
        ],
        out_specs=(anywhere, anywhere),
        scratch_shapes=[
            pltpu.VMEM((row_parts, part, width), jnp.float32),
            pltpu.SemaphoreType.DMA((row_parts + 1,)),
        ],
        compiler_params=pltpu.CompilerParams(vmem_limit_bytes=30 * 2**20),
        cost_estimate=pl.CostEstimate(
            flops=6 * rows * width * width,
            bytes_accessed=18 * rows * width + 6 * width * width,
            transcendentals=0,
        ),
        name="input_back",
    )(grad_projected, *in_hbm(full_qkv, values, residual), gain.reshape(1, -1))


def layer_outputs(middle, activated, full_ff, doc_rows):
    rows, width = middle.shape
    hidden = activated.shape[1]
    part = rows // row_parts

    def kernel(middle_ref, act_ref, weight_ref, doc_ref, query_ref, slots, sems):
        slots[pl.program_id(0)] = middle_ref[...] + dot_nn(act_ref[...], weight_ref[...])
        emit(slots, (doc_ref, query_ref), sems)

    return pl.pallas_call(
        kernel,
        grid=(row_parts,),
        out_shape=(
            jax.ShapeDtypeStruct((doc_rows, width), jnp.float32),
            jax.ShapeDtypeStruct((rows - doc_rows, width), jnp.float32),
        ),
        in_specs=[
            pl.BlockSpec((part, width), lambda step: (step, 0)),
            pl.BlockSpec((part, hidden), lambda step: (step, 0)),
            pl.BlockSpec((hidden, width), lambda step: (0, 0)),
        ],
        out_specs=(anywhere, anywhere),
        scratch_shapes=[
            pltpu.VMEM((row_parts, part, width), jnp.float32),
            pltpu.SemaphoreType.DMA((row_parts + 1,)),
        ],
        compiler_params=pltpu.CompilerParams(vmem_limit_bytes=24 * 2**20),
        cost_estimate=pl.CostEstimate(
            flops=2 * rows * width * hidden,
            bytes_accessed=8 * rows * width + 2 * hidden * (rows + width),
            transcendentals=0,
        ),
        name="layer_outputs",
    )(*in_hbm(middle, activated, full_ff))


def body(
    doc_inputs,
    query_inputs,
    doc_mask,
    query_lengths,
    doc_cotangent,
    query_cotangent,
    qkv_weight,
    out_weight,
    in_weight,
    ff_weight,
    attn_gain,
    ffn_gain,
    bias_table,
):
    doc_count, doc_length, model_width = doc_inputs.shape
    group_count, group_length = (query_inputs.shape[0], query_inputs.shape[1])
    head_count = bias_table.shape[1]
    doc_rows = doc_count * doc_length
    low = jnp.bfloat16
    routed = hand_routed()
    place = own_place() if routed else (0, 0, 0, 0)
    place_vector = jnp.stack([jnp.asarray(index, jnp.int32) for index in place])

    attention_shard = jnp.concatenate([qkv_weight, out_weight], axis=1).astype(low)
    in_shard = in_weight.astype(low)
    ff_shard = ff_weight.astype(low)

    kinds = (jnp.float32, low)
    values, normed = by_parts(
        "norm_rows",
        doc_inputs.reshape(doc_rows, model_width),
        query_inputs.reshape(-1, model_width),
        kinds,
        norm_body,
        attn_gain.reshape(1, -1),
    )
    cotangent_parts = (
        doc_cotangent.reshape(doc_rows, model_width),
        query_cotangent.reshape(-1, model_width),
    )
    places = jnp.arange(group_length, dtype=jnp.int32)
    query_mask = places[None, :] < query_lengths[:, None]
    onehot = lines_onehot(bias_table.shape[0])
    lines = jnp.einsum("pn,nh->hp", onehot, bias_table, precision=highest)
    lines = lines.reshape(head_count // 2, 2, 4 * count)
    doc_masking = jnp.where(doc_mask > 0, 0.0, -1e9).astype(jnp.float32)
    query_masking = jnp.where(query_mask, 0.0, -1e9).astype(jnp.float32)
    query_masking = query_masking.reshape(-1, 1, count)

    if routed:
        column_a = gather_column(attention_shard)
        row_f = jnp.stack(in_order(ff_shard, swap(ff_shard, dx=1), place[3]))
        column_a, row_f, normed, lines, doc_masking, query_masking, in_shard, cotangent_parts = (
            together(
                column_a, row_f, normed, lines, doc_masking, query_masking, in_shard,
                cotangent_parts,
            )
        )
        plane_a = gather_plane(place, attention_shard, column_a)
        cotangent, cot_low = by_parts("round_rows", *cotangent_parts, kinds, round_body)
        plane_a, cotangent, cot_low = together(plane_a, cotangent, cot_low)
        near_a = gather_near(place, *plane_a)
        column_i = gather_column(in_shard)
        far_a = gather_far(*near_a)
        plane_f = jnp.stack(in_order(row_f, swap(row_f, dy=1), place[0]))
        column_i, far_a, plane_f = together(column_i, far_a, plane_f)
        pieces = gather_order(near_a, far_a, gather_core(*near_a), gather_core(*far_a))
        plane_i = gather_plane(place, in_shard, column_i)
    else:
        cotangent, cot_low = by_parts("round_rows", *cotangent_parts, kinds, round_body)
        pieces = (split_rows(lax.all_gather(attention_shard, both, axis=0, tiled=True)),)
    projected, full_attention = project(place_vector, pieces, normed)
    if routed:
        plane_i, projected = together(plane_i, projected)
        near_i = gather_near(place, *plane_i)
        far_i = gather_far(*near_i)
        second_f = swap(plane_f, dz=2)
    mixed, doc_probs, query_probs = attend(
        projected, lines, doc_masking, query_masking, group_length
    )
    if routed:
        mixed, far_i, second_f = together(mixed, far_i, second_f)
        others_f = gather_others(plane_f, second_f)
        pieces = gather_order(near_i, far_i, gather_core(*near_i), gather_core(*far_i))
    else:
        pieces = (split_rows(lax.all_gather(in_shard, both, axis=0, tiled=True)),)
    middle, normed_two = middle_forward(values, mixed, full_attention, ffn_gain)
    if routed:
        pieces, normed_two = together(pieces, normed_two)
        core_f = gather_core(plane_f, second_f)
    activated, by_gate, by_up, kept, sent, full_in = gate_forward(
        place_vector, pieces, normed_two, cot_low
    )
    if routed:
        others_f, core_f, by_gate, kept, sent = together(others_f, core_f, by_gate, kept, sent)
        core_others = gather_core(*others_f)
        pieces = (plane_f, others_f[0], second_f, others_f[1])
        pieces += (core_f[0], core_others[0], core_f[1], core_others[1])
        ff_grads = NarrowScatter(kept, sent, place_vector)
        got_f = ff_grads.core()
        pieces, got_f = together(pieces, got_f)
        near_f = ff_grads.plane(got_f)
    else:
        pieces = (split_rows(lax.all_gather(ff_shard, both, axis=0, tiled=True)),)
        grad_ff = joined_halves(kept, sent)
    gates, kept, sent, full_ff = gate_back(
        place_vector, pieces, normed_two, cot_low, by_gate, by_up
    )
    if routed:
        gates, kept, sent, near_f = together(gates, kept, sent, near_f)
        in_grads = Scatter(kept, sent, place_vector, pinned=False)
        far_f = ff_grads.far(ff_grads.far_sums(got_f, near_f))
        got_i = in_grads.core()
    else:
        grad_in = joined_halves(kept, sent)
    grad_middle, grad_middle_low, grad_mixed, grad_ffn_gain = middle_back(
        gates, full_in, middle, cotangent, ffn_gain, full_attention
    )
    if routed:
        grad_mixed, far_f, got_i = together(grad_mixed, far_f, got_i)
        near_i = in_grads.plane(got_i)
        shares_f = ff_grads.column(ff_grads.column_sums(got_f, near_f, far_f))
    grad_projected, grad_table = attend_back(
        projected, grad_mixed, doc_probs, query_probs, onehot, doc_length
    )
    if routed:
        grad_projected, grad_table, shares_f, near_i = together(
            grad_projected, grad_table, shares_f, near_i
        )
        far_i = in_grads.far(got_i, near_i)
    kept, sent, small = attention_grads(
        place_vector, normed, grad_projected, mixed, grad_middle_low, full_attention, attn_gain,
        grad_ffn_gain, grad_table,
    )
    if routed:
        kept, sent, far_i, small, grad_projected, shares_f, activated = together(
            kept, sent, far_i, small, grad_projected, shares_f, activated
        )
        attention = Scatter(kept, sent, place_vector, pinned=False)
        got_a = attention.core()
        small = add_flipped(small, {"dc": 1})
        sums_i = in_grads.column_sums(got_i, near_i, far_i)
        got_a, sums_i, small, grad_projected, shares_f, activated = together(
            got_a, sums_i, small, grad_projected, shares_f, activated
        )
        near_a = attention.plane(got_a)
        shares_i = in_grads.column(sums_i)
        small = add_flipped(small, {"dz": 1})
    grad_inputs = input_back(
        grad_projected, full_attention, values, grad_middle, attn_gain, doc_rows
    )
    if routed:
        near_a, grad_inputs, small, shares_f, shares_i, activated = together(
            near_a, grad_inputs, small, shares_f, shares_i, activated
        )
        far_a = attention.far(got_a, near_a)
        small = add_flipped(small, {"dz": 2})
        far_a, small, shares_f, shares_i, activated = together(
            far_a, small, shares_f, shares_i, activated
        )
        sums_a = attention.column_sums(got_a, near_a, far_a)
        sums_a, small, shares_f, shares_i, activated = together(
            sums_a, small, shares_f, shares_i, activated
        )
        shares_a = attention.column(sums_a)
        small = add_flipped(small, {"dx": 1}, {"dy": 1})
    outputs = layer_outputs(middle, activated, full_ff, doc_rows)
    if routed:
        ff_grad_shard = summed(*shares_f)
        in_grad_shard = summed(*shares_i)
        grad_qkv = summed(*[share[:, : 3 * model_width] for share in shares_a])
        grad_out = summed(*[share[:, 3 * model_width :] for share in shares_a])
    else:
        scatter = functools.partial(
            lax.psum_scatter, axis_name=both, scatter_dimension=0, tiled=True
        )
        ff_grad_shard = scatter(grad_ff)
        in_grad_shard = scatter(grad_in)
        grad_attention = scatter(joined_halves(kept, sent))
        grad_qkv = grad_attention[:, : 3 * model_width]
        grad_out = grad_attention[:, 3 * model_width :]
        small = lax.psum(small, both)
    width_lines = model_width // 128
    in_grad_shard = in_grad_shard.reshape(in_weight.shape[0], -1, 2, tile)
    in_grad_shard = jnp.swapaxes(in_grad_shard, 1, 2).reshape(in_weight.shape)
    return (
        outputs[0].reshape(doc_inputs.shape),
        outputs[1].reshape(query_inputs.shape),
        grad_inputs[0].reshape(doc_inputs.shape),
        grad_inputs[1].reshape(query_inputs.shape),
        grad_qkv,
        grad_out,
        in_grad_shard,
        ff_grad_shard,
        small[:width_lines].reshape(model_width),
        small[width_lines : 2 * width_lines].reshape(model_width),
        small[2 * width_lines :, : bias_table.shape[0]].T,
    )


def solution(mesh):
    placed = (
        P(("dp", "fsdp"), None, None),
        P(("dp", "fsdp"), None, None),
        P(("dp", "fsdp"), None),
        P(("dp", "fsdp")),
        P(("dp", "fsdp"), None, None),
        P(("dp", "fsdp"), None, None),
        P(("dp", "fsdp"), None),
        P(("dp", "fsdp"), None),
        P(("dp", "fsdp"), None),
        P(("dp", "fsdp"), None),
        P(),
        P(),
        P(),
    )
    return jax.shard_map(
        body,
        mesh=mesh,
        in_specs=placed,
        out_specs=(
            P(("dp", "fsdp"), None, None),
            P(("dp", "fsdp"), None, None),
            P(("dp", "fsdp"), None, None),
            P(("dp", "fsdp"), None, None),
            P(("dp", "fsdp"), None),
            P(("dp", "fsdp"), None),
            P(("dp", "fsdp"), None),
            P(("dp", "fsdp"), None),
            P(),
            P(),
            P(),
        ),
        check_vma=False,
    )
```

```python
import functools
import math

import jax
import jax.numpy as jnp
from jax import lax
from jax.experimental import pallas as pl
from jax.experimental.pallas import tpu as pltpu
from jax.sharding import PartitionSpec as P

both = ("dp", "fsdp")
epsilon = 1e-06
highest = lax.Precision.HIGHEST
anywhere = pl.BlockSpec(memory_space=pl.ANY)


def place_index(y, c, z, x):
    return ((y * 2 + c) * 4 + z) * 2 + x


def flip_pairs(dy=0, dc=0, dz=0, dx=0):
    pairs = []
    for y in range(2):
        for c in range(2):
            for z in range(4):
                for x in range(2):
                    pairs.append(
                        (place_index(y, c, z, x), place_index(y ^ dy, c ^ dc, z ^ dz, x ^ dx))
                    )
    return pairs


def swap(values, **flips):
    return lax.ppermute(values, both, flip_pairs(**flips))


def hand_routed():
    return (lax.axis_size("dp"), lax.axis_size("fsdp")) == (4, 8)


def own_place():
    outer = lax.axis_index("dp")
    inner = lax.axis_index("fsdp")
    return outer // 2, outer % 2, inner // 2, inner % 2


def after(values, *earlier):
    return lax.optimization_barrier((values, *earlier))[0]


def in_hbm(*values):
    return [pltpu.with_memory_space_constraint(value, pltpu.HBM) for value in values]


def together(*values):
    return lax.optimization_barrier(values)


def fill_copies(place_ref, pieces, target, sems, by_column):
    if len(pieces) == 1:
        return [pltpu.make_async_copy(pieces[0], target, sems.at[0])]
    y, c, z, x = place_ref[0], place_ref[1], place_ref[2], place_ref[3]
    copies = []
    even = z - z % 2
    for number, piece in enumerate(pieces):
        core = c ^ (number // 4)
        kind = number % 4
        if by_column:
            where = target.at[:, core, z ^ kind]
        elif kind < 2:
            where = target.at[y ^ kind, core, pl.ds(even, 2)]
        else:
            where = target.at[:, core, pl.ds(even ^ 2, 2), x ^ (kind - 2)]
        copies.append(pltpu.make_async_copy(piece, where, sems.at[number]))
    return copies


def filled(place_ref, pieces, full_ref, held, sems, body, meanwhile=None, by_column=False):
    step = pl.program_id(0)
    kept = pltpu.make_async_copy(held, full_ref, sems.at[8])

    @pl.when(step == 0)
    def _():
        copies = fill_copies(place_ref, pieces, held, sems, by_column)
        for copy in copies:
            copy.start()
        if meanwhile is not None:
            meanwhile()
        for copy in copies:
            copy.wait()
        kept.start()

    body()

    @pl.when(step == pl.num_programs(0) - 1)
    def _():
        kept.wait()


def emit(slots, targets, sems):
    step, rows = pl.program_id(0), slots.shape[1]
    copies = []
    for number in range(slots.shape[0]):
        start = 0
        for target in targets:
            low = max(number * rows, start)
            high = min((number + 1) * rows, start + target.shape[0])
            if low < high:
                source = slots.at[number, pl.ds(low - number * rows, high - low)]
                where = target.at[pl.ds(low - start, high - low)]
                copy = pltpu.make_async_copy(source, where, sems.at[len(copies)])
                copies.append((number, copy))
            start += target.shape[0]
    for number in range(slots.shape[0]):

        @pl.when(step == number)
        def _():
            for owner, copy in copies:
                if owner == number:
                    copy.start()

    @pl.when(step == slots.shape[0] - 1)
    def _():
        for _, copy in copies:
            copy.wait()


def gather_order(near, far, core_near, core_far):
    return (near[0], far[0], near[1], far[1], core_near[0], core_far[0], core_near[1], core_far[1])


def slab(columns, rows):
    return (2, 2, 4, 2, rows // 32, columns)


def split_rows(full):
    return full.reshape(slab(full.shape[1], full.shape[0]))


def in_order(own, other, index):
    odd = index % 2 == 1
    return jnp.where(odd, other, own), jnp.where(odd, own, other)


def gather_column(shard):
    two, three, one = [swap(shard, dz=flip) for flip in (2, 3, 1)]
    return one, two, three


def gather_plane(place, shard, column):
    first = jnp.stack(in_order(shard, column[0], place[2]))
    second = jnp.stack(in_order(column[1], column[2], place[2]))
    return first, second, swap(first, dx=1), swap(second, dy=1)


def gather_near(place, first, second, first_near, second_near):
    even, odd = in_order(first, first_near, place[3])
    first = jnp.stack([even[0], odd[0], even[1], odd[1]]).reshape(2, 2, *first.shape[1:])
    second = jnp.stack(in_order(second, second_near, place[0]))
    return first, second


def gather_far(first, second):
    return swap(first, dy=1), swap(second, dx=1)


def gather_others(own, second):
    return swap(own, dz=1), swap(second, dz=1)


def gather_core(*pieces):
    return tuple(swap(piece, dc=1) for piece in pieces)


def summed(*terms):
    total = terms[0].astype(jnp.float32)
    for term in terms[1:]:
        total = total + term.astype(jnp.float32)
    return total


def joined_halves(kept, sent):
    return jnp.stack([kept, sent], axis=1).reshape(-1, kept.shape[2]).astype(jnp.float32)


def route(name, place, sources, targets, body, scratch=()):
    def spec(array, lead, pick):
        block = (*lead, *array.shape[-2:])
        return pl.BlockSpec(block, lambda step, where: (*pick(where), 0, 0))

    return pl.pallas_call(
        body,
        grid_spec=pltpu.PrefetchScalarGridSpec(
            num_scalar_prefetch=1,
            grid=(1,),
            in_specs=[spec(*source) for source in sources],
            out_specs=[spec(*target) for target in targets],
            scratch_shapes=scratch,
        ),
        out_shape=[target[0] for target in targets],
        compiler_params=pltpu.CompilerParams(vmem_limit_bytes=20 * 2**20),
        cost_estimate=pl.CostEstimate(
            flops=0,
            bytes_accessed=8 * len(sources) * math.prod(sources[0][0].shape[-2:]),
            transcendentals=0,
        ),
        name=name,
    )(place, *[source[0] for source in sources])


def whole_block(target):
    lead = target.shape[:-2]
    return target, lead, lambda where: (0,) * len(lead)


def store_sum(out_ref, *refs):
    blocks = math.prod(refs[0].shape[:-2])
    for number in range(blocks):
        terms = []
        for ref in (out_ref, *refs):
            index, rest = [], number
            for size in reversed(ref.shape[:-2]):
                index.insert(0, rest % size)
                rest //= size
            terms.append(ref.at[tuple(index)])
        terms[0][...] = summed(*[term[...] for term in terms[1:]]).astype(out_ref.dtype)


class Scatter:
    def __init__(self, kept, sent, place, pinned=True):
        self.place = place
        self.pinned = pinned
        self.block = (kept.shape[1] // 8, kept.shape[2])
        self.shape = (2, 4, 2, *self.block)
        self.kept = kept.reshape(self.shape)
        self.sent = sent

    def target(self, *lead, dtype=jnp.bfloat16):
        return jax.ShapeDtypeStruct((*lead, *self.block), dtype)

    def both(self, got, lead, pick):
        kept = in_hbm(self.kept)[0] if self.pinned else self.kept
        return [(kept, lead, pick), (got, lead, pick)]

    def core(self):
        return swap(self.sent, dc=1).reshape(self.shape)

    def plane(self, got):
        def body(place_ref, *refs):
            store_sum(refs[4], *refs[0:2])
            store_sum(refs[5], *refs[2:4])

        sources = self.both(got, (2, 2, 1), lambda where: (0, 0, 1 - where[3]))
        sources += self.both(got, (1, 2, 2), lambda where: (1 - where[0], 1, 0))
        target = whole_block(self.target(2, 2))
        one, two = route("plane", self.place, sources, [target, target], body)
        return swap(one, dx=1), swap(two, dy=1)

    def far(self, got, near):
        def body(place_ref, *refs):
            store_sum(refs[6], *refs[0:3])
            store_sum(refs[7], *refs[3:6])

        sources = [
            *self.both(got, (1, 2, 1), lambda where: (1 - where[0], 0, where[3])),
            (near[0], (1, 2), lambda where: (1 - where[0], 0)),
            *self.both(got, (1, 2, 1), lambda where: (where[0], 1, 1 - where[3])),
            (near[1], (2, 1), lambda where: (0, 1 - where[3])),
        ]
        target = whole_block(self.target(2))
        one, two = route("far", self.place, sources, [target, target], body)
        return swap(one, dy=1), swap(two, dx=1)

    def column_sources(self, near, far):
        return [
            (near[0], (1, 2), lambda where: (where[0], 0)),
            (far[0], (2,), lambda where: (0,)),
            (near[1], (2, 1), lambda where: (0, where[3])),
            (far[1], (2,), lambda where: (0,)),
        ]

    def column_terms(self, row, refs):
        if row < 2:
            return refs[0].at[0, row], refs[1].at[row]
        return refs[2].at[row - 2, 0], refs[3].at[row - 2]

    def column_sums(self, got, near, far):
        sources = self.both(got, (1, 4, 1), lambda where: (where[0], 0, where[3]))
        sources += self.column_sources(near, far)
        number = len(sources)

        def body(place_ref, *refs):
            *outs, total = refs[number:]
            for row in range(4):
                terms = (refs[0].at[0, row, 0], refs[1].at[0, row, 0])
                terms += self.column_terms(row, refs[2:number])
                total[row] = summed(*[term[...] for term in terms])
            for flip, out in enumerate(outs):
                out[...] = total[place_ref[2] ^ flip].astype(out.dtype)

        targets = [self.target(dtype=jnp.float32)] + [self.target()] * 3
        targets = [whole_block(target) for target in targets]
        scratch = [pltpu.VMEM((4, *self.block), jnp.float32)]
        return tuple(route("column", self.place, sources, targets, body, scratch))

    def column(self, sums):
        return sums[0], *[swap(share, dz=flip) for flip, share in zip((1, 2, 3), sums[1:])]


class NarrowScatter(Scatter):
    def both(self, got, lead, pick, pinned=False):
        kept, got = in_hbm(self.kept, got) if pinned else (self.kept, got)
        return [(kept, lead, pick), (got, lead, pick)]

    def plane(self, got):
        def body(place_ref, *refs):
            store_sum(refs[2], *refs[0:2])

        sources = self.both(got, (2, 4, 1), lambda where: (0, 0, 1 - where[3]), False)
        target = whole_block(self.target(2, 4))
        (sums,) = route("plane", self.place, sources, [target], body)
        return swap(sums, dx=1)

    def far_sums(self, got, near):
        def body(place_ref, *refs):
            store_sum(refs[3], *refs[0:3])

        sources = self.both(got, (1, 4, 1), lambda where: (1 - where[0], 0, where[3]))
        sources.append((near, (1, 4), lambda where: (1 - where[0], 0)))
        return route("far", self.place, sources, [whole_block(self.target(4))], body)[0]

    def far(self, sums):
        return swap(sums, dy=1)

    def column_sources(self, near, far):
        return [
            (near, (1, 4), lambda where: (where[0], 0)),
            (far, (4,), lambda where: (0,)),
        ]

    def column_terms(self, row, refs):
        return refs[0].at[0, row], refs[1].at[row]


def add_flipped(values, *steps):
    for flips in steps:
        values = values + swap(values, **flips)
    return values


count = 128


def relative_places():
    places = jnp.arange(4 * count, dtype=jnp.int32)
    return jnp.where(places < 3 * count, places - count, places - 5 * count)


def bucket_of(relative):
    distance = jnp.abs(relative)
    larger = jnp.zeros_like(distance)
    for threshold in (12, 16, 23, 32, 46, 64, 91):
        larger = larger + (distance >= threshold).astype(jnp.int32)
    bucket = jnp.where(distance < 8, distance, 8 + larger)
    return bucket + 16 * (relative > 0).astype(jnp.int32)


def lines_onehot(bucket_count):
    labels = jnp.arange(bucket_count, dtype=jnp.int32)
    return (bucket_of(relative_places())[:, None] == labels).astype(jnp.float32)


def own_lanes(head, shape):
    lanes = lax.broadcasted_iota(jnp.int32, shape, 1)
    return lanes < shape[1] // 2 if head == 0 else lanes >= shape[1] // 2


def keep_lanes(head, values):
    return jnp.where(own_lanes(head, values.shape), values, jnp.zeros_like(values))


def both_heads(values):
    return jnp.concatenate([keep_lanes(0, values), keep_lanes(1, values)], axis=0)


def joined(stacked):
    first, second = jnp.split(stacked, 2, axis=0)
    return jnp.where(own_lanes(0, first.shape), first, second).astype(jnp.bfloat16)


def softmax_rows(scores):
    raised = jnp.exp(scores - jnp.max(scores, axis=-1, keepdims=True))
    return raised * (1.0 / jnp.sum(raised, axis=-1, keepdims=True))


def dot_nt(left, right):
    return lax.dot_general(
        left, right, (((1,), (1,)), ((), ())), preferred_element_type=jnp.float32
    )


def dot_nn(left, right):
    return jnp.dot(left, right, preferred_element_type=jnp.float32)


def attend_kernel(
    docs, length, group, q_ref, k_ref, v_ref, line_ref, mask_ref, query_mask_ref,
    mixed_ref, doc_probs_ref, query_probs_ref, scores_scratch, probs_scratch,
):
    blocks = length // count
    query_start = docs * length
    query_blocks = (q_ref.shape[0] - query_start) // count
    row_group = lax.broadcasted_iota(jnp.int32, (count, count), 0) // group
    column_group = lax.broadcasted_iota(jnp.int32, (count, count), 1) // group
    bands, edges = [], []
    for head in range(2):
        line = line_ref[0, head : head + 1, :]
        band = pltpu.roll(
            jnp.broadcast_to(line, (count, 4 * count)), 0, 1, stride=1, stride_axis=0
        )
        bands.append(band)
        edges.append(
            (
                jnp.broadcast_to(line[:, 4 * count - 1 :], (1, count)),
                jnp.broadcast_to(line[:, 3 * count - 1 : 3 * count], (1, count)),
            )
        )
    for doc in range(docs):
        base = doc * length
        whole = slice(base, base + length)
        masking = mask_ref[doc : doc + 1, :]
        for head in range(2):
            own = slice(head * length, (head + 1) * length)
            scores_scratch[own, :] = dot_nt(keep_lanes(head, q_ref[whole, :]), k_ref[whole, :])
        halves = []
        for head in range(2):
            own = slice(head * length, (head + 1) * length)
            for row in range(blocks):
                rows = slice(row * count, (row + 1) * count)
                stacked = slice(head * length + row * count, head * length + (row + 1) * count)
                shifted = []
                for column in range(blocks):
                    columns = slice(column * count, (column + 1) * count)
                    away = column - row
                    block = scores_scratch[stacked, columns]
                    if abs(away) > 1:
                        block = block + (edges[head][away > 0] + masking[:, columns])
                    else:
                        start = (away + 1) * count
                        block = block + bands[head][:, start : start + count]
                        block = block + masking[:, columns]
                    shifted.append(block)
                probs = softmax_rows(jnp.concatenate(shifted, axis=1))
                doc_probs_ref[head, base + row * count : base + (row + 1) * count, :] = probs
                probs_scratch[stacked, :] = probs.astype(jnp.bfloat16)
            halves.append(dot_nn(probs_scratch[own, :], v_ref[whole, :]))
        mixed_ref[whole, :] = joined(jnp.concatenate(halves, axis=0))
    for block in range(query_blocks):
        rows = slice(query_start + block * count, query_start + (block + 1) * count)
        masking = query_mask_ref[block]
        scores = dot_nt(both_heads(q_ref[rows, :]), k_ref[rows, :])
        low = []
        for head in range(2):
            bias = jnp.where(
                row_group == column_group, bands[head][:, count : 2 * count], -1e9
            )
            probs = softmax_rows(scores[head * count : (head + 1) * count, :] + bias + masking)
            query_probs_ref[head, block * count : (block + 1) * count, :] = probs
            low.append(probs.astype(jnp.bfloat16))
        mixed_ref[rows, :] = joined(dot_nn(jnp.concatenate(low, axis=0), v_ref[rows, :]))


def pair_spec(rows, offset):
    return pl.BlockSpec((rows, 2 * 64), lambda pair: (0, offset + pair))


def attend(projected, lines, doc_mask, query_mask, group):
    docs, length = doc_mask.shape
    rows, width = projected.shape[0], projected.shape[1] // 3
    pairs = lines.shape[0]
    query_rows = rows - docs * length
    return pl.pallas_call(
        functools.partial(attend_kernel, docs, length, group),
        grid=(pairs,),
        out_shape=(
            jax.ShapeDtypeStruct((rows, width), jnp.bfloat16),
            pltpu.HBM((2 * pairs, docs * length, length), jnp.float32),
            pltpu.HBM((2 * pairs, query_rows, count), jnp.float32),
        ),
        in_specs=[
            pair_spec(rows, 0),
            pair_spec(rows, pairs),
            pair_spec(rows, 2 * pairs),
            pl.BlockSpec((1, 2, 4 * count), lambda pair: (pair, 0, 0)),
            pl.BlockSpec((docs, length), lambda pair: (0, 0)),
            pl.BlockSpec(query_mask.shape, lambda pair: (0, 0, 0)),
        ],
        out_specs=(
            pair_spec(rows, 0),
            pl.BlockSpec((2, docs * length, length), lambda pair: (pair, 0, 0)),
            pl.BlockSpec((2, query_rows, count), lambda pair: (pair, 0, 0)),
        ),
        scratch_shapes=[
            pltpu.VMEM((2 * length, length), jnp.float32),
            pltpu.VMEM((2 * length, length), jnp.bfloat16),
        ],
        compiler_params=pltpu.CompilerParams(vmem_limit_bytes=18 * 2**20),
        cost_estimate=pl.CostEstimate(
            flops=2 * 2 * pairs * (docs * length * length + query_rows * count) * 128 * 2,
            bytes_accessed=rows * width * 8 + 8 * pairs * docs * length * length,
            transcendentals=2 * pairs * (docs * length * length + query_rows * count),
        ),
        name="attend",
    )(*in_hbm(projected, projected, projected), lines, doc_mask, query_mask)


def attend_back_kernel(
    docs, length, q_ref, k_ref, v_ref, grad_ref, doc_probs_ref, query_probs_ref, onehot_ref,
    out_ref, table_ref, grads_scratch, scores_scratch, probs_scratch, lines_scratch,
):
    blocks = length // count
    query_start = docs * length
    query_blocks = (q_ref.shape[0] - query_start) // count
    low = jnp.bfloat16
    half = q_ref.shape[1] // 2
    band = [[None] * 5, [None] * 5]

    def gather(head, place, block):
        held = band[head][place]
        band[head][place] = block if held is None else held + block

    def backward(probs, grad_probs):
        product = probs * grad_probs
        return product - probs * jnp.sum(product, axis=-1, keepdims=True)

    for doc in range(docs):
        base = doc * length
        whole = slice(base, base + length)
        for head in range(2):
            own = slice(head * length, (head + 1) * length)
            grads_scratch[own, :] = dot_nt(keep_lanes(head, grad_ref[whole, :]), v_ref[whole, :])
        halves, grad_k, grad_v = [], [], []
        q_turned = q_ref[whole, :].T
        grad_turned = grad_ref[whole, :].T
        for head in range(2):
            own = slice(head * length, (head + 1) * length)
            for row in range(blocks):
                rows = slice(base + row * count, base + (row + 1) * count)
                stacked = slice(head * length + row * count, head * length + (row + 1) * count)
                probs = doc_probs_ref[head, rows, :]
                scores = backward(probs, grads_scratch[stacked, :])
                for column in range(blocks):
                    away = max(-2, min(2, column - row))
                    block = scores[:, column * count : (column + 1) * count]
                    if abs(away) == 2:
                        block = jnp.sum(block.reshape(count // 8, 8, count), axis=0)
                    gather(head, away + 2, block)
                scores_scratch[stacked, :] = scores.astype(low)
                probs_scratch[stacked, :] = probs.astype(low)
            halves.append(dot_nn(scores_scratch[own, :], k_ref[whole, :]))
            part = slice(head * half, (head + 1) * half)
            grad_k.append(dot_nn(q_turned[part, :], scores_scratch[own, :]))
            grad_v.append(dot_nn(grad_turned[part, :], probs_scratch[own, :]))
        out_ref[0, whole, :] = joined(jnp.concatenate(halves, axis=0))
        out_ref[1, whole, :] = jnp.concatenate(grad_k, axis=0).astype(low).T
        out_ref[2, whole, :] = jnp.concatenate(grad_v, axis=0).astype(low).T
    for block in range(query_blocks):
        rows = slice(query_start + block * count, query_start + (block + 1) * count)
        grad_probs = dot_nt(both_heads(grad_ref[rows, :]), v_ref[rows, :])
        low_scores, low_probs = [], []
        for head in range(2):
            probs = query_probs_ref[head, block * count : (block + 1) * count, :]
            scores = backward(probs, grad_probs[head * count : (head + 1) * count, :])
            gather(head, 2, scores)
            low_scores.append(scores.astype(low))
            low_probs.append(probs.astype(low))
        out_ref[0, rows, :] = joined(dot_nn(jnp.concatenate(low_scores, axis=0), k_ref[rows, :]))
        turned = jnp.concatenate(low_scores, axis=1).T
        turned = jnp.concatenate([turned, jnp.concatenate(low_probs, axis=1).T], axis=1)
        empty = jnp.zeros((count, 2 * half), low)
        weights = jnp.concatenate(
            [
                jnp.concatenate([q_ref[rows, :], empty], axis=1),
                jnp.concatenate([empty, grad_ref[rows, :]], axis=1),
            ],
            axis=0,
        )
        both_grads = dot_nn(turned, weights)
        out_ref[1, rows, :] = joined(both_grads[:, : 2 * half])
        out_ref[2, rows, :] = joined(both_grads[:, 2 * half :])
    lines = []
    for head in range(2):
        below, before, middle, after, above = band[head]
        wide = jnp.concatenate([before, middle, after, jnp.zeros_like(middle)], axis=1)
        eights = [wide[:8]]
        for start in range(8, count, 8):
            eights.append(pltpu.roll(wide[start : start + 8], 4 * count - start, 1))
        wide = sum(eights)
        wide = jnp.concatenate([wide[7 - row : 8 - row] for row in range(8)], axis=0)
        wide = pltpu.roll(wide, 4 * count - 7, 1, stride=1, stride_axis=0)
        wide = jnp.sum(wide, axis=0, keepdims=True)
        far = jnp.concatenate(
            [
                jnp.zeros((1, 2 * count), jnp.float32),
                jnp.sum(above, axis=0, keepdims=True),
                jnp.sum(below, axis=0, keepdims=True),
            ],
            axis=1,
        )
        lines.append(wide + far)
    pair = pl.program_id(0)
    lines_scratch[pair] = jnp.concatenate(lines, axis=0)

    @pl.when(pair == pl.num_programs(0) - 1)
    def _():
        table_ref[...] = jnp.dot(
            lines_scratch[...].reshape(-1, 4 * count),
            onehot_ref[...],
            precision=highest,
            preferred_element_type=jnp.float32,
        ).reshape(table_ref.shape)


def attend_back(projected, grad_mixed, doc_probs, query_probs, onehot, length):
    rows, width = grad_mixed.shape
    pairs = doc_probs.shape[0] // 2
    docs = doc_probs.shape[1] // length
    query_rows = query_probs.shape[1]

    return pl.pallas_call(
        functools.partial(attend_back_kernel, docs, length),
        grid=(pairs,),
        out_shape=(
            jax.ShapeDtypeStruct((3, rows, width), jnp.bfloat16),
            pltpu.HBM((pairs, 2, onehot.shape[1]), jnp.float32),
        ),
        in_specs=[
            pair_spec(rows, 0),
            pair_spec(rows, pairs),
            pair_spec(rows, 2 * pairs),
            pair_spec(rows, 0),
            pl.BlockSpec((2, docs * length, length), lambda pair: (pair, 0, 0)),
            pl.BlockSpec((2, query_rows, count), lambda pair: (pair, 0, 0)),
            pl.BlockSpec(onehot.shape, lambda pair: (0, 0)),
        ],
        out_specs=(
            pl.BlockSpec((3, rows, 2 * 64), lambda pair: (0, 0, pair)),
            pl.BlockSpec((pairs, 2, onehot.shape[1]), lambda pair: (0, 0, 0)),
        ),
        scratch_shapes=[
            pltpu.VMEM((2 * length, length), jnp.float32),
            pltpu.VMEM((2 * length, length), jnp.bfloat16),
            pltpu.VMEM((2 * length, length), jnp.bfloat16),
            pltpu.VMEM((pairs, 2, 4 * count), jnp.float32),
        ],
        compiler_params=pltpu.CompilerParams(vmem_limit_bytes=22 * 2**20),
        cost_estimate=pl.CostEstimate(
            flops=2 * 2 * pairs * (docs * length * length + query_rows * count) * 128 * 4,
            bytes_accessed=rows * width * 14 + 8 * pairs * docs * length * length,
            transcendentals=0,
        ),
        name="attend_back",
    )(*in_hbm(projected, projected, projected, grad_mixed, doc_probs, query_probs), onehot)


def dot_tn(left, right):
    return lax.dot_general(
        left, right, (((0,), (0,)), ((), ())), preferred_element_type=jnp.float32
    )


tile = 512
row_parts = 2
curve = 0.044715
slope = 0.7978845608028654


def turned_rows(place_ref, values, turned):
    quarter = values.shape[1] // 4
    flipped = values[...].T
    for outer in range(2):
        for core in range(2):
            kept = core ^ 1 ^ place_ref[1]
            start = pl.multiple_of((2 * kept + outer) * quarter, 16)
            block = flipped[(2 * outer + core) * quarter : (2 * outer + core + 1) * quarter, :]
            turned[pl.ds(start, quarter), :] = block


def split_store(values, kept_ref, sent_ref):
    quarter = values.shape[0] // 4
    low = values.astype(jnp.bfloat16)
    for outer in range(2):
        sent_ref[outer] = low[outer * quarter : (outer + 1) * quarter, :]
        kept_ref[outer] = low[(2 + outer) * quarter : (3 + outer) * quarter, :]


def gate_kernel(place_ref, n2_ref, weight, cot_ref, act_ref, by_gate_ref, by_up_ref, kept_ref, sent_ref):
    rows, width = n2_ref.shape
    hidden = weight.shape[-1] // 2
    start = pl.multiple_of(pl.program_id(0) * tile, 128)
    gate_weight = weight[..., pl.ds(start, tile)].reshape(width, tile)
    up_weight = weight[..., pl.ds(hidden + start, tile)].reshape(width, tile)

    def finish(places, gate, up):
        square = gate * gate
        bent = slope + (slope * curve) * square
        halved = 0.5 + 0.5 * jnp.tanh(gate * bent)
        value = gate * halved
        steep = halved + gate * (6.0 * bent - 4.0 * slope) * (halved - halved * halved)
        act_ref[places, :] = (value * up).astype(jnp.bfloat16)
        by_gate_ref[places, :] = up * steep
        by_up_ref[places, :] = value

    held = None
    for start in range(0, rows, 128):
        places = slice(start, start + 128)
        gate = dot_nn(n2_ref[places, :], gate_weight)
        up = dot_nn(n2_ref[places, :], up_weight)
        if held is not None:
            finish(*held)
        held = (places, gate, up)
    finish(*held)
    grad = dot_tn(act_ref[...], cot_ref[...]).astype(jnp.bfloat16)
    core = pl.program_id(0) % 2

    @pl.when(core == place_ref[1])
    def _():
        kept_ref[0] = grad

    @pl.when(core != place_ref[1])
    def _():
        sent_ref[0] = grad


def gate_forward(place, pieces, normed_two, cot_low):
    rows, width = normed_two.shape
    columns = pieces[0].shape[-1]
    hidden = columns // 2
    number = len(pieces)
    whole = pl.BlockSpec((rows, width), lambda step: (0, 0))
    column = pl.BlockSpec((rows, tile), lambda step: (0, step))
    half = pl.BlockSpec((1, tile, width), lambda step: (step // 2, 0, 0))
    assert hidden == 4 * tile

    def kernel(place_ref, *refs):
        n2_ref, cot_ref, *outs, full_ref, held, sems = refs[number:]
        filled(
            place_ref, refs[:number], full_ref, held, sems,
            lambda: gate_kernel(place_ref, n2_ref, held, cot_ref, *outs),
        )

    *results, full = pl.pallas_call(
        kernel,
        grid=(hidden // tile,),
        out_shape=(
            pltpu.HBM((rows, hidden), jnp.bfloat16),
            pltpu.HBM((rows, hidden), jnp.float32),
            pltpu.HBM((rows, hidden), jnp.float32),
            jax.ShapeDtypeStruct((2, tile, width), jnp.bfloat16),
            jax.ShapeDtypeStruct((2, tile, width), jnp.bfloat16),
            pltpu.HBM(slab(columns, width), jnp.bfloat16),
        ),
        in_specs=[scalars()] + [anywhere] * number + [whole, whole],
        out_specs=(column, column, column, half, half, anywhere),
        scratch_shapes=[
            pltpu.VMEM(slab(columns, width), jnp.bfloat16),
            pltpu.SemaphoreType.DMA((9,)),
        ],
        compiler_params=pltpu.CompilerParams(vmem_limit_bytes=34 * 2**20),
        cost_estimate=pl.CostEstimate(
            flops=6 * rows * width * hidden,
            bytes_accessed=rows * hidden * 10 + 8 * width * hidden,
            transcendentals=rows * hidden,
        ),
        name="gate_forward",
    )(place, *pieces, normed_two, *in_hbm(cot_low))
    return (*results, full.reshape(width, columns))


def gate_back_kernel(
    place_ref, n2_ref, cot_ref, ff, by_gate_ref, by_up_ref, out_ref, kept_ref, sent_ref, turned
):
    step = pl.program_id(0)
    weight = ff[step // 2, step % 2].reshape(tile, ff.shape[-1])
    incoming = dot_nt(cot_ref[...], weight)
    by_gate = (incoming * by_gate_ref[...]).astype(jnp.bfloat16)
    by_up = (incoming * by_up_ref[...]).astype(jnp.bfloat16)
    out_ref[0] = by_gate
    out_ref[1] = by_up
    split_store(dot_nn(turned[...], by_gate), kept_ref.at[:, :, :tile], sent_ref.at[:, :, :tile])
    split_store(dot_nn(turned[...], by_up), kept_ref.at[:, :, tile:], sent_ref.at[:, :, tile:])


def gate_back(place, pieces, normed_two, cot_low, by_gate, by_up):
    rows, width = normed_two.shape
    hidden = by_gate.shape[1]
    number = len(pieces)
    whole = pl.BlockSpec((rows, width), lambda step: (0, 0))
    column = pl.BlockSpec((rows, tile), lambda step: (0, step))
    half = pl.BlockSpec((2, width // 4, 2 * tile), lambda step: (0, 0, step))

    def kernel(place_ref, *refs):
        n2_ref, cot_ref, gate_ref, up_ref, *outs, full_ref, held, turned, sems = refs[number:]
        filled(
            place_ref, refs[:number], full_ref, held, sems,
            lambda: gate_back_kernel(
                place_ref, n2_ref, cot_ref, held, gate_ref, up_ref, *outs, turned
            ),
            lambda: turned_rows(place_ref, n2_ref, turned), True,
        )

    *results, full = pl.pallas_call(
        kernel,
        grid=(hidden // tile,),
        out_shape=(
            pltpu.HBM((2, rows, hidden), jnp.bfloat16),
            jax.ShapeDtypeStruct((2, width // 4, 2 * hidden), jnp.bfloat16),
            jax.ShapeDtypeStruct((2, width // 4, 2 * hidden), jnp.bfloat16),
            pltpu.HBM(slab(width, hidden), jnp.bfloat16),
        ),
        in_specs=[scalars()] + [anywhere] * number + [whole, whole, column, column],
        out_specs=(
            pl.BlockSpec((2, rows, tile), lambda step: (0, 0, step)),
            half,
            half,
            anywhere,
        ),
        scratch_shapes=[
            pltpu.VMEM(slab(width, hidden), jnp.bfloat16),
            pltpu.VMEM((width, rows), jnp.bfloat16),
            pltpu.SemaphoreType.DMA((9,)),
        ],
        compiler_params=pltpu.CompilerParams(vmem_limit_bytes=38 * 2**20),
        cost_estimate=pl.CostEstimate(
            flops=6 * rows * width * hidden,
            bytes_accessed=rows * hidden * 12 + 8 * width * hidden,
            transcendentals=0,
        ),
        name="gate_back",
    )(place, *pieces, normed_two, cot_low, *in_hbm(by_gate, by_up))
    return (*results, full.reshape(hidden, width))


def norm_back(grads, values, gain, residual):
    spread = lax.rsqrt(jnp.mean(values * values, axis=-1, keepdims=True) + epsilon)
    scaled = grads * gain
    inner = jnp.mean(scaled * values, axis=-1, keepdims=True)
    gain_grad = jnp.sum(grads * (values * spread), axis=0, keepdims=True)
    return residual + spread * scaled - values * (spread * spread * spread * inner), gain_grad


def middle_back_kernel(
    gates_hbm, weight_hbm, out_weight_hbm, middle_hbm, cot_hbm, gain_ref,
    grad_hbm, low_hbm, mixed_hbm, gain_grad_ref,
    gates, weight, out_weight, middle, cot, total, low, mixed, sems,
):
    rows, width = total.shape
    hidden = gates.shape[2]
    wide = hidden // 2
    arrivals = []

    def bring(source, target):
        copy = pltpu.make_async_copy(source, target, sems.at[len(arrivals)])
        copy.start()
        arrivals.append(copy)

    for part in range(4):
        columns = pl.ds(part % 2 * wide, wide)
        bring(gates_hbm.at[part // 2, :, columns], gates.at[part // 2, :, columns])
        columns = pl.ds(part * wide, wide)
        bring(weight_hbm.at[:, columns], weight.at[:, columns])
    bring(middle_hbm, middle)
    bring(cot_hbm, cot)
    bring(out_weight_hbm.at[:, pl.ds(3 * width, width)], out_weight)
    for part in range(4):
        arrivals[2 * part].wait()
        arrivals[2 * part + 1].wait()
        columns = slice(part % 2 * wide, part % 2 * wide + wide)
        product = dot_nt(
            gates[part // 2, :, columns], weight[:, part * wide : part * wide + wide]
        )
        if part == 0:
            total[...] = product
        else:
            total[...] += product
    for copy in arrivals[8:]:
        copy.wait()
    leaving = []
    for half in range(2):
        places = slice(half * rows // 2, (half + 1) * rows // 2)
        grad, gain_grad = norm_back(
            total[places, :], middle[places, :], gain_ref[...], cot[places, :]
        )
        total[places, :] = grad
        low[places, :] = grad.astype(jnp.bfloat16)
        if half == 0:
            gain_grad_ref[...] = gain_grad
        else:
            gain_grad_ref[...] += gain_grad
        mixed[places, :] = dot_nt(low[places, :], out_weight[...]).astype(jnp.bfloat16)
        places = pl.ds(half * rows // 2, rows // 2)
        for source, target in ((total, grad_hbm), (low, low_hbm), (mixed, mixed_hbm)):
            copy = pltpu.make_async_copy(
                source.at[places], target.at[places], sems.at[len(arrivals) + len(leaving)]
            )
            copy.start()
            leaving.append(copy)
    for copy in leaving:
        copy.wait()


def middle_back(gates, full_in, middle, cotangent, gain, full_attention):
    rows, width = middle.shape
    hidden = gates.shape[2]
    low = jnp.bfloat16
    line = pl.BlockSpec(memory_space=pltpu.VMEM)
    return pl.pallas_call(
        middle_back_kernel,
        out_shape=(
            pltpu.HBM((rows, width), jnp.float32),
            pltpu.HBM((rows, width), low),
            pltpu.HBM((rows, width), low),
            jax.ShapeDtypeStruct((1, width), jnp.float32),
        ),
        in_specs=[anywhere] * 5 + [line],
        out_specs=(anywhere, anywhere, anywhere, line),
        scratch_shapes=[
            pltpu.VMEM((2, rows, hidden), low),
            pltpu.VMEM((width, 2 * hidden), low),
            pltpu.VMEM((width, width), low),
            pltpu.VMEM((rows, width), jnp.float32),
            pltpu.VMEM((rows, width), jnp.float32),
            pltpu.VMEM((rows, width), jnp.float32),
            pltpu.VMEM((rows, width), low),
            pltpu.VMEM((rows, width), low),
            pltpu.SemaphoreType.DMA((17,)),
        ],
        compiler_params=pltpu.CompilerParams(vmem_limit_bytes=46 * 2**20),
        cost_estimate=pl.CostEstimate(
            flops=4 * rows * width * hidden + 2 * rows * width * width,
            bytes_accessed=rows * hidden * 4 + 4 * width * hidden + 18 * rows * width,
            transcendentals=0,
        ),
        name="middle_back",
    )(*in_hbm(gates, full_in, full_attention, middle, cotangent), gain.reshape(1, -1))


def scalars():
    return pl.BlockSpec(memory_space=pltpu.SMEM)


def by_parts(name, first, second, kinds, body, *extra):
    width = first.shape[1]
    rows = first.shape[0] + second.shape[0]
    starts = first.shape[0] // count

    def kernel(first_ref, second_ref, *refs):
        @pl.when(pl.program_id(0) < starts)
        def _():
            body(first_ref, *refs)

        @pl.when(pl.program_id(0) >= starts)
        def _():
            body(second_ref, *refs)

    return pl.pallas_call(
        kernel,
        grid=(rows // count,),
        out_shape=[pltpu.HBM((rows, width), kind) for kind in kinds],
        in_specs=[
            pl.BlockSpec((count, width), lambda step: (jnp.minimum(step, starts - 1), 0)),
            pl.BlockSpec((count, width), lambda step: (jnp.maximum(step - starts, 0), 0)),
        ]
        + [pl.BlockSpec(line.shape, lambda step: (0, 0)) for line in extra],
        out_specs=[pl.BlockSpec((count, width), lambda step: (step, 0))] * len(kinds),
        compiler_params=pltpu.CompilerParams(vmem_limit_bytes=20 * 2**20),
        cost_estimate=pl.CostEstimate(
            flops=4 * rows * width, bytes_accessed=10 * rows * width, transcendentals=rows
        ),
        name=name,
    )(*in_hbm(first, second), *extra)


def norm_body(rows_ref, gain_ref, values_ref, normed_ref):
    values = rows_ref[...]
    spread = lax.rsqrt(jnp.mean(values * values, axis=-1, keepdims=True) + epsilon)
    values_ref[...] = values
    normed_ref[...] = (values * spread * gain_ref[...]).astype(jnp.bfloat16)


def round_body(rows_ref, values_ref, low_ref):
    values_ref[...] = rows_ref[...]
    low_ref[...] = rows_ref[...].astype(jnp.bfloat16)


def project(place, pieces, normed):
    rows, width = normed.shape
    columns = pieces[0].shape[-1]
    number = len(pieces)

    def kernel(place_ref, *refs):
        normed_ref, out_ref, full_ref, held, sems = refs[number:]

        def body():
            start = pl.multiple_of(pl.program_id(0) * width, 128)
            weight = held[..., pl.ds(start, width)].reshape(width, width)
            out_ref[...] = dot_nn(normed_ref[...], weight).astype(jnp.bfloat16)

        filled(place_ref, refs[:number], full_ref, held, sems, body)

    projected, full = pl.pallas_call(
        kernel,
        grid=(3,),
        out_shape=(
            pltpu.HBM((rows, 3 * width), jnp.bfloat16),
            pltpu.HBM(slab(columns, width), jnp.bfloat16),
        ),
        in_specs=[scalars()]
        + [anywhere] * number
        + [pl.BlockSpec((rows, width), lambda step: (0, 0))],
        out_specs=(pl.BlockSpec((rows, width), lambda step: (0, step)), anywhere),
        scratch_shapes=[
            pltpu.VMEM(slab(columns, width), jnp.bfloat16),
            pltpu.SemaphoreType.DMA((9,)),
        ],
        compiler_params=pltpu.CompilerParams(vmem_limit_bytes=14 * 2**20),
        cost_estimate=pl.CostEstimate(
            flops=6 * rows * width * width,
            bytes_accessed=8 * rows * width + 4 * columns * width,
            transcendentals=0,
        ),
        name="project",
    )(place, *pieces, normed)
    return projected, full.reshape(width, columns)


def middle_kernel(rows_ref, mixed_ref, weight_ref, gain_ref, middle_ref, normed_ref):
    middle = rows_ref[...] + dot_nn(mixed_ref[...], weight_ref[...])
    spread = lax.rsqrt(jnp.mean(middle * middle, axis=-1, keepdims=True) + epsilon)
    middle_ref[...] = middle
    normed_ref[...] = (middle * spread * gain_ref[...]).astype(jnp.bfloat16)


def middle_forward(values, mixed, full_attention, gain, *earlier):
    rows, width = values.shape
    part = rows // 2
    block = pl.BlockSpec((part, width), lambda step: (step, 0))

    def kernel(*refs):
        middle_kernel(*refs[:4], *refs[4 + len(earlier) :])

    return pl.pallas_call(
        kernel,
        grid=(2,),
        out_shape=(
            pltpu.HBM((rows, width), jnp.float32),
            jax.ShapeDtypeStruct((rows, width), jnp.bfloat16),
        ),
        in_specs=[
            block,
            block,
            pl.BlockSpec((width, width), lambda step: (0, 3)),
            pl.BlockSpec((1, width), lambda step: (0, 0)),
        ]
        + [anywhere] * len(earlier),
        out_specs=(block, block),
        compiler_params=pltpu.CompilerParams(vmem_limit_bytes=15 * 2**20),
        cost_estimate=pl.CostEstimate(
            flops=2 * rows * width * width,
            bytes_accessed=12 * rows * width + 2 * width * width,
            transcendentals=0,
        ),
        name="middle_forward",
    )(*in_hbm(values), mixed, *in_hbm(full_attention), gain.reshape(1, -1), *earlier)


def attention_grads_kernel(
    place_ref, normed_ref, grads_ref, mixed_hbm, low_hbm, weight_0, weight_1, weight_2, weight_3,
    gain_ref, ffn_ref, table_ref, kept_ref, sent_ref, small_ref,
    turned, column, ordered, mixed_ref, low_ref, sems,
):
    step = pl.program_id(0)
    last = pl.num_programs(0) - 1
    quarter = column.shape[0] // 4
    copies = [
        pltpu.make_async_copy(mixed_hbm, mixed_ref, sems.at[0]),
        pltpu.make_async_copy(low_hbm, low_ref, sems.at[1]),
    ]

    @pl.when(step == 0)
    def _():
        for copy in copies:
            copy.start()
        turned_rows(place_ref, normed_ref, turned)
        column[...] = jnp.zeros_like(column)

    @pl.when(step < last)
    def _():
        grads = dot_nn(turned[...], grads_ref[0])
        split_store(grads, kept_ref, sent_ref)
        for number, weight in enumerate((weight_0, weight_1, weight_2, weight_3)):
            rows = slice(number * quarter, (number + 1) * quarter)
            product = grads[rows, :] * weight[...].astype(jnp.float32)
            parts = [product[:, lane : lane + 128] for lane in range(0, grads.shape[1], 128)]
            column[rows, :] += sum(parts)

    @pl.when(step == last)
    def _():
        for copy in copies:
            copy.wait()
        turned_rows(place_ref, mixed_ref, turned)
        split_store(dot_nn(turned[...], low_ref[...]), kept_ref, sent_ref)
        for number in range(4):
            row = quarter_owner(number, place_ref[1])
            start = pl.multiple_of(row * quarter, 16)
            ordered[pl.ds(start, quarter), :] = column[number * quarter : (number + 1) * quarter, :]
        gain_grad = jnp.sum(ordered[...].T, axis=0, keepdims=True) / gain_ref[...]
        small_ref[...] = jnp.zeros_like(small_ref)
        lines = gain_grad.shape[1] // 128
        for number, line in enumerate((gain_grad, ffn_ref[...])):
            for part in range(lines):
                row = number * lines + part
                small_ref[row : row + 1, :] = line[:, part * 128 : (part + 1) * 128]
        table = table_ref[...].reshape(-1, table_ref.shape[2])
        small_ref[2 * lines :, : table.shape[1]] = table


def quarter_owner(number, core):
    return 2 * (number % 2) + (core if number >= 2 else 1 - core)


def attention_grads(
    place, normed, grad_projected, mixed, grad_low, full_attention, gain, ffn_grad, table
):
    rows, width = normed.shape
    lines = 2 * (width // 128) + 2 * table.shape[0]

    def fixed(step, where):
        return 0, 0

    def column(step, where):
        return 0, 0, step

    def weight_spec(number):
        return pl.BlockSpec(
            (width // 4, width),
            lambda step, where: (quarter_owner(number, where[1]), jnp.minimum(step, 2)),
        )

    shape = jax.ShapeDtypeStruct((2, width // 4, 4 * width), jnp.bfloat16)
    half = pl.BlockSpec((2, width // 4, width), column)
    return pl.pallas_call(
        attention_grads_kernel,
        grid_spec=pltpu.PrefetchScalarGridSpec(
            num_scalar_prefetch=1,
            grid=(4,),
            in_specs=[
                pl.BlockSpec((rows, width), fixed),
                pl.BlockSpec((1, rows, width), lambda step, where: (jnp.minimum(step, 2), 0, 0)),
                anywhere,
                anywhere,
                *[weight_spec(number) for number in range(4)],
                pl.BlockSpec((1, width), fixed),
                pl.BlockSpec((1, width), fixed),
                pl.BlockSpec(table.shape, lambda step, where: (0, 0, 0)),
            ],
            out_specs=(half, half, pl.BlockSpec((lines, 128), fixed)),
            scratch_shapes=[
                pltpu.VMEM((width, rows), jnp.bfloat16),
                pltpu.VMEM((width, 128), jnp.float32),
                pltpu.VMEM((width, 128), jnp.float32),
                pltpu.VMEM((rows, width), jnp.bfloat16),
                pltpu.VMEM((rows, width), jnp.bfloat16),
                pltpu.SemaphoreType.DMA((2,)),
            ],
        ),
        out_shape=(shape, shape, jax.ShapeDtypeStruct((lines, 128), jnp.float32)),
        compiler_params=pltpu.CompilerParams(vmem_limit_bytes=36 * 2**20),
        cost_estimate=pl.CostEstimate(
            flops=8 * rows * width * width,
            bytes_accessed=12 * rows * width + 14 * width * width,
            transcendentals=0,
        ),
        name="attention_grads",
    )(
        place,
        *in_hbm(normed),
        grad_projected,
        *in_hbm(mixed, grad_low, *[full_attention] * 4),
        gain.reshape(1, -1),
        ffn_grad,
        table,
    )


def input_back(grad_projected, full_qkv, values, residual, gain, doc_rows):
    rows, width = values.shape
    part = rows // row_parts
    block = pl.BlockSpec((part, width), lambda step: (step, 0))

    def kernel(
        grads_ref, weight_ref, rows_ref, residual_ref, gain_ref,
        doc_ref, query_ref, slots, sems,
    ):
        step = pl.program_id(0)
        total = dot_nt(grads_ref[0], weight_ref[:, :width])
        for third in (1, 2):
            columns = slice(third * width, (third + 1) * width)
            total = total + dot_nt(grads_ref[third], weight_ref[:, columns])
        slots[step], _ = norm_back(total, rows_ref[...], gain_ref[...], residual_ref[...])
        emit(slots, (doc_ref, query_ref), sems)

    return pl.pallas_call(
        kernel,
        grid=(row_parts,),
        out_shape=(
            jax.ShapeDtypeStruct((doc_rows, width), jnp.float32),
            jax.ShapeDtypeStruct((rows - doc_rows, width), jnp.float32),
        ),
        in_specs=[
            pl.BlockSpec((3, part, width), lambda step: (0, step, 0)),
            pl.BlockSpec((width, 3 * width), lambda step: (0, 0)),
            block,
            block,
            pl.BlockSpec((1, width), lambda step: (0, 0)),
        ],
        out_specs=(anywhere, anywhere),
        scratch_shapes=[
            pltpu.VMEM((row_parts, part, width), jnp.float32),
            pltpu.SemaphoreType.DMA((row_parts + 1,)),
        ],
        compiler_params=pltpu.CompilerParams(vmem_limit_bytes=30 * 2**20),
        cost_estimate=pl.CostEstimate(
            flops=6 * rows * width * width,
            bytes_accessed=18 * rows * width + 6 * width * width,
            transcendentals=0,
        ),
        name="input_back",
    )(grad_projected, *in_hbm(full_qkv, values, residual), gain.reshape(1, -1))


def layer_outputs(middle, activated, full_ff, doc_rows):
    rows, width = middle.shape
    hidden = activated.shape[1]
    part = rows // row_parts

    def kernel(middle_ref, act_ref, weight_ref, doc_ref, query_ref, slots, sems):
        slots[pl.program_id(0)] = middle_ref[...] + dot_nn(act_ref[...], weight_ref[...])
        emit(slots, (doc_ref, query_ref), sems)

    return pl.pallas_call(
        kernel,
        grid=(row_parts,),
        out_shape=(
            jax.ShapeDtypeStruct((doc_rows, width), jnp.float32),
            jax.ShapeDtypeStruct((rows - doc_rows, width), jnp.float32),
        ),
        in_specs=[
            pl.BlockSpec((part, width), lambda step: (step, 0)),
            pl.BlockSpec((part, hidden), lambda step: (step, 0)),
            pl.BlockSpec((hidden, width), lambda step: (0, 0)),
        ],
        out_specs=(anywhere, anywhere),
        scratch_shapes=[
            pltpu.VMEM((row_parts, part, width), jnp.float32),
            pltpu.SemaphoreType.DMA((row_parts + 1,)),
        ],
        compiler_params=pltpu.CompilerParams(vmem_limit_bytes=24 * 2**20),
        cost_estimate=pl.CostEstimate(
            flops=2 * rows * width * hidden,
            bytes_accessed=8 * rows * width + 2 * hidden * (rows + width),
            transcendentals=0,
        ),
        name="layer_outputs",
    )(*in_hbm(middle, activated, full_ff))


def body(
    doc_inputs,
    query_inputs,
    doc_mask,
    query_lengths,
    doc_cotangent,
    query_cotangent,
    qkv_weight,
    out_weight,
    in_weight,
    ff_weight,
    attn_gain,
    ffn_gain,
    bias_table,
):
    doc_count, doc_length, model_width = doc_inputs.shape
    group_count, group_length = (query_inputs.shape[0], query_inputs.shape[1])
    head_count = bias_table.shape[1]
    doc_rows = doc_count * doc_length
    low = jnp.bfloat16
    routed = hand_routed()
    place = own_place() if routed else (0, 0, 0, 0)
    place_vector = jnp.stack([jnp.asarray(index, jnp.int32) for index in place])

    attention_shard = jnp.concatenate([qkv_weight, out_weight], axis=1).astype(low)
    in_shard = in_weight.astype(low)
    ff_shard = ff_weight.astype(low)

    kinds = (jnp.float32, low)
    values, normed = by_parts(
        "norm_rows",
        doc_inputs.reshape(doc_rows, model_width),
        query_inputs.reshape(-1, model_width),
        kinds,
        norm_body,
        attn_gain.reshape(1, -1),
    )
    cotangent_parts = (
        doc_cotangent.reshape(doc_rows, model_width),
        query_cotangent.reshape(-1, model_width),
    )
    places = jnp.arange(group_length, dtype=jnp.int32)
    query_mask = places[None, :] < query_lengths[:, None]
    onehot = lines_onehot(bias_table.shape[0])
    lines = jnp.einsum("pn,nh->hp", onehot, bias_table, precision=highest)
    lines = lines.reshape(head_count // 2, 2, 4 * count)
    doc_masking = jnp.where(doc_mask > 0, 0.0, -1e9).astype(jnp.float32)
    query_masking = jnp.where(query_mask, 0.0, -1e9).astype(jnp.float32)
    query_masking = query_masking.reshape(-1, 1, count)

    if routed:
        column_a = gather_column(attention_shard)
        row_f = jnp.stack(in_order(ff_shard, swap(ff_shard, dx=1), place[3]))
        column_a, row_f, normed, lines, doc_masking, query_masking, in_shard, cotangent_parts = (
            together(
                column_a, row_f, normed, lines, doc_masking, query_masking, in_shard,
                cotangent_parts,
            )
        )
        plane_a = gather_plane(place, attention_shard, column_a)
        cotangent, cot_low = by_parts("round_rows", *cotangent_parts, kinds, round_body)
        plane_a, cotangent, cot_low = together(plane_a, cotangent, cot_low)
        near_a = gather_near(place, *plane_a)
        column_i = gather_column(in_shard)
        far_a = gather_far(*near_a)
        plane_f = jnp.stack(in_order(row_f, swap(row_f, dy=1), place[0]))
        column_i, far_a, plane_f = together(column_i, far_a, plane_f)
        pieces = gather_order(near_a, far_a, gather_core(*near_a), gather_core(*far_a))
        plane_i = gather_plane(place, in_shard, column_i)
    else:
        cotangent, cot_low = by_parts("round_rows", *cotangent_parts, kinds, round_body)
        pieces = (split_rows(lax.all_gather(attention_shard, both, axis=0, tiled=True)),)
    projected, full_attention = project(place_vector, pieces, normed)
    if routed:
        plane_i, projected = together(plane_i, projected)
        near_i = gather_near(place, *plane_i)
        far_i = gather_far(*near_i)
        second_f = swap(plane_f, dz=2)
    mixed, doc_probs, query_probs = attend(
        projected, lines, doc_masking, query_masking, group_length
    )
    if routed:
        mixed, far_i, second_f = together(mixed, far_i, second_f)
        others_f = gather_others(plane_f, second_f)
        pieces = gather_order(near_i, far_i, gather_core(*near_i), gather_core(*far_i))
    else:
        pieces = (split_rows(lax.all_gather(in_shard, both, axis=0, tiled=True)),)
    middle, normed_two = middle_forward(values, mixed, full_attention, ffn_gain)
    if routed:
        pieces, normed_two = together(pieces, normed_two)
        core_f = gather_core(plane_f, second_f)
    activated, by_gate, by_up, kept, sent, full_in = gate_forward(
        place_vector, pieces, normed_two, cot_low
    )
    if routed:
        others_f, core_f, by_gate, kept, sent = together(others_f, core_f, by_gate, kept, sent)
        core_others = gather_core(*others_f)
        pieces = (plane_f, others_f[0], second_f, others_f[1])
        pieces += (core_f[0], core_others[0], core_f[1], core_others[1])
        ff_grads = NarrowScatter(kept, sent, place_vector)
        got_f = ff_grads.core()
        pieces, got_f = together(pieces, got_f)
        near_f = ff_grads.plane(got_f)
    else:
        pieces = (split_rows(lax.all_gather(ff_shard, both, axis=0, tiled=True)),)
        grad_ff = joined_halves(kept, sent)
    gates, kept, sent, full_ff = gate_back(
        place_vector, pieces, normed_two, cot_low, by_gate, by_up
    )
    if routed:
        gates, kept, sent, near_f = together(gates, kept, sent, near_f)
        in_grads = Scatter(kept, sent, place_vector, pinned=False)
        far_f = ff_grads.far(ff_grads.far_sums(got_f, near_f))
        got_i = in_grads.core()
    else:
        grad_in = joined_halves(kept, sent)
    grad_middle, grad_middle_low, grad_mixed, grad_ffn_gain = middle_back(
        gates, full_in, middle, cotangent, ffn_gain, full_attention
    )
    if routed:
        grad_mixed, far_f, got_i = together(grad_mixed, far_f, got_i)
        near_i = in_grads.plane(got_i)
        shares_f = ff_grads.column(ff_grads.column_sums(got_f, near_f, far_f))
    grad_projected, grad_table = attend_back(
        projected, grad_mixed, doc_probs, query_probs, onehot, doc_length
    )
    if routed:
        grad_projected, grad_table, shares_f, near_i = together(
            grad_projected, grad_table, shares_f, near_i
        )
        far_i = in_grads.far(got_i, near_i)
    kept, sent, small = attention_grads(
        place_vector, normed, grad_projected, mixed, grad_middle_low, full_attention, attn_gain,
        grad_ffn_gain, grad_table,
    )
    if routed:
        kept, sent, far_i, small, grad_projected, shares_f, activated = together(
            kept, sent, far_i, small, grad_projected, shares_f, activated
        )
        attention = Scatter(kept, sent, place_vector, pinned=False)
        got_a = attention.core()
        small = add_flipped(small, {"dc": 1})
        sums_i = in_grads.column_sums(got_i, near_i, far_i)
        got_a, sums_i, small, grad_projected, shares_f, activated = together(
            got_a, sums_i, small, grad_projected, shares_f, activated
        )
        near_a = attention.plane(got_a)
        shares_i = in_grads.column(sums_i)
        small = add_flipped(small, {"dz": 1})
    grad_inputs = input_back(
        grad_projected, full_attention, values, grad_middle, attn_gain, doc_rows
    )
    if routed:
        near_a, grad_inputs, small, shares_f, shares_i, activated = together(
            near_a, grad_inputs, small, shares_f, shares_i, activated
        )
        far_a = attention.far(got_a, near_a)
        small = add_flipped(small, {"dz": 2})
        far_a, small, shares_f, shares_i, activated = together(
            far_a, small, shares_f, shares_i, activated
        )
        sums_a = attention.column_sums(got_a, near_a, far_a)
        sums_a, small, shares_f, shares_i, activated = together(
            sums_a, small, shares_f, shares_i, activated
        )
        shares_a = attention.column(sums_a)
        small = add_flipped(small, {"dx": 1}, {"dy": 1})
    outputs = layer_outputs(middle, activated, full_ff, doc_rows)
    if routed:
        ff_grad_shard = summed(*shares_f)
        in_grad_shard = summed(*shares_i)
        grad_qkv = summed(*[share[:, : 3 * model_width] for share in shares_a])
        grad_out = summed(*[share[:, 3 * model_width :] for share in shares_a])
    else:
        scatter = functools.partial(
            lax.psum_scatter, axis_name=both, scatter_dimension=0, tiled=True
        )
        ff_grad_shard = scatter(grad_ff)
        in_grad_shard = scatter(grad_in)
        grad_attention = scatter(joined_halves(kept, sent))
        grad_qkv = grad_attention[:, : 3 * model_width]
        grad_out = grad_attention[:, 3 * model_width :]
        small = lax.psum(small, both)
    width_lines = model_width // 128
    in_grad_shard = in_grad_shard.reshape(in_weight.shape[0], -1, 2, tile)
    in_grad_shard = jnp.swapaxes(in_grad_shard, 1, 2).reshape(in_weight.shape)
    return (
        outputs[0].reshape(doc_inputs.shape),
        outputs[1].reshape(query_inputs.shape),
        grad_inputs[0].reshape(doc_inputs.shape),
        grad_inputs[1].reshape(query_inputs.shape),
        grad_qkv,
        grad_out,
        in_grad_shard,
        ff_grad_shard,
        small[:width_lines].reshape(model_width),
        small[width_lines : 2 * width_lines].reshape(model_width),
        small[2 * width_lines :, : bias_table.shape[0]].T,
    )


def solution(mesh):
    placed = (
        P(("dp", "fsdp"), None, None),
        P(("dp", "fsdp"), None, None),
        P(("dp", "fsdp"), None),
        P(("dp", "fsdp")),
        P(("dp", "fsdp"), None, None),
        P(("dp", "fsdp"), None, None),
        P(("dp", "fsdp"), None),
        P(("dp", "fsdp"), None),
        P(("dp", "fsdp"), None),
        P(("dp", "fsdp"), None),
        P(),
        P(),
        P(),
    )
    return jax.shard_map(
        body,
        mesh=mesh,
        in_specs=placed,
        out_specs=(
            P(("dp", "fsdp"), None, None),
            P(("dp", "fsdp"), None, None),
            P(("dp", "fsdp"), None, None),
            P(("dp", "fsdp"), None, None),
            P(("dp", "fsdp"), None),
            P(("dp", "fsdp"), None),
            P(("dp", "fsdp"), None),
            P(("dp", "fsdp"), None),
            P(),
            P(),
            P(),
        ),
        check_vma=False,
    )
```

```python
import functools
import math

import jax
import jax.numpy as jnp
from jax import lax
from jax.experimental import pallas as pl
from jax.experimental.pallas import tpu as pltpu
from jax.sharding import PartitionSpec as P

both = ("dp", "fsdp")
epsilon = 1e-06
highest = lax.Precision.HIGHEST
anywhere = pl.BlockSpec(memory_space=pl.ANY)


def place_index(y, c, z, x):
    return ((y * 2 + c) * 4 + z) * 2 + x


def flip_pairs(dy=0, dc=0, dz=0, dx=0):
    pairs = []
    for y in range(2):
        for c in range(2):
            for z in range(4):
                for x in range(2):
                    pairs.append(
                        (place_index(y, c, z, x), place_index(y ^ dy, c ^ dc, z ^ dz, x ^ dx))
                    )
    return pairs


def swap(values, **flips):
    return lax.ppermute(values, both, flip_pairs(**flips))


def hand_routed():
    return (lax.axis_size("dp"), lax.axis_size("fsdp")) == (4, 8)


def own_place():
    outer = lax.axis_index("dp")
    inner = lax.axis_index("fsdp")
    return outer // 2, outer % 2, inner // 2, inner % 2


def after(values, *earlier):
    return lax.optimization_barrier((values, *earlier))[0]


def in_hbm(*values):
    return [pltpu.with_memory_space_constraint(value, pltpu.HBM) for value in values]


def together(*values):
    return lax.optimization_barrier(values)


def fill_copies(place_ref, pieces, target, sems, by_column):
    if len(pieces) == 1:
        return [pltpu.make_async_copy(pieces[0], target, sems.at[0])]
    y, c, z, x = place_ref[0], place_ref[1], place_ref[2], place_ref[3]
    copies = []
    even = z - z % 2
    for number, piece in enumerate(pieces):
        core = c ^ (number // 4)
        kind = number % 4
        if by_column:
            where = target.at[:, core, z ^ kind]
        elif kind < 2:
            where = target.at[y ^ kind, core, pl.ds(even, 2)]
        else:
            where = target.at[:, core, pl.ds(even ^ 2, 2), x ^ (kind - 2)]
        copies.append(pltpu.make_async_copy(piece, where, sems.at[number]))
    return copies


def filled(place_ref, pieces, full_ref, held, sems, body, meanwhile=None, by_column=False):
    step = pl.program_id(0)
    kept = pltpu.make_async_copy(held, full_ref, sems.at[8])

    @pl.when(step == 0)
    def _():
        copies = fill_copies(place_ref, pieces, held, sems, by_column)
        for copy in copies:
            copy.start()
        if meanwhile is not None:
            meanwhile()
        for copy in copies:
            copy.wait()
        kept.start()

    body()

    @pl.when(step == pl.num_programs(0) - 1)
    def _():
        kept.wait()


def emit(slots, targets, sems):
    step, rows = pl.program_id(0), slots.shape[1]
    copies = []
    for number in range(slots.shape[0]):
        start = 0
        for target in targets:
            low = max(number * rows, start)
            high = min((number + 1) * rows, start + target.shape[0])
            if low < high:
                source = slots.at[number, pl.ds(low - number * rows, high - low)]
                where = target.at[pl.ds(low - start, high - low)]
                copy = pltpu.make_async_copy(source, where, sems.at[len(copies)])
                copies.append((number, copy))
            start += target.shape[0]
    for number in range(slots.shape[0]):

        @pl.when(step == number)
        def _():
            for owner, copy in copies:
                if owner == number:
                    copy.start()

    @pl.when(step == slots.shape[0] - 1)
    def _():
        for _, copy in copies:
            copy.wait()


def gather_order(near, far, core_near, core_far):
    return (near[0], far[0], near[1], far[1], core_near[0], core_far[0], core_near[1], core_far[1])


def slab(columns, rows):
    return (2, 2, 4, 2, rows // 32, columns)


def split_rows(full):
    return full.reshape(slab(full.shape[1], full.shape[0]))


def in_order(own, other, index):
    odd = index % 2 == 1
    return jnp.where(odd, other, own), jnp.where(odd, own, other)


def gather_column(shard):
    two, three, one = [swap(shard, dz=flip) for flip in (2, 3, 1)]
    return one, two, three


def gather_plane(place, shard, column):
    first = jnp.stack(in_order(shard, column[0], place[2]))
    second = jnp.stack(in_order(column[1], column[2], place[2]))
    return first, second, swap(first, dx=1), swap(second, dy=1)


def gather_near(place, first, second, first_near, second_near):
    even, odd = in_order(first, first_near, place[3])
    first = jnp.stack([even[0], odd[0], even[1], odd[1]]).reshape(2, 2, *first.shape[1:])
    second = jnp.stack(in_order(second, second_near, place[0]))
    return first, second


def gather_far(first, second):
    return swap(first, dy=1), swap(second, dx=1)


def gather_others(own, second):
    return swap(own, dz=1), swap(second, dz=1)


def gather_core(*pieces):
    return tuple(swap(piece, dc=1) for piece in pieces)


def summed(*terms):
    total = terms[0].astype(jnp.float32)
    for term in terms[1:]:
        total = total + term.astype(jnp.float32)
    return total


def joined_halves(kept, sent):
    return jnp.stack([kept, sent], axis=1).reshape(-1, kept.shape[2]).astype(jnp.float32)


def route(name, place, sources, targets, body, scratch=()):
    def spec(array, lead, pick):
        block = (*lead, *array.shape[-2:])
        return pl.BlockSpec(block, lambda step, where: (*pick(where), 0, 0))

    return pl.pallas_call(
        body,
        grid_spec=pltpu.PrefetchScalarGridSpec(
            num_scalar_prefetch=1,
            grid=(1,),
            in_specs=[spec(*source) for source in sources],
            out_specs=[spec(*target) for target in targets],
            scratch_shapes=scratch,
        ),
        out_shape=[target[0] for target in targets],
        compiler_params=pltpu.CompilerParams(vmem_limit_bytes=20 * 2**20),
        cost_estimate=pl.CostEstimate(
            flops=0,
            bytes_accessed=8 * len(sources) * math.prod(sources[0][0].shape[-2:]),
            transcendentals=0,
        ),
        name=name,
    )(place, *[source[0] for source in sources])


def whole_block(target):
    lead = target.shape[:-2]
    return target, lead, lambda where: (0,) * len(lead)


def store_sum(out_ref, *refs):
    blocks = math.prod(refs[0].shape[:-2])
    for number in range(blocks):
        terms = []
        for ref in (out_ref, *refs):
            index, rest = [], number
            for size in reversed(ref.shape[:-2]):
                index.insert(0, rest % size)
                rest //= size
            terms.append(ref.at[tuple(index)])
        terms[0][...] = summed(*[term[...] for term in terms[1:]]).astype(out_ref.dtype)


class Scatter:
    def __init__(self, kept, sent, place, pinned=True):
        self.place = place
        self.pinned = pinned
        self.block = (kept.shape[1] // 8, kept.shape[2])
        self.shape = (2, 4, 2, *self.block)
        self.kept = kept.reshape(self.shape)
        self.sent = sent

    def target(self, *lead, dtype=jnp.bfloat16):
        return jax.ShapeDtypeStruct((*lead, *self.block), dtype)

    def both(self, got, lead, pick):
        kept = in_hbm(self.kept)[0] if self.pinned else self.kept
        return [(kept, lead, pick), (got, lead, pick)]

    def core(self):
        return swap(self.sent, dc=1).reshape(self.shape)

    def plane(self, got):
        def body(place_ref, *refs):
            store_sum(refs[4], *refs[0:2])
            store_sum(refs[5], *refs[2:4])

        sources = self.both(got, (2, 2, 1), lambda where: (0, 0, 1 - where[3]))
        sources += self.both(got, (1, 2, 2), lambda where: (1 - where[0], 1, 0))
        target = whole_block(self.target(2, 2))
        one, two = route("plane", self.place, sources, [target, target], body)
        return swap(one, dx=1), swap(two, dy=1)

    def far(self, got, near):
        def body(place_ref, *refs):
            store_sum(refs[6], *refs[0:3])
            store_sum(refs[7], *refs[3:6])

        sources = [
            *self.both(got, (1, 2, 1), lambda where: (1 - where[0], 0, where[3])),
            (near[0], (1, 2), lambda where: (1 - where[0], 0)),
            *self.both(got, (1, 2, 1), lambda where: (where[0], 1, 1 - where[3])),
            (near[1], (2, 1), lambda where: (0, 1 - where[3])),
        ]
        target = whole_block(self.target(2))
        one, two = route("far", self.place, sources, [target, target], body)
        return swap(one, dy=1), swap(two, dx=1)

    def column_sources(self, near, far):
        return [
            (near[0], (1, 2), lambda where: (where[0], 0)),
            (far[0], (2,), lambda where: (0,)),
            (near[1], (2, 1), lambda where: (0, where[3])),
            (far[1], (2,), lambda where: (0,)),
        ]

    def column_terms(self, row, refs):
        if row < 2:
            return refs[0].at[0, row], refs[1].at[row]
        return refs[2].at[row - 2, 0], refs[3].at[row - 2]

    def column_sums(self, got, near, far):
        sources = self.both(got, (1, 4, 1), lambda where: (where[0], 0, where[3]))
        sources += self.column_sources(near, far)
        number = len(sources)

        def body(place_ref, *refs):
            *outs, total = refs[number:]
            for row in range(4):
                terms = (refs[0].at[0, row, 0], refs[1].at[0, row, 0])
                terms += self.column_terms(row, refs[2:number])
                total[row] = summed(*[term[...] for term in terms])
            for flip, out in enumerate(outs):
                out[...] = total[place_ref[2] ^ flip].astype(out.dtype)

        targets = [self.target(dtype=jnp.float32)] + [self.target()] * 3
        targets = [whole_block(target) for target in targets]
        scratch = [pltpu.VMEM((4, *self.block), jnp.float32)]
        return tuple(route("column", self.place, sources, targets, body, scratch))

    def column(self, sums):
        return sums[0], *[swap(share, dz=flip) for flip, share in zip((1, 2, 3), sums[1:])]


class NarrowScatter(Scatter):
    def both(self, got, lead, pick, pinned=False):
        kept, got = in_hbm(self.kept, got) if pinned else (self.kept, got)
        return [(kept, lead, pick), (got, lead, pick)]

    def plane(self, got):
        def body(place_ref, *refs):
            store_sum(refs[2], *refs[0:2])

        sources = self.both(got, (2, 4, 1), lambda where: (0, 0, 1 - where[3]), False)
        target = whole_block(self.target(2, 4))
        (sums,) = route("plane", self.place, sources, [target], body)
        return swap(sums, dx=1)

    def far_sums(self, got, near):
        def body(place_ref, *refs):
            store_sum(refs[3], *refs[0:3])

        sources = self.both(got, (1, 4, 1), lambda where: (1 - where[0], 0, where[3]))
        sources.append((near, (1, 4), lambda where: (1 - where[0], 0)))
        return route("far", self.place, sources, [whole_block(self.target(4))], body)[0]

    def far(self, sums):
        return swap(sums, dy=1)

    def column_sources(self, near, far):
        return [
            (near, (1, 4), lambda where: (where[0], 0)),
            (far, (4,), lambda where: (0,)),
        ]

    def column_terms(self, row, refs):
        return refs[0].at[0, row], refs[1].at[row]


def add_flipped(values, *steps):
    for flips in steps:
        values = values + swap(values, **flips)
    return values


count = 128


def relative_places():
    places = jnp.arange(4 * count, dtype=jnp.int32)
    return jnp.where(places < 3 * count, places - count, places - 5 * count)


def bucket_of(relative):
    distance = jnp.abs(relative)
    larger = jnp.zeros_like(distance)
    for threshold in (12, 16, 23, 32, 46, 64, 91):
        larger = larger + (distance >= threshold).astype(jnp.int32)
    bucket = jnp.where(distance < 8, distance, 8 + larger)
    return bucket + 16 * (relative > 0).astype(jnp.int32)


def lines_onehot(bucket_count):
    labels = jnp.arange(bucket_count, dtype=jnp.int32)
    return (bucket_of(relative_places())[:, None] == labels).astype(jnp.float32)


def own_lanes(head, shape):
    lanes = lax.broadcasted_iota(jnp.int32, shape, 1)
    return lanes < shape[1] // 2 if head == 0 else lanes >= shape[1] // 2


def keep_lanes(head, values):
    return jnp.where(own_lanes(head, values.shape), values, jnp.zeros_like(values))


def both_heads(values):
    return jnp.concatenate([keep_lanes(0, values), keep_lanes(1, values)], axis=0)


def joined(stacked):
    first, second = jnp.split(stacked, 2, axis=0)
    return jnp.where(own_lanes(0, first.shape), first, second).astype(jnp.bfloat16)


def softmax_rows(scores):
    raised = jnp.exp(scores - jnp.max(scores, axis=-1, keepdims=True))
    return raised * (1.0 / jnp.sum(raised, axis=-1, keepdims=True))


def dot_nt(left, right):
    return lax.dot_general(
        left, right, (((1,), (1,)), ((), ())), preferred_element_type=jnp.float32
    )


def dot_nn(left, right):
    return jnp.dot(left, right, preferred_element_type=jnp.float32)


def attend_kernel(
    docs, length, group, q_ref, k_ref, v_ref, line_ref, mask_ref, query_mask_ref,
    mixed_ref, doc_probs_ref, query_probs_ref, scores_scratch, probs_scratch,
):
    blocks = length // count
    query_start = docs * length
    query_blocks = (q_ref.shape[0] - query_start) // count
    row_group = lax.broadcasted_iota(jnp.int32, (count, count), 0) // group
    column_group = lax.broadcasted_iota(jnp.int32, (count, count), 1) // group
    bands, edges = [], []
    for head in range(2):
        line = line_ref[0, head : head + 1, :]
        band = pltpu.roll(
            jnp.broadcast_to(line, (count, 4 * count)), 0, 1, stride=1, stride_axis=0
        )
        bands.append(band)
        edges.append(
            (
                jnp.broadcast_to(line[:, 4 * count - 1 :], (1, count)),
                jnp.broadcast_to(line[:, 3 * count - 1 : 3 * count], (1, count)),
            )
        )
    for doc in range(docs):
        base = doc * length
        whole = slice(base, base + length)
        masking = mask_ref[doc : doc + 1, :]
        for head in range(2):
            own = slice(head * length, (head + 1) * length)
            scores_scratch[own, :] = dot_nt(keep_lanes(head, q_ref[whole, :]), k_ref[whole, :])
        halves = []
        for head in range(2):
            own = slice(head * length, (head + 1) * length)
            for row in range(blocks):
                rows = slice(row * count, (row + 1) * count)
                stacked = slice(head * length + row * count, head * length + (row + 1) * count)
                shifted = []
                for column in range(blocks):
                    columns = slice(column * count, (column + 1) * count)
                    away = column - row
                    block = scores_scratch[stacked, columns]
                    if abs(away) > 1:
                        block = block + (edges[head][away > 0] + masking[:, columns])
                    else:
                        start = (away + 1) * count
                        block = block + bands[head][:, start : start + count]
                        block = block + masking[:, columns]
                    shifted.append(block)
                probs = softmax_rows(jnp.concatenate(shifted, axis=1))
                doc_probs_ref[head, base + row * count : base + (row + 1) * count, :] = probs
                probs_scratch[stacked, :] = probs.astype(jnp.bfloat16)
            halves.append(dot_nn(probs_scratch[own, :], v_ref[whole, :]))
        mixed_ref[whole, :] = joined(jnp.concatenate(halves, axis=0))
    for block in range(query_blocks):
        rows = slice(query_start + block * count, query_start + (block + 1) * count)
        masking = query_mask_ref[block]
        scores = dot_nt(both_heads(q_ref[rows, :]), k_ref[rows, :])
        low = []
        for head in range(2):
            bias = jnp.where(
                row_group == column_group, bands[head][:, count : 2 * count], -1e9
            )
            probs = softmax_rows(scores[head * count : (head + 1) * count, :] + bias + masking)
            query_probs_ref[head, block * count : (block + 1) * count, :] = probs
            low.append(probs.astype(jnp.bfloat16))
        mixed_ref[rows, :] = joined(dot_nn(jnp.concatenate(low, axis=0), v_ref[rows, :]))


def pair_spec(rows, offset):
    return pl.BlockSpec((rows, 2 * 64), lambda pair: (0, offset + pair))


def attend(projected, lines, doc_mask, query_mask, group):
    docs, length = doc_mask.shape
    rows, width = projected.shape[0], projected.shape[1] // 3
    pairs = lines.shape[0]
    query_rows = rows - docs * length
    return pl.pallas_call(
        functools.partial(attend_kernel, docs, length, group),
        grid=(pairs,),
        out_shape=(
            jax.ShapeDtypeStruct((rows, width), jnp.bfloat16),
            pltpu.HBM((2 * pairs, docs * length, length), jnp.float32),
            pltpu.HBM((2 * pairs, query_rows, count), jnp.float32),
        ),
        in_specs=[
            pair_spec(rows, 0),
            pair_spec(rows, pairs),
            pair_spec(rows, 2 * pairs),
            pl.BlockSpec((1, 2, 4 * count), lambda pair: (pair, 0, 0)),
            pl.BlockSpec((docs, length), lambda pair: (0, 0)),
            pl.BlockSpec(query_mask.shape, lambda pair: (0, 0, 0)),
        ],
        out_specs=(
            pair_spec(rows, 0),
            pl.BlockSpec((2, docs * length, length), lambda pair: (pair, 0, 0)),
            pl.BlockSpec((2, query_rows, count), lambda pair: (pair, 0, 0)),
        ),
        scratch_shapes=[
            pltpu.VMEM((2 * length, length), jnp.float32),
            pltpu.VMEM((2 * length, length), jnp.bfloat16),
        ],
        compiler_params=pltpu.CompilerParams(vmem_limit_bytes=18 * 2**20),
        cost_estimate=pl.CostEstimate(
            flops=2 * 2 * pairs * (docs * length * length + query_rows * count) * 128 * 2,
            bytes_accessed=rows * width * 8 + 8 * pairs * docs * length * length,
            transcendentals=2 * pairs * (docs * length * length + query_rows * count),
        ),
        name="attend",
    )(*in_hbm(projected, projected, projected), lines, doc_mask, query_mask)


def attend_back_kernel(
    docs, length, q_ref, k_ref, v_ref, grad_ref, doc_probs_ref, query_probs_ref, onehot_ref,
    out_ref, table_ref, grads_scratch, scores_scratch, probs_scratch, lines_scratch,
):
    blocks = length // count
    query_start = docs * length
    query_blocks = (q_ref.shape[0] - query_start) // count
    low = jnp.bfloat16
    half = q_ref.shape[1] // 2
    band = [[None] * 5, [None] * 5]

    def gather(head, place, block):
        held = band[head][place]
        band[head][place] = block if held is None else held + block

    def backward(probs, grad_probs):
        product = probs * grad_probs
        return product - probs * jnp.sum(product, axis=-1, keepdims=True)

    for doc in range(docs):
        base = doc * length
        whole = slice(base, base + length)
        for head in range(2):
            own = slice(head * length, (head + 1) * length)
            grads_scratch[own, :] = dot_nt(keep_lanes(head, grad_ref[whole, :]), v_ref[whole, :])
        halves, grad_k, grad_v = [], [], []
        q_turned = q_ref[whole, :].T
        grad_turned = grad_ref[whole, :].T
        for head in range(2):
            own = slice(head * length, (head + 1) * length)
            for row in range(blocks):
                rows = slice(base + row * count, base + (row + 1) * count)
                stacked = slice(head * length + row * count, head * length + (row + 1) * count)
                probs = doc_probs_ref[head, rows, :]
                scores = backward(probs, grads_scratch[stacked, :])
                for column in range(blocks):
                    away = max(-2, min(2, column - row))
                    block = scores[:, column * count : (column + 1) * count]
                    if abs(away) == 2:
                        block = jnp.sum(block.reshape(count // 8, 8, count), axis=0)
                    gather(head, away + 2, block)
                scores_scratch[stacked, :] = scores.astype(low)
                probs_scratch[stacked, :] = probs.astype(low)
            halves.append(dot_nn(scores_scratch[own, :], k_ref[whole, :]))
            part = slice(head * half, (head + 1) * half)
            grad_k.append(dot_nn(q_turned[part, :], scores_scratch[own, :]))
            grad_v.append(dot_nn(grad_turned[part, :], probs_scratch[own, :]))
        out_ref[0, whole, :] = joined(jnp.concatenate(halves, axis=0))
        out_ref[1, whole, :] = jnp.concatenate(grad_k, axis=0).astype(low).T
        out_ref[2, whole, :] = jnp.concatenate(grad_v, axis=0).astype(low).T
    for block in range(query_blocks):
        rows = slice(query_start + block * count, query_start + (block + 1) * count)
        grad_probs = dot_nt(both_heads(grad_ref[rows, :]), v_ref[rows, :])
        low_scores, low_probs = [], []
        for head in range(2):
            probs = query_probs_ref[head, block * count : (block + 1) * count, :]
            scores = backward(probs, grad_probs[head * count : (head + 1) * count, :])
            gather(head, 2, scores)
            low_scores.append(scores.astype(low))
            low_probs.append(probs.astype(low))
        out_ref[0, rows, :] = joined(dot_nn(jnp.concatenate(low_scores, axis=0), k_ref[rows, :]))
        turned = jnp.concatenate(low_scores, axis=1).T
        turned = jnp.concatenate([turned, jnp.concatenate(low_probs, axis=1).T], axis=1)
        empty = jnp.zeros((count, 2 * half), low)
        weights = jnp.concatenate(
            [
                jnp.concatenate([q_ref[rows, :], empty], axis=1),
                jnp.concatenate([empty, grad_ref[rows, :]], axis=1),
            ],
            axis=0,
        )
        both_grads = dot_nn(turned, weights)
        out_ref[1, rows, :] = joined(both_grads[:, : 2 * half])
        out_ref[2, rows, :] = joined(both_grads[:, 2 * half :])
    lines = []
    for head in range(2):
        below, before, middle, after, above = band[head]
        wide = jnp.concatenate([before, middle, after, jnp.zeros_like(middle)], axis=1)
        eights = [wide[:8]]
        for start in range(8, count, 8):
            eights.append(pltpu.roll(wide[start : start + 8], 4 * count - start, 1))
        wide = sum(eights)
        wide = jnp.concatenate([wide[7 - row : 8 - row] for row in range(8)], axis=0)
        wide = pltpu.roll(wide, 4 * count - 7, 1, stride=1, stride_axis=0)
        wide = jnp.sum(wide, axis=0, keepdims=True)
        far = jnp.concatenate(
            [
                jnp.zeros((1, 2 * count), jnp.float32),
                jnp.sum(above, axis=0, keepdims=True),
                jnp.sum(below, axis=0, keepdims=True),
            ],
            axis=1,
        )
        lines.append(wide + far)
    pair = pl.program_id(0)
    lines_scratch[pair] = jnp.concatenate(lines, axis=0)

    @pl.when(pair == pl.num_programs(0) - 1)
    def _():
        table_ref[...] = jnp.dot(
            lines_scratch[...].reshape(-1, 4 * count),
            onehot_ref[...],
            precision=highest,
            preferred_element_type=jnp.float32,
        ).reshape(table_ref.shape)


def attend_back(projected, grad_mixed, doc_probs, query_probs, onehot, length):
    rows, width = grad_mixed.shape
    pairs = doc_probs.shape[0] // 2
    docs = doc_probs.shape[1] // length
    query_rows = query_probs.shape[1]

    return pl.pallas_call(
        functools.partial(attend_back_kernel, docs, length),
        grid=(pairs,),
        out_shape=(
            jax.ShapeDtypeStruct((3, rows, width), jnp.bfloat16),
            pltpu.HBM((pairs, 2, onehot.shape[1]), jnp.float32),
        ),
        in_specs=[
            pair_spec(rows, 0),
            pair_spec(rows, pairs),
            pair_spec(rows, 2 * pairs),
            pair_spec(rows, 0),
            pl.BlockSpec((2, docs * length, length), lambda pair: (pair, 0, 0)),
            pl.BlockSpec((2, query_rows, count), lambda pair: (pair, 0, 0)),
            pl.BlockSpec(onehot.shape, lambda pair: (0, 0)),
        ],
        out_specs=(
            pl.BlockSpec((3, rows, 2 * 64), lambda pair: (0, 0, pair)),
            pl.BlockSpec((pairs, 2, onehot.shape[1]), lambda pair: (0, 0, 0)),
        ),
        scratch_shapes=[
            pltpu.VMEM((2 * length, length), jnp.float32),
            pltpu.VMEM((2 * length, length), jnp.bfloat16),
            pltpu.VMEM((2 * length, length), jnp.bfloat16),
            pltpu.VMEM((pairs, 2, 4 * count), jnp.float32),
        ],
        compiler_params=pltpu.CompilerParams(vmem_limit_bytes=22 * 2**20),
        cost_estimate=pl.CostEstimate(
            flops=2 * 2 * pairs * (docs * length * length + query_rows * count) * 128 * 4,
            bytes_accessed=rows * width * 14 + 8 * pairs * docs * length * length,
            transcendentals=0,
        ),
        name="attend_back",
    )(*in_hbm(projected, projected, projected, grad_mixed, doc_probs, query_probs), onehot)


def dot_tn(left, right):
    return lax.dot_general(
        left, right, (((0,), (0,)), ((), ())), preferred_element_type=jnp.float32
    )


tile = 512
row_parts = 2
curve = 0.044715
slope = 0.7978845608028654


def turned_rows(place_ref, values, turned):
    quarter = values.shape[1] // 4
    flipped = values[...].T
    for outer in range(2):
        for core in range(2):
            kept = core ^ 1 ^ place_ref[1]
            start = pl.multiple_of((2 * kept + outer) * quarter, 16)
            block = flipped[(2 * outer + core) * quarter : (2 * outer + core + 1) * quarter, :]
            turned[pl.ds(start, quarter), :] = block


def split_store(values, kept_ref, sent_ref):
    quarter = values.shape[0] // 4
    low = values.astype(jnp.bfloat16)
    for outer in range(2):
        sent_ref[outer] = low[outer * quarter : (outer + 1) * quarter, :]
        kept_ref[outer] = low[(2 + outer) * quarter : (3 + outer) * quarter, :]


def gate_kernel(place_ref, n2_ref, weight, cot_ref, act_ref, by_gate_ref, by_up_ref, kept_ref, sent_ref):
    rows, width = n2_ref.shape
    hidden = weight.shape[-1] // 2
    start = pl.multiple_of(pl.program_id(0) * tile, 128)
    gate_weight = weight[..., pl.ds(start, tile)].reshape(width, tile)
    up_weight = weight[..., pl.ds(hidden + start, tile)].reshape(width, tile)

    def finish(places, gate, up):
        square = gate * gate
        bent = slope + (slope * curve) * square
        halved = 0.5 + 0.5 * jnp.tanh(gate * bent)
        value = gate * halved
        steep = halved + gate * (6.0 * bent - 4.0 * slope) * (halved - halved * halved)
        act_ref[places, :] = (value * up).astype(jnp.bfloat16)
        by_gate_ref[places, :] = up * steep
        by_up_ref[places, :] = value

    held = None
    for start in range(0, rows, 128):
        places = slice(start, start + 128)
        gate = dot_nn(n2_ref[places, :], gate_weight)
        up = dot_nn(n2_ref[places, :], up_weight)
        if held is not None:
            finish(*held)
        held = (places, gate, up)
    finish(*held)
    grad = dot_tn(act_ref[...], cot_ref[...]).astype(jnp.bfloat16)
    core = pl.program_id(0) % 2

    @pl.when(core == place_ref[1])
    def _():
        kept_ref[0] = grad

    @pl.when(core != place_ref[1])
    def _():
        sent_ref[0] = grad


def gate_forward(place, pieces, normed_two, cot_low):
    rows, width = normed_two.shape
    columns = pieces[0].shape[-1]
    hidden = columns // 2
    number = len(pieces)
    whole = pl.BlockSpec((rows, width), lambda step: (0, 0))
    column = pl.BlockSpec((rows, tile), lambda step: (0, step))
    half = pl.BlockSpec((1, tile, width), lambda step: (step // 2, 0, 0))
    assert hidden == 4 * tile

    def kernel(place_ref, *refs):
        n2_ref, cot_ref, *outs, full_ref, held, sems = refs[number:]
        filled(
            place_ref, refs[:number], full_ref, held, sems,
            lambda: gate_kernel(place_ref, n2_ref, held, cot_ref, *outs),
        )

    *results, full = pl.pallas_call(
        kernel,
        grid=(hidden // tile,),
        out_shape=(
            pltpu.HBM((rows, hidden), jnp.bfloat16),
            pltpu.HBM((rows, hidden), jnp.float32),
            pltpu.HBM((rows, hidden), jnp.float32),
            jax.ShapeDtypeStruct((2, tile, width), jnp.bfloat16),
            jax.ShapeDtypeStruct((2, tile, width), jnp.bfloat16),
            pltpu.HBM(slab(columns, width), jnp.bfloat16),
        ),
        in_specs=[scalars()] + [anywhere] * number + [whole, whole],
        out_specs=(column, column, column, half, half, anywhere),
        scratch_shapes=[
            pltpu.VMEM(slab(columns, width), jnp.bfloat16),
            pltpu.SemaphoreType.DMA((9,)),
        ],
        compiler_params=pltpu.CompilerParams(vmem_limit_bytes=34 * 2**20),
        cost_estimate=pl.CostEstimate(
            flops=6 * rows * width * hidden,
            bytes_accessed=rows * hidden * 10 + 8 * width * hidden,
            transcendentals=rows * hidden,
        ),
        name="gate_forward",
    )(place, *pieces, normed_two, cot_low)
    return (*results, full.reshape(width, columns))


def gate_back_kernel(
    place_ref, n2_ref, cot_ref, ff, by_gate_ref, by_up_ref, out_ref, kept_ref, sent_ref, turned
):
    step = pl.program_id(0)
    weight = ff[step // 2, step % 2].reshape(tile, ff.shape[-1])
    incoming = dot_nt(cot_ref[...], weight)
    by_gate = (incoming * by_gate_ref[...]).astype(jnp.bfloat16)
    by_up = (incoming * by_up_ref[...]).astype(jnp.bfloat16)
    out_ref[0] = by_gate
    out_ref[1] = by_up
    split_store(dot_nn(turned[...], by_gate), kept_ref.at[:, :, :tile], sent_ref.at[:, :, :tile])
    split_store(dot_nn(turned[...], by_up), kept_ref.at[:, :, tile:], sent_ref.at[:, :, tile:])


def gate_back(place, pieces, normed_two, cot_low, by_gate, by_up):
    rows, width = normed_two.shape
    hidden = by_gate.shape[1]
    number = len(pieces)
    whole = pl.BlockSpec((rows, width), lambda step: (0, 0))
    column = pl.BlockSpec((rows, tile), lambda step: (0, step))
    half = pl.BlockSpec((2, width // 4, 2 * tile), lambda step: (0, 0, step))

    def kernel(place_ref, *refs):
        n2_ref, cot_ref, gate_ref, up_ref, *outs, full_ref, held, turned, sems = refs[number:]
        filled(
            place_ref, refs[:number], full_ref, held, sems,
            lambda: gate_back_kernel(
                place_ref, n2_ref, cot_ref, held, gate_ref, up_ref, *outs, turned
            ),
            lambda: turned_rows(place_ref, n2_ref, turned), True,
        )

    *results, full = pl.pallas_call(
        kernel,
        grid=(hidden // tile,),
        out_shape=(
            pltpu.HBM((2, rows, hidden), jnp.bfloat16),
            jax.ShapeDtypeStruct((2, width // 4, 2 * hidden), jnp.bfloat16),
            jax.ShapeDtypeStruct((2, width // 4, 2 * hidden), jnp.bfloat16),
            pltpu.HBM(slab(width, hidden), jnp.bfloat16),
        ),
        in_specs=[scalars()] + [anywhere] * number + [whole, whole, column, column],
        out_specs=(
            pl.BlockSpec((2, rows, tile), lambda step: (0, 0, step)),
            half,
            half,
            anywhere,
        ),
        scratch_shapes=[
            pltpu.VMEM(slab(width, hidden), jnp.bfloat16),
            pltpu.VMEM((width, rows), jnp.bfloat16),
            pltpu.SemaphoreType.DMA((9,)),
        ],
        compiler_params=pltpu.CompilerParams(vmem_limit_bytes=38 * 2**20),
        cost_estimate=pl.CostEstimate(
            flops=6 * rows * width * hidden,
            bytes_accessed=rows * hidden * 12 + 8 * width * hidden,
            transcendentals=0,
        ),
        name="gate_back",
    )(place, *pieces, normed_two, cot_low, *in_hbm(by_gate, by_up))
    return (*results, full.reshape(hidden, width))


def norm_back(grads, values, gain, residual):
    spread = lax.rsqrt(jnp.mean(values * values, axis=-1, keepdims=True) + epsilon)
    scaled = grads * gain
    inner = jnp.mean(scaled * values, axis=-1, keepdims=True)
    gain_grad = jnp.sum(grads * (values * spread), axis=0, keepdims=True)
    return residual + spread * scaled - values * (spread * spread * spread * inner), gain_grad


def middle_back_kernel(
    gates_hbm, weight_hbm, out_weight_hbm, middle_hbm, cot_hbm, gain_ref,
    grad_hbm, low_hbm, mixed_hbm, gain_grad_ref,
    gates, weight, out_weight, middle, cot, total, low, mixed, sems,
):
    rows, width = total.shape
    hidden = gates.shape[2]
    wide = hidden // 2
    arrivals = []

    def bring(source, target):
        copy = pltpu.make_async_copy(source, target, sems.at[len(arrivals)])
        copy.start()
        arrivals.append(copy)

    for part in range(4):
        columns = pl.ds(part % 2 * wide, wide)
        bring(gates_hbm.at[part // 2, :, columns], gates.at[part // 2, :, columns])
        columns = pl.ds(part * wide, wide)
        bring(weight_hbm.at[:, columns], weight.at[:, columns])
    bring(middle_hbm, middle)
    bring(cot_hbm, cot)
    bring(out_weight_hbm.at[:, pl.ds(3 * width, width)], out_weight)
    for part in range(4):
        arrivals[2 * part].wait()
        arrivals[2 * part + 1].wait()
        columns = slice(part % 2 * wide, part % 2 * wide + wide)
        product = dot_nt(
            gates[part // 2, :, columns], weight[:, part * wide : part * wide + wide]
        )
        if part == 0:
            total[...] = product
        else:
            total[...] += product
    for copy in arrivals[8:]:
        copy.wait()
    leaving = []
    for half in range(2):
        places = slice(half * rows // 2, (half + 1) * rows // 2)
        grad, gain_grad = norm_back(
            total[places, :], middle[places, :], gain_ref[...], cot[places, :]
        )
        total[places, :] = grad
        low[places, :] = grad.astype(jnp.bfloat16)
        if half == 0:
            gain_grad_ref[...] = gain_grad
        else:
            gain_grad_ref[...] += gain_grad
        mixed[places, :] = dot_nt(low[places, :], out_weight[...]).astype(jnp.bfloat16)
        places = pl.ds(half * rows // 2, rows // 2)
        for source, target in ((total, grad_hbm), (low, low_hbm), (mixed, mixed_hbm)):
            copy = pltpu.make_async_copy(
                source.at[places], target.at[places], sems.at[len(arrivals) + len(leaving)]
            )
            copy.start()
            leaving.append(copy)
    for copy in leaving:
        copy.wait()


def middle_back(gates, full_in, middle, cotangent, gain, full_attention):
    rows, width = middle.shape
    hidden = gates.shape[2]
    low = jnp.bfloat16
    line = pl.BlockSpec(memory_space=pltpu.VMEM)
    return pl.pallas_call(
        middle_back_kernel,
        out_shape=(
            pltpu.HBM((rows, width), jnp.float32),
            pltpu.HBM((rows, width), low),
            pltpu.HBM((rows, width), low),
            jax.ShapeDtypeStruct((1, width), jnp.float32),
        ),
        in_specs=[anywhere] * 5 + [line],
        out_specs=(anywhere, anywhere, anywhere, line),
        scratch_shapes=[
            pltpu.VMEM((2, rows, hidden), low),
            pltpu.VMEM((width, 2 * hidden), low),
            pltpu.VMEM((width, width), low),
            pltpu.VMEM((rows, width), jnp.float32),
            pltpu.VMEM((rows, width), jnp.float32),
            pltpu.VMEM((rows, width), jnp.float32),
            pltpu.VMEM((rows, width), low),
            pltpu.VMEM((rows, width), low),
            pltpu.SemaphoreType.DMA((17,)),
        ],
        compiler_params=pltpu.CompilerParams(vmem_limit_bytes=46 * 2**20),
        cost_estimate=pl.CostEstimate(
            flops=4 * rows * width * hidden + 2 * rows * width * width,
            bytes_accessed=rows * hidden * 4 + 4 * width * hidden + 18 * rows * width,
            transcendentals=0,
        ),
        name="middle_back",
    )(*in_hbm(gates, full_in, full_attention, middle, cotangent), gain.reshape(1, -1))


def scalars():
    return pl.BlockSpec(memory_space=pltpu.SMEM)


def by_parts(name, first, second, kinds, body, *extra):
    width = first.shape[1]
    rows = first.shape[0] + second.shape[0]
    starts = first.shape[0] // count

    def kernel(first_ref, second_ref, *refs):
        @pl.when(pl.program_id(0) < starts)
        def _():
            body(first_ref, *refs)

        @pl.when(pl.program_id(0) >= starts)
        def _():
            body(second_ref, *refs)

    return pl.pallas_call(
        kernel,
        grid=(rows // count,),
        out_shape=[pltpu.HBM((rows, width), kind) for kind in kinds],
        in_specs=[
            pl.BlockSpec((count, width), lambda step: (jnp.minimum(step, starts - 1), 0)),
            pl.BlockSpec((count, width), lambda step: (jnp.maximum(step - starts, 0), 0)),
        ]
        + [pl.BlockSpec(line.shape, lambda step: (0, 0)) for line in extra],
        out_specs=[pl.BlockSpec((count, width), lambda step: (step, 0))] * len(kinds),
        compiler_params=pltpu.CompilerParams(vmem_limit_bytes=20 * 2**20),
        cost_estimate=pl.CostEstimate(
            flops=4 * rows * width, bytes_accessed=10 * rows * width, transcendentals=rows
        ),
        name=name,
    )(*in_hbm(first, second), *extra)


def norm_body(rows_ref, gain_ref, values_ref, normed_ref):
    values = rows_ref[...]
    spread = lax.rsqrt(jnp.mean(values * values, axis=-1, keepdims=True) + epsilon)
    values_ref[...] = values
    normed_ref[...] = (values * spread * gain_ref[...]).astype(jnp.bfloat16)


def round_body(rows_ref, values_ref, low_ref):
    values_ref[...] = rows_ref[...]
    low_ref[...] = rows_ref[...].astype(jnp.bfloat16)


def project(place, pieces, normed):
    rows, width = normed.shape
    columns = pieces[0].shape[-1]
    number = len(pieces)

    def kernel(place_ref, *refs):
        normed_ref, out_ref, full_ref, held, sems = refs[number:]

        def body():
            start = pl.multiple_of(pl.program_id(0) * width, 128)
            weight = held[..., pl.ds(start, width)].reshape(width, width)
            out_ref[...] = dot_nn(normed_ref[...], weight).astype(jnp.bfloat16)

        filled(place_ref, refs[:number], full_ref, held, sems, body)

    projected, full = pl.pallas_call(
        kernel,
        grid=(3,),
        out_shape=(
            pltpu.HBM((rows, 3 * width), jnp.bfloat16),
            pltpu.HBM(slab(columns, width), jnp.bfloat16),
        ),
        in_specs=[scalars()]
        + [anywhere] * number
        + [pl.BlockSpec((rows, width), lambda step: (0, 0))],
        out_specs=(pl.BlockSpec((rows, width), lambda step: (0, step)), anywhere),
        scratch_shapes=[
            pltpu.VMEM(slab(columns, width), jnp.bfloat16),
            pltpu.SemaphoreType.DMA((9,)),
        ],
        compiler_params=pltpu.CompilerParams(vmem_limit_bytes=14 * 2**20),
        cost_estimate=pl.CostEstimate(
            flops=6 * rows * width * width,
            bytes_accessed=8 * rows * width + 4 * columns * width,
            transcendentals=0,
        ),
        name="project",
    )(place, *pieces, normed)
    return projected, full.reshape(width, columns)


def middle_kernel(rows_ref, mixed_ref, weight_ref, gain_ref, middle_ref, normed_ref):
    middle = rows_ref[...] + dot_nn(mixed_ref[...], weight_ref[...])
    spread = lax.rsqrt(jnp.mean(middle * middle, axis=-1, keepdims=True) + epsilon)
    middle_ref[...] = middle
    normed_ref[...] = (middle * spread * gain_ref[...]).astype(jnp.bfloat16)


def middle_forward(values, mixed, full_attention, gain, *earlier):
    rows, width = values.shape
    part = rows // 2
    block = pl.BlockSpec((part, width), lambda step: (step, 0))

    def kernel(*refs):
        middle_kernel(*refs[:4], *refs[4 + len(earlier) :])

    return pl.pallas_call(
        kernel,
        grid=(2,),
        out_shape=(
            pltpu.HBM((rows, width), jnp.float32),
            jax.ShapeDtypeStruct((rows, width), jnp.bfloat16),
        ),
        in_specs=[
            block,
            block,
            pl.BlockSpec((width, width), lambda step: (0, 3)),
            pl.BlockSpec((1, width), lambda step: (0, 0)),
        ]
        + [anywhere] * len(earlier),
        out_specs=(block, block),
        compiler_params=pltpu.CompilerParams(vmem_limit_bytes=15 * 2**20),
        cost_estimate=pl.CostEstimate(
            flops=2 * rows * width * width,
            bytes_accessed=12 * rows * width + 2 * width * width,
            transcendentals=0,
        ),
        name="middle_forward",
    )(*in_hbm(values), mixed, *in_hbm(full_attention), gain.reshape(1, -1), *earlier)


def attention_grads_kernel(
    place_ref, normed_ref, grads_ref, mixed_hbm, low_hbm, weight_0, weight_1, weight_2, weight_3,
    gain_ref, ffn_ref, table_ref, kept_ref, sent_ref, small_ref,
    turned, column, ordered, mixed_ref, low_ref, sems,
):
    step = pl.program_id(0)
    last = pl.num_programs(0) - 1
    quarter = column.shape[0] // 4
    copies = [
        pltpu.make_async_copy(mixed_hbm, mixed_ref, sems.at[0]),
        pltpu.make_async_copy(low_hbm, low_ref, sems.at[1]),
    ]

    @pl.when(step == 0)
    def _():
        for copy in copies:
            copy.start()
        turned_rows(place_ref, normed_ref, turned)
        column[...] = jnp.zeros_like(column)

    @pl.when(step < last)
    def _():
        grads = dot_nn(turned[...], grads_ref[0])
        split_store(grads, kept_ref, sent_ref)
        for number, weight in enumerate((weight_0, weight_1, weight_2, weight_3)):
            rows = slice(number * quarter, (number + 1) * quarter)
            product = grads[rows, :] * weight[...].astype(jnp.float32)
            parts = [product[:, lane : lane + 128] for lane in range(0, grads.shape[1], 128)]
            column[rows, :] += sum(parts)

    @pl.when(step == last)
    def _():
        for copy in copies:
            copy.wait()
        turned_rows(place_ref, mixed_ref, turned)
        split_store(dot_nn(turned[...], low_ref[...]), kept_ref, sent_ref)
        for number in range(4):
            row = quarter_owner(number, place_ref[1])
            start = pl.multiple_of(row * quarter, 16)
            ordered[pl.ds(start, quarter), :] = column[number * quarter : (number + 1) * quarter, :]
        gain_grad = jnp.sum(ordered[...].T, axis=0, keepdims=True) / gain_ref[...]
        small_ref[...] = jnp.zeros_like(small_ref)
        lines = gain_grad.shape[1] // 128
        for number, line in enumerate((gain_grad, ffn_ref[...])):
            for part in range(lines):
                row = number * lines + part
                small_ref[row : row + 1, :] = line[:, part * 128 : (part + 1) * 128]
        table = table_ref[...].reshape(-1, table_ref.shape[2])
        small_ref[2 * lines :, : table.shape[1]] = table


def quarter_owner(number, core):
    return 2 * (number % 2) + (core if number >= 2 else 1 - core)


def attention_grads(
    place, normed, grad_projected, mixed, grad_low, full_attention, gain, ffn_grad, table
):
    rows, width = normed.shape
    lines = 2 * (width // 128) + 2 * table.shape[0]

    def fixed(step, where):
        return 0, 0

    def column(step, where):
        return 0, 0, step

    def weight_spec(number):
        return pl.BlockSpec(
            (width // 4, width),
            lambda step, where: (quarter_owner(number, where[1]), jnp.minimum(step, 2)),
        )

    shape = jax.ShapeDtypeStruct((2, width // 4, 4 * width), jnp.bfloat16)
    half = pl.BlockSpec((2, width // 4, width), column)
    return pl.pallas_call(
        attention_grads_kernel,
        grid_spec=pltpu.PrefetchScalarGridSpec(
            num_scalar_prefetch=1,
            grid=(4,),
            in_specs=[
                pl.BlockSpec((rows, width), fixed),
                pl.BlockSpec((1, rows, width), lambda step, where: (jnp.minimum(step, 2), 0, 0)),
                anywhere,
                anywhere,
                *[weight_spec(number) for number in range(4)],
                pl.BlockSpec((1, width), fixed),
                pl.BlockSpec((1, width), fixed),
                pl.BlockSpec(table.shape, lambda step, where: (0, 0, 0)),
            ],
            out_specs=(half, half, pl.BlockSpec((lines, 128), fixed)),
            scratch_shapes=[
                pltpu.VMEM((width, rows), jnp.bfloat16),
                pltpu.VMEM((width, 128), jnp.float32),
                pltpu.VMEM((width, 128), jnp.float32),
                pltpu.VMEM((rows, width), jnp.bfloat16),
                pltpu.VMEM((rows, width), jnp.bfloat16),
                pltpu.SemaphoreType.DMA((2,)),
            ],
        ),
        out_shape=(shape, shape, jax.ShapeDtypeStruct((lines, 128), jnp.float32)),
        compiler_params=pltpu.CompilerParams(vmem_limit_bytes=36 * 2**20),
        cost_estimate=pl.CostEstimate(
            flops=8 * rows * width * width,
            bytes_accessed=12 * rows * width + 14 * width * width,
            transcendentals=0,
        ),
        name="attention_grads",
    )(
        place,
        *in_hbm(normed),
        grad_projected,
        *in_hbm(mixed, grad_low, *[full_attention] * 4),
        gain.reshape(1, -1),
        ffn_grad,
        table,
    )


def input_back(grad_projected, full_qkv, values, residual, gain, doc_rows):
    rows, width = values.shape
    part = rows // row_parts
    block = pl.BlockSpec((part, width), lambda step: (step, 0))

    def kernel(
        grads_ref, weight_ref, rows_ref, residual_ref, gain_ref,
        doc_ref, query_ref, slots, sems,
    ):
        step = pl.program_id(0)
        total = dot_nt(grads_ref[0], weight_ref[:, :width])
        for third in (1, 2):
            columns = slice(third * width, (third + 1) * width)
            total = total + dot_nt(grads_ref[third], weight_ref[:, columns])
        slots[step], _ = norm_back(total, rows_ref[...], gain_ref[...], residual_ref[...])
        emit(slots, (doc_ref, query_ref), sems)

    return pl.pallas_call(
        kernel,
        grid=(row_parts,),
        out_shape=(
            jax.ShapeDtypeStruct((doc_rows, width), jnp.float32),
            jax.ShapeDtypeStruct((rows - doc_rows, width), jnp.float32),
        ),
        in_specs=[
            pl.BlockSpec((3, part, width), lambda step: (0, step, 0)),
            pl.BlockSpec((width, 3 * width), lambda step: (0, 0)),
            block,
            block,
            pl.BlockSpec((1, width), lambda step: (0, 0)),
        ],
        out_specs=(anywhere, anywhere),
        scratch_shapes=[
            pltpu.VMEM((row_parts, part, width), jnp.float32),
            pltpu.SemaphoreType.DMA((row_parts + 1,)),
        ],
        compiler_params=pltpu.CompilerParams(vmem_limit_bytes=30 * 2**20),
        cost_estimate=pl.CostEstimate(
            flops=6 * rows * width * width,
            bytes_accessed=18 * rows * width + 6 * width * width,
            transcendentals=0,
        ),
        name="input_back",
    )(grad_projected, *in_hbm(full_qkv, values, residual), gain.reshape(1, -1))


def layer_outputs(middle, activated, full_ff, doc_rows):
    rows, width = middle.shape
    hidden = activated.shape[1]
    part = rows // row_parts

    def kernel(middle_ref, act_ref, weight_ref, doc_ref, query_ref, slots, sems):
        slots[pl.program_id(0)] = middle_ref[...] + dot_nn(act_ref[...], weight_ref[...])
        emit(slots, (doc_ref, query_ref), sems)

    return pl.pallas_call(
        kernel,
        grid=(row_parts,),
        out_shape=(
            jax.ShapeDtypeStruct((doc_rows, width), jnp.float32),
            jax.ShapeDtypeStruct((rows - doc_rows, width), jnp.float32),
        ),
        in_specs=[
            pl.BlockSpec((part, width), lambda step: (step, 0)),
            pl.BlockSpec((part, hidden), lambda step: (step, 0)),
            pl.BlockSpec((hidden, width), lambda step: (0, 0)),
        ],
        out_specs=(anywhere, anywhere),
        scratch_shapes=[
            pltpu.VMEM((row_parts, part, width), jnp.float32),
            pltpu.SemaphoreType.DMA((row_parts + 1,)),
        ],
        compiler_params=pltpu.CompilerParams(vmem_limit_bytes=24 * 2**20),
        cost_estimate=pl.CostEstimate(
            flops=2 * rows * width * hidden,
            bytes_accessed=8 * rows * width + 2 * hidden * (rows + width),
            transcendentals=0,
        ),
        name="layer_outputs",
    )(*in_hbm(middle, activated, full_ff))


def body(
    doc_inputs,
    query_inputs,
    doc_mask,
    query_lengths,
    doc_cotangent,
    query_cotangent,
    qkv_weight,
    out_weight,
    in_weight,
    ff_weight,
    attn_gain,
    ffn_gain,
    bias_table,
):
    doc_count, doc_length, model_width = doc_inputs.shape
    group_count, group_length = (query_inputs.shape[0], query_inputs.shape[1])
    head_count = bias_table.shape[1]
    doc_rows = doc_count * doc_length
    low = jnp.bfloat16
    routed = hand_routed()
    place = own_place() if routed else (0, 0, 0, 0)
    place_vector = jnp.stack([jnp.asarray(index, jnp.int32) for index in place])

    attention_shard = jnp.concatenate([qkv_weight, out_weight], axis=1).astype(low)
    in_shard = in_weight.astype(low)
    ff_shard = ff_weight.astype(low)

    kinds = (jnp.float32, low)
    values, normed = by_parts(
        "norm_rows",
        doc_inputs.reshape(doc_rows, model_width),
        query_inputs.reshape(-1, model_width),
        kinds,
        norm_body,
        attn_gain.reshape(1, -1),
    )
    cotangent_parts = (
        doc_cotangent.reshape(doc_rows, model_width),
        query_cotangent.reshape(-1, model_width),
    )
    places = jnp.arange(group_length, dtype=jnp.int32)
    query_mask = places[None, :] < query_lengths[:, None]
    onehot = lines_onehot(bias_table.shape[0])
    lines = jnp.einsum("pn,nh->hp", onehot, bias_table, precision=highest)
    lines = lines.reshape(head_count // 2, 2, 4 * count)
    doc_masking = jnp.where(doc_mask > 0, 0.0, -1e9).astype(jnp.float32)
    query_masking = jnp.where(query_mask, 0.0, -1e9).astype(jnp.float32)
    query_masking = query_masking.reshape(-1, 1, count)

    if routed:
        column_a = gather_column(attention_shard)
        row_f = jnp.stack(in_order(ff_shard, swap(ff_shard, dx=1), place[3]))
        column_a, row_f, normed, lines, doc_masking, query_masking, in_shard, cotangent_parts = (
            together(
                column_a, row_f, normed, lines, doc_masking, query_masking, in_shard,
                cotangent_parts,
            )
        )
        plane_a = gather_plane(place, attention_shard, column_a)
        cotangent, cot_low = by_parts("round_rows", *cotangent_parts, kinds, round_body)
        plane_a, cotangent, cot_low = together(plane_a, cotangent, cot_low)
        near_a = gather_near(place, *plane_a)
        column_i = gather_column(in_shard)
        far_a = gather_far(*near_a)
        plane_f = jnp.stack(in_order(row_f, swap(row_f, dy=1), place[0]))
        column_i, far_a, plane_f = together(column_i, far_a, plane_f)
        pieces = gather_order(near_a, far_a, gather_core(*near_a), gather_core(*far_a))
        plane_i = gather_plane(place, in_shard, column_i)
    else:
        cotangent, cot_low = by_parts("round_rows", *cotangent_parts, kinds, round_body)
        pieces = (split_rows(lax.all_gather(attention_shard, both, axis=0, tiled=True)),)
    projected, full_attention = project(place_vector, pieces, normed)
    if routed:
        plane_i, projected = together(plane_i, projected)
        near_i = gather_near(place, *plane_i)
        far_i = gather_far(*near_i)
        second_f = swap(plane_f, dz=2)
    mixed, doc_probs, query_probs = attend(
        projected, lines, doc_masking, query_masking, group_length
    )
    if routed:
        mixed, far_i, second_f = together(mixed, far_i, second_f)
        others_f = gather_others(plane_f, second_f)
        pieces = gather_order(near_i, far_i, gather_core(*near_i), gather_core(*far_i))
    else:
        pieces = (split_rows(lax.all_gather(in_shard, both, axis=0, tiled=True)),)
    middle, normed_two = middle_forward(values, mixed, full_attention, ffn_gain)
    if routed:
        pieces, normed_two = together(pieces, normed_two)
        core_f = gather_core(plane_f, second_f)
    activated, by_gate, by_up, kept, sent, full_in = gate_forward(
        place_vector, pieces, normed_two, cot_low
    )
    if routed:
        others_f, core_f, by_gate, kept, sent = together(others_f, core_f, by_gate, kept, sent)
        core_others = gather_core(*others_f)
        pieces = (plane_f, others_f[0], second_f, others_f[1])
        pieces += (core_f[0], core_others[0], core_f[1], core_others[1])
        ff_grads = NarrowScatter(kept, sent, place_vector)
        got_f = ff_grads.core()
        pieces, got_f = together(pieces, got_f)
        near_f = ff_grads.plane(got_f)
    else:
        pieces = (split_rows(lax.all_gather(ff_shard, both, axis=0, tiled=True)),)
        grad_ff = joined_halves(kept, sent)
    gates, kept, sent, full_ff = gate_back(
        place_vector, pieces, normed_two, cot_low, by_gate, by_up
    )
    if routed:
        gates, kept, sent, near_f = together(gates, kept, sent, near_f)
        in_grads = Scatter(kept, sent, place_vector, pinned=False)
        far_f = ff_grads.far(ff_grads.far_sums(got_f, near_f))
        got_i = in_grads.core()
    else:
        grad_in = joined_halves(kept, sent)
    grad_middle, grad_middle_low, grad_mixed, grad_ffn_gain = middle_back(
        gates, full_in, middle, cotangent, ffn_gain, full_attention
    )
    if routed:
        grad_mixed, far_f, got_i = together(grad_mixed, far_f, got_i)
        near_i = in_grads.plane(got_i)
        shares_f = ff_grads.column(ff_grads.column_sums(got_f, near_f, far_f))
    grad_projected, grad_table = attend_back(
        projected, grad_mixed, doc_probs, query_probs, onehot, doc_length
    )
    if routed:
        grad_projected, grad_table, shares_f, near_i = together(
            grad_projected, grad_table, shares_f, near_i
        )
        far_i = in_grads.far(got_i, near_i)
    kept, sent, small = attention_grads(
        place_vector, normed, grad_projected, mixed, grad_middle_low, full_attention, attn_gain,
        grad_ffn_gain, grad_table,
    )
    if routed:
        kept, sent, far_i, small, grad_projected, shares_f, activated = together(
            kept, sent, far_i, small, grad_projected, shares_f, activated
        )
        attention = Scatter(kept, sent, place_vector, pinned=False)
        got_a = attention.core()
        small = add_flipped(small, {"dc": 1})
        sums_i = in_grads.column_sums(got_i, near_i, far_i)
        got_a, sums_i, small, grad_projected, shares_f, activated = together(
            got_a, sums_i, small, grad_projected, shares_f, activated
        )
        near_a = attention.plane(got_a)
        shares_i = in_grads.column(sums_i)
        small = add_flipped(small, {"dz": 1})
    grad_inputs = input_back(
        grad_projected, full_attention, values, grad_middle, attn_gain, doc_rows
    )
    if routed:
        near_a, grad_inputs, small, shares_f, shares_i, activated = together(
            near_a, grad_inputs, small, shares_f, shares_i, activated
        )
        far_a = attention.far(got_a, near_a)
        small = add_flipped(small, {"dz": 2})
        far_a, small, shares_f, shares_i, activated = together(
            far_a, small, shares_f, shares_i, activated
        )
        sums_a = attention.column_sums(got_a, near_a, far_a)
        sums_a, small, shares_f, shares_i, activated = together(
            sums_a, small, shares_f, shares_i, activated
        )
        shares_a = attention.column(sums_a)
        small = add_flipped(small, {"dx": 1}, {"dy": 1})
    outputs = layer_outputs(middle, activated, full_ff, doc_rows)
    if routed:
        ff_grad_shard = summed(*shares_f)
        in_grad_shard = summed(*shares_i)
        grad_qkv = summed(*[share[:, : 3 * model_width] for share in shares_a])
        grad_out = summed(*[share[:, 3 * model_width :] for share in shares_a])
    else:
        scatter = functools.partial(
            lax.psum_scatter, axis_name=both, scatter_dimension=0, tiled=True
        )
        ff_grad_shard = scatter(grad_ff)
        in_grad_shard = scatter(grad_in)
        grad_attention = scatter(joined_halves(kept, sent))
        grad_qkv = grad_attention[:, : 3 * model_width]
        grad_out = grad_attention[:, 3 * model_width :]
        small = lax.psum(small, both)
    width_lines = model_width // 128
    in_grad_shard = in_grad_shard.reshape(in_weight.shape[0], -1, 2, tile)
    in_grad_shard = jnp.swapaxes(in_grad_shard, 1, 2).reshape(in_weight.shape)
    return (
        outputs[0].reshape(doc_inputs.shape),
        outputs[1].reshape(query_inputs.shape),
        grad_inputs[0].reshape(doc_inputs.shape),
        grad_inputs[1].reshape(query_inputs.shape),
        grad_qkv,
        grad_out,
        in_grad_shard,
        ff_grad_shard,
        small[:width_lines].reshape(model_width),
        small[width_lines : 2 * width_lines].reshape(model_width),
        small[2 * width_lines :, : bias_table.shape[0]].T,
    )


def solution(mesh):
    placed = (
        P(("dp", "fsdp"), None, None),
        P(("dp", "fsdp"), None, None),
        P(("dp", "fsdp"), None),
        P(("dp", "fsdp")),
        P(("dp", "fsdp"), None, None),
        P(("dp", "fsdp"), None, None),
        P(("dp", "fsdp"), None),
        P(("dp", "fsdp"), None),
        P(("dp", "fsdp"), None),
        P(("dp", "fsdp"), None),
        P(),
        P(),
        P(),
    )
    return jax.shard_map(
        body,
        mesh=mesh,
        in_specs=placed,
        out_specs=(
            P(("dp", "fsdp"), None, None),
            P(("dp", "fsdp"), None, None),
            P(("dp", "fsdp"), None, None),
            P(("dp", "fsdp"), None, None),
            P(("dp", "fsdp"), None),
            P(("dp", "fsdp"), None),
            P(("dp", "fsdp"), None),
            P(("dp", "fsdp"), None),
            P(),
            P(),
            P(),
        ),
        check_vma=False,
    )
```
